512 devices in a mesh: row: 32 (over y_lo, z), col: 16 (over y_hi, x, core).
Axes of the slice: x: 4, y: 8 (y_hi: 2, y_lo: 4; y = y_hi * 4 + y_lo), z: 8, core: 2. Of those that a mesh axis runs over, the one named last changes fastest.
Arguments:
- hamiltonian_blocks: float32 [32, 16, 4, 128, 128], P('row', 'col'), may hold values from -0.25 to 0.25
- block_rows: int32 [32, 16, 4], P('row', 'col'), may hold values from 0 to 31
- block_cols: int32 [32, 16, 4], P('row', 'col'), may hold values from 0 to 31
- current_states: float32 [8, 131072], P(None, 'row'), may hold values from -6 to 6
- previous_steps: float32 [8, 131072], P(None, 'row'), may hold values from -6 to 6
Outputs:
- ritz_basis: float32 [24, 131072], P(None, ('row', 'col'))
- rayleigh_matrix: float32 [24, 24], replicated
The draws below stay inside these ranges and needn't reach their ends.
All inputs are finite; a program needn't handle non-finite values.
Results may differ from the reference program's by a relative error of at most 0.0003.
Values sent between devices are 32-bit elements; how exact they have to be, the bound alone decides.
A program may use at most 64 MiB of HBM per device.

```python
import jax
import jax.numpy as jnp
from jax import lax

K = 8
B = 128
SEGB = 32
NBLK_DEV = 4
ROWS = 131072
N_ROW = 32
N_COL = 16


def with_ends(entries, own_key, low, high):
    dims = entries.shape
    place = [jax.random.randint(jax.random.fold_in(own_key, axis), (), 0, dims[axis]) for axis in range(len(dims))]
    entries = entries.at[tuple(place)].set(low)
    longest = dims.index(max(dims))
    place[longest] = (place[longest] + 1) % dims[longest]
    return entries.at[tuple(place)].set(high)


def block_levels(key, extent, pieces, smallest, high):
    def one(position, parts):
        steps = jax.random.uniform(jax.random.fold_in(jax.random.fold_in(key, 6), position), (parts,), jnp.float32, smallest / len(pieces), high / len(pieces))
        return jnp.repeat(jnp.exp(steps), extent[position] // parts).reshape((-1,) + (1,) * (len(extent) - position - 1))

    factor_of = one(*pieces[0])
    for cut in pieces[1:]:
        factor_of = factor_of * one(*cut)
    return factor_of


def gaussian(rng, dims, deviation, limit, split=(), kind=jnp.bfloat16):
    level = block_levels(rng, dims, split, -0.22, 0.18) if split else 1.0
    array = jax.random.normal(rng, dims, jnp.float32) * deviation * level
    return jnp.minimum(jnp.maximum(array, -limit), limit).astype(kind)


def setup_inputs(seed: int = 0) -> dict:
    streams_of = jax.random.split(jax.random.key(seed), 6)
    return {
        "hamiltonian_blocks": gaussian(streams_of[0], (N_ROW, N_COL, NBLK_DEV, B, B), (2 * B * NBLK_DEV * N_COL // SEGB) ** -0.5, 0.25, ((0, 32), (1, 16)), jnp.float32),
        "block_rows": with_ends(jax.random.randint(streams_of[1], (N_ROW, N_COL, NBLK_DEV), 0, SEGB), jax.random.fold_in(streams_of[1], 1), 0, SEGB - 1).astype(jnp.int32),
        "block_cols": with_ends(jax.random.randint(streams_of[2], (N_ROW, N_COL, NBLK_DEV), 0, SEGB), jax.random.fold_in(streams_of[2], 1), 0, SEGB - 1).astype(jnp.int32),
        "current_states": gaussian(streams_of[3], (K, ROWS), 1.0, 6.0, ((1, 32),), jnp.float32),
        "previous_steps": gaussian(streams_of[4], (K, ROWS), 1.0, 6.0, ((1, 32),), jnp.float32),
    }


exactness = lax.Precision.HIGHEST

def local_terms(tiles, row_index, col_index, owned, remote):
    positions = jnp.arange(owned.shape[1], dtype=jnp.int32)
    owned_rows = jnp.take(owned, row_index, axis=1)
    remote_cols = jnp.take(remote, col_index, axis=1)
    direct = jnp.einsum('knb,ncb->knc', remote_cols, tiles, precision=exactness)
    mirrored = jnp.einsum('knc,ncb->knb', owned_rows, tiles, precision=exactness)
    row_onehot = (row_index[:, None] == positions[None, :]).astype(jnp.float32)
    col_onehot = (col_index[:, None] == positions[None, :]).astype(jnp.float32)
    into_owned = jnp.einsum('knc,ns->ksc', direct, row_onehot, precision=exactness)
    into_remote = jnp.einsum('knb,ns->ksb', mirrored, col_onehot, precision=exactness)
    return (into_owned, into_remote)

def apply_operator(blocks, rows, cols, vectors):
    width = vectors.shape[0]
    segments = vectors.reshape(width, N_ROW, SEGB, B)
    flat_blocks = blocks.reshape(N_ROW * N_COL, NBLK_DEV, B, B)
    flat_rows = rows.reshape(N_ROW * N_COL, NBLK_DEV)
    flat_cols = cols.reshape(N_ROW * N_COL, NBLK_DEV)

    def visit(total, item):
        device, tiles, row_index, col_index = item
        grid_row = device // N_COL
        grid_col = device % N_COL
        partner = (grid_row + grid_col) % N_ROW
        owned = lax.dynamic_index_in_dim(segments, grid_row, 1, keepdims=False)
        remote = lax.dynamic_index_in_dim(segments, partner, 1, keepdims=False)
        into_owned, into_remote = local_terms(tiles, row_index, col_index, owned, remote)
        total = total.at[:, grid_row].add(into_owned)
        total = total.at[:, partner].add(into_remote)
        return (total, None)
    devices = jnp.arange(N_ROW * N_COL, dtype=jnp.int32)
    start = jnp.zeros(segments.shape, jnp.float32)
    total, unused = lax.scan(visit, start, (devices, flat_blocks, flat_rows, flat_cols))
    return total.reshape(width, N_ROW * SEGB * B)

def reference(hamiltonian_blocks, block_rows, block_cols, current_states, previous_steps):
    count = current_states.shape[1]
    images = apply_operator(hamiltonian_blocks, block_rows, block_cols, current_states)
    theta_matrix = jnp.dot(current_states, images.T, precision=exactness) / count
    residual = images - jnp.dot(theta_matrix.T, current_states, precision=exactness)
    basis_raw = jnp.concatenate([residual, current_states, previous_steps], 0)
    gram = jnp.dot(basis_raw, basis_raw.T, precision=exactness) / count
    lower = jnp.linalg.cholesky(gram)
    identity = jnp.eye(3 * K, dtype=gram.dtype)
    inverse = lax.linalg.triangular_solve(lower, identity, left_side=True, lower=True)
    ritz_basis = jnp.dot(inverse, basis_raw, precision=exactness)
    further = apply_operator(hamiltonian_blocks, block_rows, block_cols, jnp.concatenate([residual, previous_steps], 0))
    images_all = jnp.concatenate([further[:K], images, further[K:]], 0)
    projected = jnp.dot(inverse, images_all, precision=exactness)
    rayleigh_matrix = jnp.dot(ritz_basis, projected.T, precision=exactness) / count
    return (ritz_basis, rayleigh_matrix)
```

```python
import functools

import jax
import jax.numpy as jnp
from jax import lax
from jax.experimental import pallas as pl
from jax.experimental.pallas import tpu as pltpu
from jax.sharding import PartitionSpec as P

MESH = pl.DeviceIdType.MESH
F32 = jnp.float32
exactness = lax.Precision.HIGHEST

Z, YL, YH, L = 8, 4, 2, 8
Y = YL * YH
N_ROW, N_COL = Z * YL, L * YH
K, B, SEGB, NB = 8, 128, 32, 4
SEG = SEGB * B
SHARE = SEG // N_COL
ROWS = N_ROW * SEG
rem, div = lax.rem, lax.div


def nn(a, b):
    return jnp.dot(a, b, precision=exactness, preferred_element_type=F32)


def nt(a, b):
    return lax.dot_general(a, b, (((1,), (1,)), ((), ())), precision=exactness, preferred_element_type=F32)


def lane_ids(shape):
    return lax.broadcasted_iota(jnp.int32, shape, 1)


def row_ids(shape):
    return lax.broadcasted_iota(jnp.int32, shape, 0)


def padded(a):
    return jnp.concatenate([a, jnp.zeros((B - a.shape[0], a.shape[1]), F32)], 0)


def transposed(a):
    n = a.shape[0]
    unit = (lane_ids((n, n)) == row_ids((n, n))).astype(F32)
    return nt(unit, a[:, :n])


def packed(a):
    return a[0:8] + pltpu.roll(a[8:16], 32, 1) + pltpu.roll(a[16:24], 64, 1)


def unpacked(t):
    a = jnp.concatenate([t, pltpu.roll(t, 96, 1), pltpu.roll(t, 64, 1)], 0)
    return jnp.where(lane_ids(a.shape) < 24, a, 0.0)


def inverse_factor(gram):
    rows, lanes = row_ids(gram.shape), lane_ids(gram.shape)
    left = gram
    right = (rows == lanes).astype(F32)
    for j in range(24):
        pivot = left[j : j + 1, j : j + 1]
        factor = jnp.where(rows[:, :1] > j, left[:, j : j + 1] / pivot, 0.0)
        top, unit = left[j : j + 1], right[j : j + 1]
        left = left - factor * top
        right = right - factor * unit
    diagonal = jnp.sum(jnp.where(rows == lanes, left, 0.0), 1, keepdims=True)
    return right / jnp.sqrt(diagonal)


def kernel(rows_ref, cols_ref, h_ref, x_ref, p_ref, q_ref, ray_ref,
           h, x, x_far, p, p_far, d, m, got_d, got_m, piece, y, y_far, mine, buf_a, buf_b,
           load_sem, x_sem, p_sem, xs_sem, ps_sem, d_sem, m_sem, ds_sem, ms_sem,
           y_sem, yfar_sem, ys_sem, yfs_sem, a_sem, b_sem, as_sem, bs_sem, step2, step3):
    r, c = lax.axis_index("row"), lax.axis_index("col")
    z, y_lo, l, y_hi = rem(r, Z), div(r, Z), rem(c, L), div(c, L)
    yy = y_hi * YL + y_lo

    def at(y_at, z_at, l_at):
        return (rem(y_at, YL) * Z + z_at, div(y_at, YL) * L + l_at)

    def send(src, dst, ss, rs, dev):
        pltpu.make_async_remote_copy(src_ref=src, dst_ref=dst, send_sem=ss, recv_sem=rs,
                                     device_id=dev, device_id_type=MESH).start()

    def done(ref, sem):
        pltpu.make_async_copy(ref, ref, sem).wait()

    q = rem(r + c, N_ROW)
    source = at(rem(yy + y_hi + div(z + l, Z), Y), rem(z + l, Z), l)
    users = []
    for hi in range(YH):
        u_row = rem(r + 2 * N_ROW - L * hi - l, N_ROW)
        u_y = rem(YL * hi + div(u_row, Z) + hi + div(rem(u_row, Z) + l, Z), Y)
        here = u_y == yy
        if hi == 0:
            here = jnp.logical_and(here, l != 0)
        users.append((here, (u_row, L * hi + l)))
    reads = c != 0

    barrier = pltpu.get_barrier_semaphore()

    @pl.when(reads)
    def _():
        pl.semaphore_signal(barrier, inc=1, device_id=source, device_id_type=MESH)

    def greet(n, sem, place):
        def one(k, carry):
            pl.semaphore_signal(sem, inc=1, device_id=place(k), device_id_type=MESH)
            return carry
        lax.fori_loop(1, n, one, 0)

    greet(Z, barrier, lambda k: at(yy, rem(z + k, Z), l))
    greet(Y, barrier, lambda k: at(rem(yy + k, Y), z, l))
    greet(L, barrier, lambda k: at(yy, z, rem(l + k, L)))

    pltpu.make_async_copy(h_ref, h, load_sem.at[0]).start()
    pltpu.make_async_copy(x_ref, x, load_sem.at[1]).start()
    pltpu.make_async_copy(p_ref, p, load_sem.at[2]).start()

    users_here = users[0][0].astype(jnp.int32) + users[1][0].astype(jnp.int32)
    pl.semaphore_wait(barrier, Z - 1 + Y - 1 + L - 1 + users_here)

    for i, (here, place) in enumerate(users):
        @pl.when(here)
        def _(i=i, place=place):
            send(x_ref, x_far, xs_sem.at[i], x_sem, place)

    @pl.when(jnp.logical_not(reads))
    def _():
        pltpu.make_async_copy(x_ref, x_far, x_sem).start()
        pltpu.make_async_copy(p_ref, p_far, p_sem).start()

    greet(Y, step2, lambda k: at(rem(yy + k, Y), z, l))
    pl.semaphore_wait(step2, Y - 1)
    greet(Z, step3, lambda k: at(yy, rem(z + k, Z), l))
    pltpu.make_async_copy(h_ref, h, load_sem.at[0]).wait()
    pltpu.make_async_copy(x_ref, x, load_sem.at[1]).wait()
    pltpu.make_async_copy(p_ref, p, load_sem.at[2]).wait()

    def blocks(ref, places):
        found = [ref[:, :B]] * NB
        for b in range(1, SEGB):
            here = ref[:, b * B : (b + 1) * B]
            found = [jnp.where(places[n] == b, here, found[n]) for n in range(NB)]
        return found

    def spread(terms, places, out):
        for b in range(SEGB):
            total = jnp.where(places[0] == b, terms[0], 0.0)
            for n in range(1, NB):
                total = total + jnp.where(places[n] == b, terms[n], 0.0)
            out[:, b * B : (b + 1) * B] = total

    row_at = [jnp.full((K, B), rows_ref[n], jnp.int32) for n in range(NB)]
    col_at = [jnp.full((K, B), cols_ref[n], jnp.int32) for n in range(NB)]
    x_row, p_row = blocks(x, row_at), blocks(p, row_at)
    both = [nn(jnp.concatenate([x_row[n], p_row[n]], 0), h[n]) for n in range(NB)]
    spread([both[n][:K] for n in range(NB)], col_at, m)

    pl.semaphore_wait(step3, Z - 1)

    def send_m(k, carry):
        j = rem(c + k, N_COL)
        src, dst = m.at[:, pl.ds(pl.multiple_of(j * SHARE, SHARE), SHARE)], got_m.at[c]
        local = jnp.logical_and(c == 0, k == 0)

        @pl.when(local)
        def _():
            pltpu.make_async_copy(src, dst, m_sem).start()

        @pl.when(jnp.logical_not(local))
        def _():
            send(src, dst, ms_sem, m_sem, (q, j))
        return carry

    lax.fori_loop(0, N_COL, send_m, 0)

    done(x_far, x_sem)
    x_col = blocks(x_far, col_at)
    direct = [nt(x_col[n], h[n]) for n in range(NB)]
    spread(direct, row_at, d)

    def send_d(k, carry):
        j = rem(c + k, N_COL)
        send(d.at[:, pl.ds(pl.multiple_of(j * SHARE, SHARE), SHARE)], got_d.at[c], ds_sem, d_sem, (r, j))
        return carry

    own = pl.ds(pl.multiple_of(c * SHARE, SHARE), SHARE)
    pltpu.make_async_copy(d.at[:, own], got_d.at[c], d_sem).start()
    lax.fori_loop(1, N_COL, send_d, 0)

    y_par, y_pair = rem(yy, 2), div(yy, 2)
    slot_a = y_par * L + l
    slot_b = y_pair * Z + z

    def first(i, tile):
        mine[i, 0] = tile
        pltpu.make_async_copy(mine.at[i, 0], buf_a.at[i, slot_a], a_sem.at[i]).start()

        def one(k, carry):
            y_to = 2 * y_pair + rem(y_par + div(k, L), 2)
            send(mine.at[i, 0], buf_a.at[i, slot_a], as_sem.at[i], a_sem.at[i], at(y_to, z, rem(l + k, L)))
            return carry
        lax.fori_loop(1, 2 * L, one, 0)

    def second(i):
        done(buf_a.at[i], a_sem.at[i])
        total = buf_a[i, 0]
        for s in range(1, 2 * L):
            total = total + buf_a[i, s]
        mine[i, 1] = total
        pltpu.make_async_copy(mine.at[i, 1], buf_b.at[i, slot_b], b_sem.at[i]).start()

        def one(k, carry):
            y_to = 2 * rem(y_pair + div(k, Z), Y // 2) + y_par
            send(mine.at[i, 1], buf_b.at[i, slot_b], bs_sem.at[i], b_sem.at[i], at(y_to, rem(z + k, Z), l))
            return carry
        lax.fori_loop(1, Z * Y // 2, one, 0)

    def third(i):
        done(buf_b.at[i], b_sem.at[i])
        total = buf_b[i, 0]
        for s in range(1, Z * Y // 2):
            total = total + buf_b[i, s]
        return total

    m_x = jnp.concatenate([both[n][:K] for n in range(NB)], 1)
    m_p = jnp.concatenate([both[n][K:] for n in range(NB)], 1)
    xc = jnp.concatenate(x_col, 1)
    first(0, nt(m_x, padded(xc)))

    for i, (here, place) in enumerate(users):
        @pl.when(here)
        def _(i=i, place=place):
            send(p_ref, p_far, ps_sem.at[i], p_sem, place)

    second(0)

    done(got_m, m_sem)
    done(got_d, d_sem)
    total = got_d[0]
    for s in range(1, N_COL):
        total = total + got_d[s]
    for s in range(N_COL):
        total = total + got_m[s]
    piece[...] = total
    pltpu.make_async_copy(piece, y.at[:, own], y_sem).start()

    def send_y(k, carry):
        local = jnp.logical_and(c == 0, k == 0)

        @pl.when(local)
        def _():
            pltpu.make_async_copy(piece, y_far.at[:, own], yfar_sem).start()

        @pl.when(jnp.logical_not(local))
        def _():
            send(piece, y_far.at[:, own], yfs_sem, yfar_sem, (rem(r + N_ROW - k, N_ROW), k))

        @pl.when(k != 0)
        def _():
            send(piece, y.at[:, own], ys_sem, y_sem, (r, rem(c + k, N_COL)))
        return carry

    lax.fori_loop(0, N_COL, send_y, 0)

    cross = third(0)[:, :K]
    theta = (cross + transposed(cross)) / ROWS
    x_own, p_own = x[:, own], p[:, own]
    taken = nn(theta, jnp.concatenate(x_row + x_col + [x_own], 1))
    basis = jnp.concatenate([total - taken[:, 2 * NB * B :], x_own, p_own], 0)
    first(1, packed(nt(basis, padded(basis))))

    done(p_far, p_sem)
    p_col = jnp.concatenate(blocks(p_far, col_at), 1)
    second(1)

    done(y, y_sem)
    y_row = blocks(y, row_at)
    m_r = jnp.concatenate([nn(y_row[n] - taken[:, n * B : (n + 1) * B], h[n]) for n in range(NB)], 1)

    done(y_far, yfar_sem)
    r_col = jnp.concatenate(blocks(y_far, col_at), 1) - taken[:, NB * B : 2 * NB * B]
    first(2, packed(nt(jnp.concatenate([m_r, m_x, m_p], 0), padded(jnp.concatenate([r_col, xc, p_col], 0)))))
    second(2)

    inverse = inverse_factor(unpacked(third(1)) / ROWS)[:, :24]
    q_ref[...] = nn(inverse, basis)

    half = unpacked(third(2))[:, :24]
    ray_ref[...] = nt(nn(inverse, (half + transposed(half)) / ROWS), inverse)

    for i, (here, place) in enumerate(users):
        @pl.when(here)
        def _(i=i):
            done(x_ref, xs_sem.at[i])
            done(p_ref, ps_sem.at[i])

    @pl.when(reads)
    def _():
        done(got_m, ms_sem)
        done(got_m, yfs_sem)

    @pl.when(jnp.logical_not(reads))
    def _():
        done(got_m.at[pl.ds(0, N_COL - 1)], ms_sem)
        done(got_m.at[pl.ds(0, N_COL - 1)], yfs_sem)

    done(got_d.at[pl.ds(0, N_COL - 1)], ds_sem)
    done(got_d.at[pl.ds(0, N_COL - 1)], ys_sem)
    for i in range(3):
        done(buf_a.at[i, pl.ds(0, 2 * L - 1)], as_sem.at[i])
        done(buf_b.at[i, pl.ds(0, Z * Y // 2 - 1)], bs_sem.at[i])


def body(hamiltonian_blocks, block_rows, block_cols, current_states, previous_steps):
    vmem, smem, anywhere = (pl.BlockSpec(memory_space=s) for s in (pltpu.VMEM, pltpu.SMEM, pl.ANY))
    dma, regular = pltpu.SemaphoreType.DMA, pltpu.SemaphoreType.REGULAR
    return pl.pallas_call(
        kernel,
        out_shape=(jax.ShapeDtypeStruct((3 * K, SHARE), F32), jax.ShapeDtypeStruct((3 * K, 3 * K), F32)),
        in_specs=[smem, smem, anywhere, anywhere, anywhere],
        out_specs=(vmem, vmem),
        scratch_shapes=[
            pltpu.VMEM((NB, B, B), F32),
            pltpu.VMEM((K, SEG), F32),
            pltpu.VMEM((K, SEG), F32),
            pltpu.VMEM((K, SEG), F32),
            pltpu.VMEM((K, SEG), F32),
            pltpu.VMEM((K, SEG), F32),
            pltpu.VMEM((K, SEG), F32),
            pltpu.VMEM((N_COL, K, SHARE), F32),
            pltpu.VMEM((N_COL, K, SHARE), F32),
            pltpu.VMEM((K, SHARE), F32),
            pltpu.VMEM((K, SEG), F32),
            pltpu.VMEM((K, SEG), F32),
            pltpu.VMEM((3, 2, 8, B), F32),
            pltpu.VMEM((3, 2 * L, 8, B), F32),
            pltpu.VMEM((3, Z * Y // 2, 8, B), F32),
            dma((3,)), dma, dma, dma((2,)), dma((2,)), dma, dma, dma, dma,
            dma, dma, dma, dma, dma((3,)), dma((3,)), dma((3,)), dma((3,)), regular, regular,
        ],
        compiler_params=pltpu.CompilerParams(collective_id=0, has_side_effects=True, vmem_limit_bytes=32 * 1024 * 1024),
        name="lobpcg_step",
    )(block_rows.reshape(NB), block_cols.reshape(NB), hamiltonian_blocks.reshape(NB, B, B), current_states, previous_steps)


def solution(mesh):
    return jax.shard_map(
        body,
        mesh=mesh,
        in_specs=(
            P("row", "col", None, None, None),
            P("row", "col", None),
            P("row", "col", None),
            P(None, "row"),
            P(None, "row"),
        ),
        out_specs=(P(None, ("row", "col")), P()),
        check_vma=False,
    )
```

```python
import functools

import jax
import jax.numpy as jnp
from jax import lax
from jax.experimental import pallas as pl
from jax.experimental.pallas import tpu as pltpu
from jax.sharding import PartitionSpec as P

MESH = pl.DeviceIdType.MESH
F32 = jnp.float32
exactness = lax.Precision.HIGHEST

Z, YL, YH, L = 8, 4, 2, 8
Y = YL * YH
N_ROW, N_COL = Z * YL, L * YH
K, B, SEGB, NB = 8, 128, 32, 4
SEG = SEGB * B
SHARE = SEG // N_COL
ROWS = N_ROW * SEG
rem, div = lax.rem, lax.div


def nn(a, b):
    return jnp.dot(a, b, precision=exactness, preferred_element_type=F32)


def nt(a, b):
    return lax.dot_general(a, b, (((1,), (1,)), ((), ())), precision=exactness, preferred_element_type=F32)


def lane_ids(shape):
    return lax.broadcasted_iota(jnp.int32, shape, 1)


def row_ids(shape):
    return lax.broadcasted_iota(jnp.int32, shape, 0)


def padded(a):
    return jnp.concatenate([a, jnp.zeros((B - a.shape[0], a.shape[1]), F32)], 0)


def packed(a):
    return a[0:8] + pltpu.roll(a[8:16], 32, 1) + pltpu.roll(a[16:24], 64, 1)


def unpacked(t):
    a = jnp.concatenate([t, pltpu.roll(t, 96, 1), pltpu.roll(t, 64, 1)], 0)
    return jnp.where(lane_ids(a.shape) < 24, a, 0.0)


def inverse_factor(gram):
    rows, lanes = row_ids(gram.shape), lane_ids(gram.shape)
    left = gram
    right = (rows == lanes).astype(F32)
    for j in range(24):
        pivot = left[j : j + 1, j : j + 1]
        factor = jnp.where(rows[:, :1] > j, left[:, j : j + 1] / pivot, 0.0)
        top, unit = left[j : j + 1], right[j : j + 1]
        left = left - factor * top
        right = right - factor * unit
    diagonal = jnp.sum(jnp.where(rows == lanes, left, 0.0), 1, keepdims=True)
    return right / jnp.sqrt(diagonal)


def kernel(rows_ref, cols_ref, h_ref, x_ref, p_ref, q_ref, ray_ref,
           rows, cols, h, x, x_far, p, p_far, p_pick, asked, wanted, d, m, got_d, got_m, piece, y, y_far, mine, buf_a, buf_b,
           load_sem, x_sem, p_sem, want_sem, wants_sem, xs_sem, ps_sem, d_sem, m_sem, ds_sem, ms_sem,
           y_sem, yfar_sem, ys_sem, yfs_sem, a_sem, b_sem, as_sem, bs_sem, step2, step3):
    r, c = lax.axis_index("row"), lax.axis_index("col")
    z, y_lo, l, y_hi = rem(r, Z), div(r, Z), rem(c, L), div(c, L)
    yy = y_hi * YL + y_lo

    def at(y_at, z_at, l_at):
        return (rem(y_at, YL) * Z + z_at, div(y_at, YL) * L + l_at)

    def send(src, dst, ss, rs, dev):
        pltpu.make_async_remote_copy(src_ref=src, dst_ref=dst, send_sem=ss, recv_sem=rs,
                                     device_id=dev, device_id_type=MESH).start()

    def done(ref, sem):
        pltpu.make_async_copy(ref, ref, sem).wait()

    q = rem(r + c, N_ROW)
    source = at(rem(yy + y_hi + div(z + l, Z), Y), rem(z + l, Z), l)
    users = []
    for hi in range(YH):
        u_row = rem(r + 2 * N_ROW - L * hi - l, N_ROW)
        u_y = rem(YL * hi + div(u_row, Z) + hi + div(rem(u_row, Z) + l, Z), Y)
        here = u_y == yy
        if hi == 0:
            here = jnp.logical_and(here, l != 0)
        users.append((here, (u_row, L * hi + l)))
    reads = c != 0

    barrier = pltpu.get_barrier_semaphore()

    @pl.when(reads)
    def _():
        pl.semaphore_signal(barrier, inc=1, device_id=source, device_id_type=MESH)

    def greet(n, sem, place):
        def one(k, carry):
            pl.semaphore_signal(sem, inc=1, device_id=place(k), device_id_type=MESH)
            return carry
        lax.fori_loop(1, n, one, 0)

    greet(Z, barrier, lambda k: at(yy, rem(z + k, Z), l))
    greet(Y, barrier, lambda k: at(rem(yy + k, Y), z, l))
    greet(L, barrier, lambda k: at(yy, z, rem(l + k, L)))

    loads = [pltpu.make_async_copy(src, dst, load_sem.at[i]) for i, (src, dst) in enumerate(
        ((rows_ref, rows), (cols_ref, cols), (x_ref, x), (h_ref, h), (p_ref, p)))]
    for load in loads:
        load.start()

    users_here = users[0][0].astype(jnp.int32) + users[1][0].astype(jnp.int32)
    pl.semaphore_wait(barrier, Z - 1 + Y - 1 + L - 1 + users_here)

    for i, (here, place) in enumerate(users):
        @pl.when(here)
        def _(i=i, place=place):
            send(x_ref, x_far, xs_sem.at[i], x_sem, place)

    @pl.when(jnp.logical_not(reads))
    def _():
        pltpu.make_async_copy(x_ref, x_far, x_sem).start()

    greet(Y, step2, lambda k: at(rem(yy + k, Y), z, l))
    pl.semaphore_wait(step2, Y - 1)
    greet(Z, step3, lambda k: at(yy, rem(z + k, Z), l))
    for load in loads:
        load.wait()

    def blocks(ref, places):
        found = [ref[:, :B]] * NB
        for b in range(1, SEGB):
            here = ref[:, b * B : (b + 1) * B]
            found = [jnp.where(places[n] == b, here, found[n]) for n in range(NB)]
        return found

    def spread(terms, places, out):
        for b in range(SEGB):
            total = jnp.where(places[0] == b, terms[0], 0.0)
            for n in range(1, NB):
                total = total + jnp.where(places[n] == b, terms[n], 0.0)
            out[:, b * B : (b + 1) * B] = total

    row_at = [jnp.full((K, B), rows[n], jnp.int32) for n in range(NB)]
    col_at = [jnp.full((K, B), cols[n], jnp.int32) for n in range(NB)]
    x_row, p_row = blocks(x, row_at), blocks(p, row_at)
    both = [nn(jnp.concatenate([x_row[n], p_row[n]], 0), h[n]) for n in range(NB)]
    spread([both[n][:K] for n in range(NB)], col_at, m)

    pl.semaphore_wait(step3, Z - 1)

    asks = jnp.zeros((8, B), jnp.int32)
    for n in range(NB):
        asks = jnp.where(row_ids((8, B)) == n, col_at[n], asks)
    asked[...] = asks

    @pl.when(reads)
    def _():
        for hi in range(YH):
            @pl.when(y_hi == hi)
            def _(hi=hi):
                send(asked, wanted.at[hi], wants_sem, want_sem.at[hi], source)

    near_last = (4, 5, 3, 6, 2, 7, 1, 0)
    for k in range(N_COL):
        j = rem(rem(y_hi + 1 + k // L, YH) * L + rem(l + near_last[k % L], L), N_COL)
        src, dst = m.at[:, pl.ds(pl.multiple_of(j * SHARE, SHARE), SHARE)], got_m.at[c]
        if k < N_COL - 1:
            send(src, dst, ms_sem, m_sem, (q, j))
        else:
            @pl.when(reads)
            def _(src=src, dst=dst, j=j):
                send(src, dst, ms_sem, m_sem, (q, j))

            @pl.when(jnp.logical_not(reads))
            def _(src=src, dst=dst):
                pltpu.make_async_copy(src, dst, m_sem).start()

    done(x_far, x_sem)
    x_col = blocks(x_far, col_at)
    direct = [nt(x_col[n], h[n]) for n in range(NB)]
    spread(direct, row_at, d)

    own = pl.ds(pl.multiple_of(c * SHARE, SHARE), SHARE)
    for k in range(N_COL - 1):
        j = rem(y_hi + 1 + k // L, YH) * L + rem(l + near_last[k % L], L)
        send(d.at[:, pl.ds(pl.multiple_of(j * SHARE, SHARE), SHARE)], got_d.at[c], ds_sem, d_sem, (r, j))
    pltpu.make_async_copy(d.at[:, own], got_d.at[c], d_sem).start()

    y_par, y_pair = rem(yy, 2), div(yy, 2)
    slot_a = y_par * L + l
    slot_b = y_pair * Z + z

    def first(i, tile):
        mine[i, 0] = tile
        for k in range(2 * L - 1):
            y_to = 2 * y_pair + rem(y_par + 1 + k // L, 2)
            send(mine.at[i, 0], buf_a.at[i, slot_a], as_sem.at[i], a_sem.at[i], at(y_to, z, rem(l + near_last[k % L], L)))
        pltpu.make_async_copy(mine.at[i, 0], buf_a.at[i, slot_a], a_sem.at[i]).start()

    def second(i):
        done(buf_a.at[i], a_sem.at[i])
        total = buf_a[i, 0]
        for s in range(1, 2 * L):
            total = total + buf_a[i, s]
        mine[i, 1] = total
        for y_k in (2, 1, 3, 0):
            for z_k in near_last:
                if y_k or z_k:
                    y_to = 2 * rem(y_pair + y_k, Y // 2) + y_par
                    send(mine.at[i, 1], buf_b.at[i, slot_b], bs_sem.at[i], b_sem.at[i], at(y_to, rem(z + z_k, Z), l))
        pltpu.make_async_copy(mine.at[i, 1], buf_b.at[i, slot_b], b_sem.at[i]).start()

    def third(i):
        done(buf_b.at[i], b_sem.at[i])
        total = buf_b[i, 0]
        for s in range(1, Z * Y // 2):
            total = total + buf_b[i, s]
        return total

    m_x = jnp.concatenate([both[n][:K] for n in range(NB)], 1)
    m_p = jnp.concatenate([both[n][K:] for n in range(NB)], 1)
    xc = jnp.concatenate(x_col, 1)
    first(0, nt(m_x, padded(xc)) + nt(xc, padded(m_x)))

    for i, (here, place) in enumerate(users):
        @pl.when(here)
        def _(i=i, place=place):
            done(wanted.at[i], want_sem.at[i])
            asks = wanted[i]
            found = blocks(p, [jnp.broadcast_to(asks[n : n + 1], (K, B)) for n in range(NB)])
            p_pick[i] = jnp.concatenate(found, 1)
            send(p_pick.at[i], p_far, ps_sem.at[i], p_sem, place)

    @pl.when(jnp.logical_not(reads))
    def _():
        p_far[...] = jnp.concatenate(blocks(p, col_at), 1)

    second(0)

    done(got_m, m_sem)
    done(got_d, d_sem)
    total = got_d[0]
    for s in range(1, N_COL):
        total = total + got_d[s]
    for s in range(N_COL):
        total = total + got_m[s]
    piece[...] = total
    for k in range(N_COL):
        hi, l_to = rem(y_hi + 1 + k // L, YH), near_last[k % L]
        to = hi * L + l_to
        place = (rem(r + N_ROW - to, N_ROW), to)
        if l_to:
            send(piece, y_far.at[:, own], yfs_sem, yfar_sem, place)
        else:
            local = jnp.logical_and(c == 0, to == 0)

            @pl.when(local)
            def _():
                pltpu.make_async_copy(piece, y_far.at[:, own], yfar_sem).start()

            @pl.when(jnp.logical_not(local))
            def _(place=place):
                send(piece, y_far.at[:, own], yfs_sem, yfar_sem, place)

        if k < N_COL - 1:
            send(piece, y.at[:, own], ys_sem, y_sem, (r, hi * L + rem(l + l_to, L)))
    pltpu.make_async_copy(piece, y.at[:, own], y_sem).start()

    theta = third(0)[:, :K] / ROWS
    x_own, p_own = x[:, own], p[:, own]
    taken = nn(theta, jnp.concatenate(x_row + x_col + [x_own], 1))
    basis = jnp.concatenate([total - taken[:, 2 * NB * B :], x_own, p_own], 0)
    first(1, packed(nt(basis, padded(basis))))

    @pl.when(reads)
    def _():
        done(p_far, p_sem)

    p_col = p_far[...]
    second(1)

    done(y, y_sem)
    y_row = blocks(y, row_at)
    m_r = jnp.concatenate([nn(y_row[n] - taken[:, n * B : (n + 1) * B], h[n]) for n in range(NB)], 1)

    done(y_far, yfar_sem)
    r_col = jnp.concatenate(blocks(y_far, col_at), 1) - taken[:, NB * B : 2 * NB * B]
    left, right = jnp.concatenate([m_r, m_x, m_p], 0), jnp.concatenate([r_col, xc, p_col], 0)
    first(2, packed(nt(left, padded(right)) + nt(right, padded(left))))
    second(2)

    inverse = inverse_factor(unpacked(third(1)) / ROWS)[:, :24]
    q_ref[...] = nn(inverse, basis)

    for i, (here, place) in enumerate(users):
        @pl.when(here)
        def _(i=i):
            done(x_ref, xs_sem.at[i])

    @pl.when(reads)
    def _():
        done(asked, wants_sem)

    for i, (here, place) in enumerate(users):
        @pl.when(here)
        def _(i=i):
            done(p_pick.at[i], ps_sem.at[i])

    @pl.when(reads)
    def _():
        done(got_m, ms_sem)

    @pl.when(jnp.logical_not(reads))
    def _():
        done(got_m.at[pl.ds(0, N_COL - 1)], ms_sem)

    @pl.when(reads)
    def _():
        done(got_m, yfs_sem)

    @pl.when(jnp.logical_not(reads))
    def _():
        done(got_m.at[pl.ds(0, N_COL - 1)], yfs_sem)

    done(got_d.at[pl.ds(0, N_COL - 1)], ys_sem)

    done(got_d.at[pl.ds(0, N_COL - 1)], ds_sem)

    done(buf_a.at[0, pl.ds(0, 2 * L - 1)], as_sem.at[0])
    done(buf_b.at[0, pl.ds(0, Z * Y // 2 - 1)], bs_sem.at[0])
    done(buf_a.at[1, pl.ds(0, 2 * L - 1)], as_sem.at[1])
    done(buf_b.at[1, pl.ds(0, Z * Y // 2 - 1)], bs_sem.at[1])
    done(buf_a.at[2, pl.ds(0, 2 * L - 1)], as_sem.at[2])

    ray_ref[...] = nt(nn(inverse, unpacked(third(2))[:, :24] / ROWS), inverse)
    done(buf_b.at[2, pl.ds(0, Z * Y // 2 - 1)], bs_sem.at[2])


def body(hamiltonian_blocks, block_rows, block_cols, current_states, previous_steps):
    vmem, anywhere = (pl.BlockSpec(memory_space=s) for s in (pltpu.VMEM, pl.ANY))
    dma, regular = pltpu.SemaphoreType.DMA, pltpu.SemaphoreType.REGULAR
    return pl.pallas_call(
        kernel,
        out_shape=(jax.ShapeDtypeStruct((3 * K, SHARE), F32), jax.ShapeDtypeStruct((3 * K, 3 * K), F32)),
        in_specs=[anywhere, anywhere, anywhere, anywhere, anywhere],
        out_specs=(vmem, vmem),
        scratch_shapes=[
            pltpu.SMEM((NB,), jnp.int32),
            pltpu.SMEM((NB,), jnp.int32),
            pltpu.VMEM((NB, B, B), F32),
            pltpu.VMEM((K, SEG), F32),
            pltpu.VMEM((K, SEG), F32),
            pltpu.VMEM((K, SEG), F32),
            pltpu.VMEM((K, NB * B), F32),
            pltpu.VMEM((YH, K, NB * B), F32),
            pltpu.VMEM((8, B), jnp.int32),
            pltpu.VMEM((YH, 8, B), jnp.int32),
            pltpu.VMEM((K, SEG), F32),
            pltpu.VMEM((K, SEG), F32),
            pltpu.VMEM((N_COL, K, SHARE), F32),
            pltpu.VMEM((N_COL, K, SHARE), F32),
            pltpu.VMEM((K, SHARE), F32),
            pltpu.VMEM((K, SEG), F32),
            pltpu.VMEM((K, SEG), F32),
            pltpu.VMEM((3, 2, 8, B), F32),
            pltpu.VMEM((3, 2 * L, 8, B), F32),
            pltpu.VMEM((3, Z * Y // 2, 8, B), F32),
            dma((5,)), dma, dma, dma((YH,)), dma, dma((2,)), dma((2,)), dma, dma, dma, dma,
            dma, dma, dma, dma, dma((3,)), dma((3,)), dma((3,)), dma((3,)), regular, regular,
        ],
        compiler_params=pltpu.CompilerParams(collective_id=0, has_side_effects=True, vmem_limit_bytes=62 * 1024 * 1024),
        name="lobpcg_step",
    )(block_rows.reshape(NB), block_cols.reshape(NB), hamiltonian_blocks.reshape(NB, B, B), current_states, previous_steps)


def solution(mesh):
    return jax.shard_map(
        body,
        mesh=mesh,
        in_specs=(
            P("row", "col", None, None, None),
            P("row", "col", None),
            P("row", "col", None),
            P(None, "row"),
            P(None, "row"),
        ),
        out_specs=(P(None, ("row", "col")), P()),
        check_vma=False,
    )
```

```python
import functools

import jax
import jax.numpy as jnp
from jax import lax
from jax.experimental import pallas as pl
from jax.experimental.pallas import tpu as pltpu
from jax.sharding import PartitionSpec as P

MESH = pl.DeviceIdType.MESH
F32 = jnp.float32
exactness = lax.Precision.HIGHEST

Z, YL, YH, L = 8, 4, 2, 8
Y = YL * YH
N_ROW, N_COL = Z * YL, L * YH
K, B, SEGB, NB = 8, 128, 32, 4
SEG = SEGB * B
SHARE, OWNED = SEG // N_COL, SEG // L
ROWS = N_ROW * SEG
rem, div = lax.rem, lax.div


def nn(a, b):
    return jnp.dot(a, b, precision=exactness, preferred_element_type=F32)


def nt(a, b):
    return lax.dot_general(a, b, (((1,), (1,)), ((), ())), precision=exactness, preferred_element_type=F32)


def lane_ids(shape):
    return lax.broadcasted_iota(jnp.int32, shape, 1)


def row_ids(shape):
    return lax.broadcasted_iota(jnp.int32, shape, 0)


def padded(a):
    return jnp.concatenate([a, jnp.zeros((B - a.shape[0], a.shape[1]), F32)], 0)


def packed(a):
    return a[0:8] + pltpu.roll(a[8:16], 32, 1) + pltpu.roll(a[16:24], 64, 1)


def unpacked(t):
    a = jnp.concatenate([t, pltpu.roll(t, 96, 1), pltpu.roll(t, 64, 1)], 0)
    return jnp.where(lane_ids(a.shape) < 24, a, 0.0)


def inverse_factor(gram):
    rows, lanes = row_ids(gram.shape), lane_ids(gram.shape)
    left = gram
    right = (rows == lanes).astype(F32)
    for j in range(24):
        pivot = left[j : j + 1, j : j + 1]
        factor = jnp.where(rows[:, :1] > j, left[:, j : j + 1] / pivot, 0.0)
        top, unit = left[j : j + 1], right[j : j + 1]
        left = left - factor * top
        right = right - factor * unit
    diagonal = jnp.sum(jnp.where(rows == lanes, left, 0.0), 1, keepdims=True)
    return right / jnp.sqrt(diagonal)


def kernel(rows_ref, cols_ref, h_ref, x_ref, p_ref, q_ref, ray_ref,
           rows, cols, h, x, x_far, p, p_far, p_pick, asked, wanted, m, m_near, d, got, part, other, piece, y, y_far, mine,
           buf_a, buf_b, load_sem, x_sem, xs_sem, m_sem, ms_sem, want_sem, wants_sem, p_sem, ps_sem, d_sem, ds_sem, o_sem, os_sem,
           y_sem, ys_sem, yfar_sem, yfs_sem, a_sem, b_sem, as_sem, bs_sem, step2, step3):
    r, c = lax.axis_index("row"), lax.axis_index("col")
    z, y_lo, l, y_hi = rem(r, Z), div(r, Z), rem(c, L), div(c, L)
    yy = y_hi * YL + y_lo

    def at(y_at, z_at, l_at):
        return (rem(y_at, YL) * Z + z_at, div(y_at, YL) * L + l_at)

    def send(src, dst, ss, rs, dev):
        pltpu.make_async_remote_copy(src_ref=src, dst_ref=dst, send_sem=ss, recv_sem=rs,
                                     device_id=dev, device_id_type=MESH).start()

    def done(ref, sem):
        pltpu.make_async_copy(ref, ref, sem).wait()

    reads = c != 0
    q = rem(r + c, N_ROW)
    turned = jnp.logical_and(div(q, Z) == 0, z + l >= Z).astype(jnp.int32)
    source = (q, rem(y_hi + turned, YH) * L + l)

    def user(l_at):
        over = jnp.logical_and(y_lo == 0, z < l_at).astype(jnp.int32)
        to = rem(y_hi + over, YH) * L + l_at
        return rem(r + N_ROW - to, N_ROW), to

    barrier = pltpu.get_barrier_semaphore()

    @pl.when(reads)
    def _():
        pl.semaphore_signal(barrier, inc=1, device_id=source, device_id_type=MESH)
        pl.semaphore_signal(barrier, inc=1, device_id=user(l), device_id_type=MESH)

    def greet(n, sem, place):
        for k in range(1, n):
            pl.semaphore_signal(sem, inc=1, device_id=place(k), device_id_type=MESH)

    greet(Z, barrier, lambda k: at(yy, rem(z + k, Z), l))
    greet(Y, barrier, lambda k: at(rem(yy + k, Y), z, l))
    greet(L, barrier, lambda k: at(yy, z, rem(l + k, L)))

    loads = [pltpu.make_async_copy(src, dst, load_sem.at[i]) for i, (src, dst) in enumerate(
        ((rows_ref, rows), (cols_ref, cols), (x_ref, x), (h_ref, h), (p_ref, p)))]
    for load in loads:
        load.start()

    pl.semaphore_wait(barrier, Z - 1 + Y - 1 + L - 1 + 2 * reads.astype(jnp.int32))

    @pl.when(reads)
    def _():
        send(x_ref, x_far, xs_sem, x_sem, user(l))

    @pl.when(jnp.logical_not(reads))
    def _():
        pltpu.make_async_copy(x_ref, x_far, x_sem).start()

    greet(Y, step2, lambda k: at(rem(yy + k, Y), z, l))

    def blocks(ref, places):
        found = [ref[:, :B]] * NB
        for b in range(1, SEGB):
            here = ref[:, b * B : (b + 1) * B]
            found = [jnp.where(places[n] == b, here, found[n]) for n in range(NB)]
        return found

    for load in loads[:4]:
        load.wait()
    row_at = [jnp.full((K, B), rows[n], jnp.int32) for n in range(NB)]
    col_at = [jnp.full((K, B), cols[n], jnp.int32) for n in range(NB)]
    x_row = blocks(x, row_at)
    m_x = jnp.concatenate([nn(x_row[n], h[n]) for n in range(NB)], 1)

    asks = jnp.zeros((8, B), jnp.int32)
    for n in range(NB):
        asks = jnp.where(row_ids((8, B)) == n, col_at[n], asks)

    @pl.when(reads)
    def _():
        m[...] = m_x
        asked[...] = asks
        send(m, m_near, ms_sem, m_sem, source)
        send(asked, wanted, wants_sem, want_sem, source)

    @pl.when(jnp.logical_not(reads))
    def _():
        m_near[...] = m_x
        wanted[...] = asks

    pl.semaphore_wait(step2, Y - 1)
    greet(Z, step3, lambda k: at(yy, rem(z + k, Z), l))
    loads[4].wait()
    p_row = blocks(p, row_at)
    m_p = jnp.concatenate([nn(p_row[n], h[n]) for n in range(NB)], 1)

    done(x_far, x_sem)
    x_col = blocks(x_far, col_at)
    direct = [nt(x_col[n], h[n]) for n in range(NB)]
    xc = jnp.concatenate(x_col, 1)

    @pl.when(reads)
    def _():
        done(m_near, m_sem)
        done(wanted, want_sem)

    want = wanted[...]
    want_at = [jnp.broadcast_to(want[n : n + 1], (K, B)) for n in range(NB)]
    terms = [direct[n] for n in range(NB)] + [m_near[:, n * B : (n + 1) * B] for n in range(NB)]
    for b in range(SEGB):
        total = jnp.zeros((K, B), F32)
        for place, term in zip(row_at + want_at, terms):
            total = total + jnp.where(place == b, term, 0.0)
        d[:, b * B : (b + 1) * B] = total
    pl.semaphore_wait(step3, Z - 1)

    near_last = (4, 5, 3, 6, 2, 7, 1, 0)

    def share(l_at):
        return pl.ds(pl.multiple_of(l_at * OWNED, OWNED), OWNED)

    for k in near_last[:-1]:
        j = rem(l + k, L)
        send(d.at[:, share(j)], got.at[l], ds_sem, d_sem, at(yy, z, j))
    pltpu.make_async_copy(d.at[:, share(l)], got.at[l], d_sem).start()

    y_par, y_pair = rem(yy, 2), div(yy, 2)
    slot_a = y_par * L + l
    slot_b = y_pair * Z + z

    def first(i, tile):
        mine[i, 0] = tile
        for k in range(2 * L - 1):
            y_to = 2 * y_pair + rem(y_par + 1 + k // L, 2)
            send(mine.at[i, 0], buf_a.at[i, slot_a], as_sem.at[i], a_sem.at[i], at(y_to, z, rem(l + near_last[k % L], L)))
        pltpu.make_async_copy(mine.at[i, 0], buf_a.at[i, slot_a], a_sem.at[i]).start()

    def second(i):
        done(buf_a.at[i], a_sem.at[i])
        total = buf_a[i, 0]
        for s in range(1, 2 * L):
            total = total + buf_a[i, s]
        mine[i, 1] = total
        for y_k in (2, 1, 3, 0):
            for z_k in near_last:
                if y_k or z_k:
                    y_to = 2 * rem(y_pair + y_k, Y // 2) + y_par
                    send(mine.at[i, 1], buf_b.at[i, slot_b], bs_sem.at[i], b_sem.at[i], at(y_to, rem(z + z_k, Z), l))
        pltpu.make_async_copy(mine.at[i, 1], buf_b.at[i, slot_b], b_sem.at[i]).start()

    def third(i):
        done(buf_b.at[i], b_sem.at[i])
        total = buf_b[i, 0]
        for s in range(1, Z * Y // 2):
            total = total + buf_b[i, s]
        return total

    first(0, nt(m_x, padded(xc)) + nt(xc, padded(m_x)))

    @pl.when(reads)
    def _():
        p_pick[...] = jnp.concatenate(blocks(p, want_at), 1)
        send(p_pick, p_far, ps_sem, p_sem, user(l))

    @pl.when(jnp.logical_not(reads))
    def _():
        p_far[...] = jnp.concatenate(blocks(p, col_at), 1)

    done(got, d_sem)
    total = got[0]
    for s in range(1, L):
        total = total + got[s]
    part[...] = total
    send(part, other, os_sem, o_sem, (r, rem(y_hi + 1, YH) * L + l))
    second(0)
    done(other, o_sem)
    total = part[...] + other[...]
    piece[...] = total

    mine_of = share(l)
    for l_to in near_last:
        if l_to:
            send(piece, y_far.at[:, mine_of], yfs_sem, yfar_sem, user(l_to))
        else:
            @pl.when(c == 0)
            def _():
                pltpu.make_async_copy(piece, y_far.at[:, mine_of], yfar_sem).start()

            @pl.when(reads)
            def _():
                send(piece, y_far.at[:, mine_of], yfs_sem, yfar_sem, user(0))

    for k in near_last[:-1]:
        send(piece, y.at[:, mine_of], ys_sem, y_sem, at(yy, z, rem(l + k, L)))
    pltpu.make_async_copy(piece, y.at[:, mine_of], y_sem).start()

    theta = third(0)[:, :K] / ROWS
    half = pl.ds(pl.multiple_of(l * OWNED + y_hi * SHARE, SHARE), SHARE)
    half_of = pl.ds(pl.multiple_of(y_hi * SHARE, SHARE), SHARE)
    own = pl.ds(pl.multiple_of(c * SHARE, SHARE), SHARE)
    taken = nn(theta, jnp.concatenate(x_row + x_col + [x[:, half], x[:, own]], 1))
    basis = jnp.concatenate([piece[:, half_of] - taken[:, 2 * NB * B : 2 * NB * B + SHARE], x[:, half], p[:, half]], 0)
    first(1, packed(nt(basis, padded(basis))))

    @pl.when(reads)
    def _():
        done(p_far, p_sem)

    p_col = p_far[...]
    done(y, y_sem)
    y_row = blocks(y, row_at)
    m_r = jnp.concatenate([nn(y_row[n] - taken[:, n * B : (n + 1) * B], h[n]) for n in range(NB)], 1)

    done(y_far, yfar_sem)
    r_col = jnp.concatenate(blocks(y_far, col_at), 1) - taken[:, NB * B : 2 * NB * B]
    left, right = jnp.concatenate([m_r, m_x, m_p], 0), jnp.concatenate([r_col, xc, p_col], 0)
    first(2, packed(nt(left, padded(right)) + nt(right, padded(left))))
    second(1)
    second(2)
    inverse = inverse_factor(unpacked(third(1)) / ROWS)[:, :24]
    q_ref[...] = nn(inverse, jnp.concatenate([y[:, own] - taken[:, 2 * NB * B + SHARE :], x[:, own], p[:, own]], 0))

    @pl.when(reads)
    def _():
        done(x_ref, xs_sem)

    @pl.when(reads)
    def _():
        done(m, ms_sem)
        done(asked, wants_sem)

    @pl.when(reads)
    def _():
        done(p_pick, ps_sem)

    done(got.at[pl.ds(0, L - 1)], ds_sem)
    done(part, os_sem)
    done(got.at[pl.ds(0, L - 1)], yfs_sem)
    done(got.at[pl.ds(0, L - 1)], ys_sem)

    @pl.when(reads)
    def _():
        done(piece, yfs_sem)

    done(buf_a.at[0, pl.ds(0, 2 * L - 1)], as_sem.at[0])
    done(buf_b.at[0, pl.ds(0, Z * Y // 2 - 1)], bs_sem.at[0])
    done(buf_a.at[1, pl.ds(0, 2 * L - 1)], as_sem.at[1])
    done(buf_b.at[1, pl.ds(0, Z * Y // 2 - 1)], bs_sem.at[1])
    done(buf_a.at[2, pl.ds(0, 2 * L - 1)], as_sem.at[2])

    ray_ref[...] = nt(nn(inverse, unpacked(third(2))[:, :24] / ROWS), inverse)
    done(buf_b.at[2, pl.ds(0, Z * Y // 2 - 1)], bs_sem.at[2])


def body(hamiltonian_blocks, block_rows, block_cols, current_states, previous_steps):
    vmem, anywhere = (pl.BlockSpec(memory_space=s) for s in (pltpu.VMEM, pl.ANY))
    dma, regular = pltpu.SemaphoreType.DMA, pltpu.SemaphoreType.REGULAR
    return pl.pallas_call(
        kernel,
        out_shape=(jax.ShapeDtypeStruct((3 * K, SHARE), F32), jax.ShapeDtypeStruct((3 * K, 3 * K), F32)),
        in_specs=[anywhere, anywhere, anywhere, anywhere, anywhere],
        out_specs=(vmem, vmem),
        scratch_shapes=[
            pltpu.SMEM((NB,), jnp.int32),
            pltpu.SMEM((NB,), jnp.int32),
            pltpu.VMEM((NB, B, B), F32),
            pltpu.VMEM((K, SEG), F32),
            pltpu.VMEM((K, SEG), F32),
            pltpu.VMEM((K, SEG), F32),
            pltpu.VMEM((K, NB * B), F32),
            pltpu.VMEM((K, NB * B), F32),
            pltpu.VMEM((8, B), jnp.int32),
            pltpu.VMEM((8, B), jnp.int32),
            pltpu.VMEM((K, NB * B), F32),
            pltpu.VMEM((K, NB * B), F32),
            pltpu.VMEM((K, SEG), F32),
            pltpu.VMEM((L, K, OWNED), F32),
            pltpu.VMEM((K, OWNED), F32),
            pltpu.VMEM((K, OWNED), F32),
            pltpu.VMEM((K, OWNED), F32),
            pltpu.VMEM((K, SEG), F32),
            pltpu.VMEM((K, SEG), F32),
            pltpu.VMEM((3, 2, 8, B), F32),
            pltpu.VMEM((3, 2 * L, 8, B), F32),
            pltpu.VMEM((3, Z * Y // 2, 8, B), F32),
            dma((5,)), dma, dma, dma, dma, dma, dma, dma, dma, dma, dma, dma, dma,
            dma, dma, dma, dma, dma((3,)), dma((3,)), dma((3,)), dma((3,)), regular, regular,
        ],
        compiler_params=pltpu.CompilerParams(collective_id=0, has_side_effects=True, vmem_limit_bytes=62 * 1024 * 1024),
        name="lobpcg_step",
    )(block_rows.reshape(NB), block_cols.reshape(NB), hamiltonian_blocks.reshape(NB, B, B), current_states, previous_steps)


def solution(mesh):
    return jax.shard_map(
        body,
        mesh=mesh,
        in_specs=(
            P("row", "col", None, None, None),
            P("row", "col", None),
            P("row", "col", None),
            P(None, "row"),
            P(None, "row"),
        ),
        out_specs=(P(None, ("row", "col")), P()),
        check_vma=False,
    )
```

```python
import functools

import jax
import jax.numpy as jnp
from jax import lax
from jax.experimental import pallas as pl
from jax.experimental.pallas import tpu as pltpu
from jax.sharding import PartitionSpec as P

MESH = pl.DeviceIdType.MESH
F32 = jnp.float32
exactness = lax.Precision.HIGHEST

Z, YL, YH, L = 8, 4, 2, 8
Y = YL * YH
N_ROW, N_COL = Z * YL, L * YH
K, B, SEGB, NB = 8, 128, 32, 4
SEG = SEGB * B
SHARE, OWNED = SEG // N_COL, SEG // L
ROWS = N_ROW * SEG
rem, div = lax.rem, lax.div


def nn(a, b):
    return jnp.dot(a, b, precision=exactness, preferred_element_type=F32)


def nt(a, b):
    return lax.dot_general(a, b, (((1,), (1,)), ((), ())), precision=exactness, preferred_element_type=F32)


def lane_ids(shape):
    return lax.broadcasted_iota(jnp.int32, shape, 1)


def row_ids(shape):
    return lax.broadcasted_iota(jnp.int32, shape, 0)


def padded(a):
    return jnp.concatenate([a, jnp.zeros((B - a.shape[0], a.shape[1]), F32)], 0)


def summed(terms):
    while len(terms) > 1:
        terms = [sum(terms[i + 1 : i + 2], terms[i]) for i in range(0, len(terms), 2)]
    return terms[0]


def packed(a):
    return a[0:8] + pltpu.roll(a[8:16], 32, 1) + pltpu.roll(a[16:24], 64, 1)


def unpacked(t):
    a = jnp.concatenate([t, pltpu.roll(t, 96, 1), pltpu.roll(t, 64, 1)], 0)
    return jnp.where(lane_ids(a.shape) < 24, a, 0.0)


def inverse_factor(gram):
    rows, lanes = row_ids(gram.shape), lane_ids(gram.shape)
    left = gram
    right = (rows == lanes).astype(F32)
    for j in range(24):
        pivot = left[j : j + 1, j : j + 1]
        factor = jnp.where(rows[:, :1] > j, left[:, j : j + 1] / pivot, 0.0)
        top, unit = left[j : j + 1], right[j : j + 1]
        left = left - factor * top
        right = right - factor * unit
    diagonal = jnp.sum(jnp.where(rows == lanes, left, 0.0), 1, keepdims=True)
    return right / jnp.sqrt(diagonal)


def kernel(rows_ref, cols_ref, h_ref, x_ref, p_ref, q_ref, ray_ref,
           rows, cols, h, x, x_far, p, p_far, p_pick, asked, wanted, m, m_near, d, got, part, other, piece, y, y_far, mine,
           line, buf_a, buf_b, buf_c, load_sem, x_sem, xs_sem, m_sem, ms_sem, want_sem, wants_sem, p_sem, ps_sem, d_sem, ds_sem, o_sem, os_sem,
           y_sem, ys_sem, yfar_sem, yfs_sem, a_sem, b_sem, c_sem, as_sem, bs_sem, cs_sem, step2, step3):
    r, c = lax.axis_index("row"), lax.axis_index("col")
    z, y_lo, l, y_hi = rem(r, Z), div(r, Z), rem(c, L), div(c, L)
    yy = y_hi * YL + y_lo

    def at(y_at, z_at, l_at):
        return (rem(y_at, YL) * Z + z_at, div(y_at, YL) * L + l_at)

    def send(src, dst, ss, rs, dev):
        pltpu.make_async_remote_copy(src_ref=src, dst_ref=dst, send_sem=ss, recv_sem=rs,
                                     device_id=dev, device_id_type=MESH).start()

    def done(ref, sem):
        pltpu.make_async_copy(ref, ref, sem).wait()

    reads = c != 0
    q = rem(r + c, N_ROW)
    turned = jnp.logical_and(div(q, Z) == 0, z + l >= Z).astype(jnp.int32)
    source = (q, rem(y_hi + turned, YH) * L + l)

    def user(l_at):
        over = jnp.logical_and(y_lo == 0, z < l_at).astype(jnp.int32)
        to = rem(y_hi + over, YH) * L + l_at
        return rem(r + N_ROW - to, N_ROW), to

    barrier = pltpu.get_barrier_semaphore()

    @pl.when(reads)
    def _():
        pl.semaphore_signal(barrier, inc=1, device_id=source, device_id_type=MESH)
        pl.semaphore_signal(barrier, inc=1, device_id=user(l), device_id_type=MESH)

    def greet(n, sem, place):
        for k in range(1, n):
            pl.semaphore_signal(sem, inc=1, device_id=place(k), device_id_type=MESH)

    greet(Z, barrier, lambda k: at(yy, rem(z + k, Z), l))
    greet(Y, barrier, lambda k: at(rem(yy + k, Y), z, l))
    greet(L, barrier, lambda k: at(yy, z, rem(l + k, L)))

    loads = [pltpu.make_async_copy(src, dst, load_sem.at[i]) for i, (src, dst) in enumerate(
        ((rows_ref, rows), (cols_ref, cols), (x_ref, x), (h_ref, h), (p_ref, p)))]
    for load in loads:
        load.start()

    pl.semaphore_wait(barrier, Z - 1 + Y - 1 + L - 1 + 2 * reads.astype(jnp.int32))

    @pl.when(reads)
    def _():
        send(x_ref, x_far, xs_sem, x_sem, user(l))

    @pl.when(jnp.logical_not(reads))
    def _():
        pltpu.make_async_copy(x_ref, x_far, x_sem).start()

    greet(Y, step2, lambda k: at(rem(yy + k, Y), z, l))

    def blocks(ref, places):
        found = [ref[:, :B]] * NB
        for b in range(1, SEGB):
            here = ref[:, b * B : (b + 1) * B]
            found = [jnp.where(places[n] == b, here, found[n]) for n in range(NB)]
        return found

    for load in loads[:4]:
        load.wait()
    row_at = [jnp.full((K, B), rows[n], jnp.int32) for n in range(NB)]
    col_at = [jnp.full((K, B), cols[n], jnp.int32) for n in range(NB)]
    x_row = blocks(x, row_at)
    m_x = jnp.concatenate([nn(x_row[n], h[n]) for n in range(NB)], 1)

    asks = jnp.zeros((8, B), jnp.int32)
    for n in range(NB):
        asks = jnp.where(row_ids((8, B)) == n, col_at[n], asks)

    @pl.when(reads)
    def _():
        m[...] = m_x
        asked[...] = asks
        send(m, m_near, ms_sem, m_sem, source)
        send(asked, wanted, wants_sem, want_sem, source)

    @pl.when(jnp.logical_not(reads))
    def _():
        m_near[...] = m_x
        wanted[...] = asks

    pl.semaphore_wait(step2, Y - 1)
    greet(Z, step3, lambda k: at(yy, rem(z + k, Z), l))
    loads[4].wait()
    p_row = blocks(p, row_at)
    m_p = jnp.concatenate([nn(p_row[n], h[n]) for n in range(NB)], 1)

    done(x_far, x_sem)
    x_col = blocks(x_far, col_at)
    direct = [nt(x_col[n], h[n]) for n in range(NB)]
    xc = jnp.concatenate(x_col, 1)
    near_last = (4, 5, 3, 6, 2, 7, 1, 0)

    y_par, y_pair = rem(yy, 2), div(yy, 2)
    slot_a = y_par * L + l
    slot_b = y_pair * Z + z

    def first(tile):
        mine[0] = tile
        for k in range(2 * L - 1):
            y_to = 2 * y_pair + rem(y_par + 1 + k // L, 2)
            send(mine.at[0], buf_a.at[slot_a], as_sem, a_sem, at(y_to, z, rem(l + near_last[k % L], L)))
        pltpu.make_async_copy(mine.at[0], buf_a.at[slot_a], a_sem).start()

    def second():
        done(buf_a, a_sem)
        mine[1] = summed([buf_a[s] for s in range(2 * L)])
        for y_k in (2, 1, 3, 0):
            for z_k in near_last:
                if y_k or z_k:
                    y_to = 2 * rem(y_pair + y_k, Y // 2) + y_par
                    send(mine.at[1], buf_b.at[slot_b], bs_sem, b_sem, at(y_to, rem(z + z_k, Z), l))
        pltpu.make_async_copy(mine.at[1], buf_b.at[slot_b], b_sem).start()

    def third():
        done(buf_b, b_sem)
        return summed([buf_b[s] for s in range(Z * Y // 2)])

    def start(i, step, tile):
        line[i, step] = tile
        slot = (l, yy, z)[step]
        for k in near_last[:-1]:
            to = (at(yy, z, rem(l + k, L)), at(rem(yy + k, Y), z, l), at(yy, rem(z + k, Z), l))[step]
            send(line.at[i, step], buf_c.at[i, step, slot], cs_sem.at[i, step], c_sem.at[i, step], to)
        pltpu.make_async_copy(line.at[i, step], buf_c.at[i, step, slot], c_sem.at[i, step]).start()

    def finish(i, step):
        done(buf_c.at[i, step], c_sem.at[i, step])
        return summed([buf_c[i, step, s] for s in range(8)])

    pl.semaphore_wait(step3, Z - 1)
    start(0, 0, nt(m_x, padded(xc)) + nt(xc, padded(m_x)))


    @pl.when(reads)
    def _():
        done(m_near, m_sem)
        done(wanted, want_sem)

    want = wanted[...]
    want_at = [jnp.broadcast_to(want[n : n + 1], (K, B)) for n in range(NB)]
    terms = [direct[n] for n in range(NB)] + [m_near[:, n * B : (n + 1) * B] for n in range(NB)]
    for b in range(SEGB):
        total = jnp.zeros((K, B), F32)
        for place, term in zip(row_at + want_at, terms):
            total = total + jnp.where(place == b, term, 0.0)
        d[:, b * B : (b + 1) * B] = total

    def share(l_at):
        return pl.ds(pl.multiple_of(l_at * OWNED, OWNED), OWNED)

    for k in near_last[:-1]:
        j = rem(l + k, L)
        send(d.at[:, share(j)], got.at[l], ds_sem, d_sem, at(yy, z, j))
    pltpu.make_async_copy(d.at[:, share(l)], got.at[l], d_sem).start()

    @pl.when(reads)
    def _():
        p_pick[...] = jnp.concatenate(blocks(p, want_at), 1)
        send(p_pick, p_far, ps_sem, p_sem, user(l))

    @pl.when(jnp.logical_not(reads))
    def _():
        p_far[...] = jnp.concatenate(blocks(p, col_at), 1)

    start(0, 1, finish(0, 0))
    done(got, d_sem)
    part[...] = summed([got[s] for s in range(L)])
    send(part, other, os_sem, o_sem, (r, rem(y_hi + 1, YH) * L + l))
    start(0, 2, finish(0, 1))
    done(other, o_sem)
    piece[...] = part[...] + other[...]

    mine_of = share(l)
    for l_to in near_last:
        if l_to:
            send(piece, y_far.at[:, mine_of], yfs_sem, yfar_sem, user(l_to))
        else:
            @pl.when(c == 0)
            def _():
                pltpu.make_async_copy(piece, y_far.at[:, mine_of], yfar_sem).start()

            @pl.when(reads)
            def _():
                send(piece, y_far.at[:, mine_of], yfs_sem, yfar_sem, user(0))

    for k in near_last[:-1]:
        send(piece, y.at[:, mine_of], ys_sem, y_sem, at(yy, z, rem(l + k, L)))
    pltpu.make_async_copy(piece, y.at[:, mine_of], y_sem).start()

    theta = finish(0, 2)[:, :K] / ROWS
    half = pl.ds(pl.multiple_of(l * OWNED + y_hi * SHARE, SHARE), SHARE)
    half_of = pl.ds(pl.multiple_of(y_hi * SHARE, SHARE), SHARE)
    own = pl.ds(pl.multiple_of(c * SHARE, SHARE), SHARE)
    residual = piece[:, half_of] - nn(theta, x[:, half])
    basis = jnp.concatenate([residual, x[:, half], p[:, half]], 0)
    start(1, 0, packed(nt(basis, padded(basis))))
    taken = nn(theta, jnp.concatenate([m_x, xc, x[:, own]], 1))

    @pl.when(reads)
    def _():
        done(p_far, p_sem)

    p_col = p_far[...]
    done(y, y_sem)
    y_row = blocks(y, row_at)
    m_r = jnp.concatenate([nn(y_row[n], h[n]) for n in range(NB)], 1) - taken[:, : NB * B]

    done(y_far, yfar_sem)
    r_col = jnp.concatenate(blocks(y_far, col_at), 1) - taken[:, NB * B : 2 * NB * B]
    left, right = jnp.concatenate([m_r, m_x, m_p], 0), jnp.concatenate([r_col, xc, p_col], 0)
    first(packed(nt(left, padded(right)) + nt(right, padded(left))))
    start(1, 1, finish(1, 0))
    second()
    start(1, 2, finish(1, 1))
    inverse = inverse_factor(unpacked(finish(1, 2)) / ROWS)[:, :24]
    q_ref[...] = nn(inverse, jnp.concatenate([y[:, own] - taken[:, 2 * NB * B :], x[:, own], p[:, own]], 0))

    @pl.when(reads)
    def _():
        done(x_ref, xs_sem)

    @pl.when(reads)
    def _():
        done(m, ms_sem)
        done(asked, wants_sem)

    @pl.when(reads)
    def _():
        done(p_pick, ps_sem)

    done(got.at[pl.ds(0, L - 1)], ds_sem)
    done(part, os_sem)
    done(got.at[pl.ds(0, L - 1)], yfs_sem)
    done(got.at[pl.ds(0, L - 1)], ys_sem)

    @pl.when(reads)
    def _():
        done(piece, yfs_sem)

    for step in range(3):
        done(buf_c.at[0, step, pl.ds(0, 7)], cs_sem.at[0, step])
    for step in range(3):
        done(buf_c.at[1, step, pl.ds(0, 7)], cs_sem.at[1, step])
    done(buf_a.at[pl.ds(0, 2 * L - 1)], as_sem)

    ray_ref[...] = nt(nn(inverse, unpacked(third())[:, :24] / ROWS), inverse)
    done(buf_b.at[pl.ds(0, Z * Y // 2 - 1)], bs_sem)


def body(hamiltonian_blocks, block_rows, block_cols, current_states, previous_steps):
    vmem, anywhere = (pl.BlockSpec(memory_space=s) for s in (pltpu.VMEM, pl.ANY))
    dma, regular = pltpu.SemaphoreType.DMA, pltpu.SemaphoreType.REGULAR
    return pl.pallas_call(
        kernel,
        out_shape=(jax.ShapeDtypeStruct((3 * K, SHARE), F32), jax.ShapeDtypeStruct((3 * K, 3 * K), F32)),
        in_specs=[anywhere, anywhere, anywhere, anywhere, anywhere],
        out_specs=(vmem, vmem),
        scratch_shapes=[
            pltpu.SMEM((NB,), jnp.int32),
            pltpu.SMEM((NB,), jnp.int32),
            pltpu.VMEM((NB, B, B), F32),
            pltpu.VMEM((K, SEG), F32),
            pltpu.VMEM((K, SEG), F32),
            pltpu.VMEM((K, SEG), F32),
            pltpu.VMEM((K, NB * B), F32),
            pltpu.VMEM((K, NB * B), F32),
            pltpu.VMEM((8, B), jnp.int32),
            pltpu.VMEM((8, B), jnp.int32),
            pltpu.VMEM((K, NB * B), F32),
            pltpu.VMEM((K, NB * B), F32),
            pltpu.VMEM((K, SEG), F32),
            pltpu.VMEM((L, K, OWNED), F32),
            pltpu.VMEM((K, OWNED), F32),
            pltpu.VMEM((K, OWNED), F32),
            pltpu.VMEM((K, OWNED), F32),
            pltpu.VMEM((K, SEG), F32),
            pltpu.VMEM((K, SEG), F32),
            pltpu.VMEM((2, 8, B), F32),
            pltpu.VMEM((2, 3, 8, B), F32),
            pltpu.VMEM((2 * L, 8, B), F32),
            pltpu.VMEM((Z * Y // 2, 8, B), F32),
            pltpu.VMEM((2, 3, 8, 8, B), F32),
            dma((5,)), dma, dma, dma, dma, dma, dma, dma, dma, dma, dma, dma, dma,
            dma, dma, dma, dma, dma, dma, dma((2, 3)), dma, dma, dma((2, 3)), regular, regular,
        ],
        compiler_params=pltpu.CompilerParams(collective_id=0, has_side_effects=True, vmem_limit_bytes=62 * 1024 * 1024),
        name="lobpcg_step",
    )(block_rows.reshape(NB), block_cols.reshape(NB), hamiltonian_blocks.reshape(NB, B, B), current_states, previous_steps)


def solution(mesh):
    return jax.shard_map(
        body,
        mesh=mesh,
        in_specs=(
            P("row", "col", None, None, None),
            P("row", "col", None),
            P("row", "col", None),
            P(None, "row"),
            P(None, "row"),
        ),
        out_specs=(P(None, ("row", "col")), P()),
        check_vma=False,
    )
```

```python
import functools

import jax
import jax.numpy as jnp
from jax import lax
from jax.experimental import pallas as pl
from jax.experimental.pallas import tpu as pltpu
from jax.sharding import PartitionSpec as P

MESH = pl.DeviceIdType.MESH
F32 = jnp.float32
exactness = lax.Precision.HIGHEST

Z, YL, YH, L = 8, 4, 2, 8
Y = YL * YH
N_ROW, N_COL = Z * YL, L * YH
K, B, SEGB, NB = 8, 128, 32, 4
SEG = SEGB * B
SHARE, OWNED = SEG // N_COL, SEG // L
ROWS = N_ROW * SEG
rem, div = lax.rem, lax.div


def nn(a, b):
    return jnp.dot(a, b, precision=exactness, preferred_element_type=F32)


def nt(a, b):
    return lax.dot_general(a, b, (((1,), (1,)), ((), ())), precision=exactness, preferred_element_type=F32)


def lane_ids(shape):
    return lax.broadcasted_iota(jnp.int32, shape, 1)


def row_ids(shape):
    return lax.broadcasted_iota(jnp.int32, shape, 0)


def padded(a):
    return jnp.concatenate([a, jnp.zeros((B - a.shape[0], a.shape[1]), F32)], 0)


def summed(terms):
    while len(terms) > 1:
        terms = [sum(terms[i + 1 : i + 2], terms[i]) for i in range(0, len(terms), 2)]
    return terms[0]


def packed(a):
    return a[0:8] + pltpu.roll(a[8:16], 32, 1) + pltpu.roll(a[16:24], 64, 1)


def unpacked(t):
    a = jnp.concatenate([t, pltpu.roll(t, 96, 1), pltpu.roll(t, 64, 1)], 0)
    return jnp.where(lane_ids(a.shape) < 24, a, 0.0)


def inverse_factor(gram):
    rows, lanes = row_ids(gram.shape), lane_ids(gram.shape)
    left = gram
    right = (rows == lanes).astype(F32)
    for j in range(24):
        pivot = left[j : j + 1, j : j + 1]
        factor = jnp.where(rows[:, :1] > j, left[:, j : j + 1] / pivot, 0.0)
        top, unit = left[j : j + 1], right[j : j + 1]
        left = left - factor * top
        right = right - factor * unit
    diagonal = jnp.sum(jnp.where(rows == lanes, left, 0.0), 1, keepdims=True)
    return right / jnp.sqrt(diagonal)


def kernel(rows_ref, cols_ref, h_ref, x_ref, p_ref, q_ref, ray_ref,
           rows, cols, h, x, p, pick, far, asked, wanted, m, m_near, d, got, part, other, piece, y, y_far, mine,
           line, buf_a, buf_b, buf_c, load_sem, m_sem, ms_sem, want_sem, wants_sem, f_sem, fs_sem, d_sem, ds_sem, o_sem, os_sem,
           y_sem, ys_sem, yfar_sem, yfs_sem, a_sem, b_sem, c_sem, as_sem, bs_sem, cs_sem, step2, step3):
    r, c = lax.axis_index("row"), lax.axis_index("col")
    z, y_lo, l, y_hi = rem(r, Z), div(r, Z), rem(c, L), div(c, L)
    yy = y_hi * YL + y_lo

    def at(y_at, z_at, l_at):
        return (rem(y_at, YL) * Z + z_at, div(y_at, YL) * L + l_at)

    def send(src, dst, ss, rs, dev):
        pltpu.make_async_remote_copy(src_ref=src, dst_ref=dst, send_sem=ss, recv_sem=rs,
                                     device_id=dev, device_id_type=MESH).start()

    def done(ref, sem):
        pltpu.make_async_copy(ref, ref, sem).wait()

    reads = c != 0
    q = rem(r + c, N_ROW)
    turned = jnp.logical_and(div(q, Z) == 0, z + l >= Z).astype(jnp.int32)
    source = (q, rem(y_hi + turned, YH) * L + l)

    def user(l_at):
        over = jnp.logical_and(y_lo == 0, z < l_at).astype(jnp.int32)
        to = rem(y_hi + over, YH) * L + l_at
        return rem(r + N_ROW - to, N_ROW), to

    barrier = pltpu.get_barrier_semaphore()

    @pl.when(reads)
    def _():
        pl.semaphore_signal(barrier, inc=1, device_id=source, device_id_type=MESH)
        pl.semaphore_signal(barrier, inc=1, device_id=user(l), device_id_type=MESH)

    def greet(n, sem, place):
        for k in range(1, n):
            pl.semaphore_signal(sem, inc=1, device_id=place(k), device_id_type=MESH)

    greet(Z, barrier, lambda k: at(yy, rem(z + k, Z), l))
    greet(Y, barrier, lambda k: at(rem(yy + k, Y), z, l))
    greet(L, barrier, lambda k: at(yy, z, rem(l + k, L)))

    loads = [pltpu.make_async_copy(src, dst, load_sem.at[i]) for i, (src, dst) in enumerate(
        ((rows_ref, rows), (cols_ref, cols), (x_ref, x), (h_ref, h), (p_ref, p)))]
    for load in loads:
        load.start()

    for load in loads[:2]:
        load.wait()
    row_at = [jnp.full((K, B), rows[n], jnp.int32) for n in range(NB)]
    col_at = [jnp.full((K, B), cols[n], jnp.int32) for n in range(NB)]
    asks = jnp.zeros((8, B), jnp.int32)
    for n in range(NB):
        asks = jnp.where(row_ids((8, B)) == n, col_at[n], asks)
    asked[...] = asks

    @pl.when(jnp.logical_not(reads))
    def _():
        wanted[...] = asks

    pl.semaphore_wait(barrier, Z - 1 + Y - 1 + L - 1 + 2 * reads.astype(jnp.int32))

    @pl.when(reads)
    def _():
        send(asked, wanted, wants_sem, want_sem, source)

    greet(Y, step2, lambda k: at(rem(yy + k, Y), z, l))

    def blocks(ref, places):
        found = [ref[:, :B]] * NB
        for b in range(1, SEGB):
            here = ref[:, b * B : (b + 1) * B]
            found = [jnp.where(places[n] == b, here, found[n]) for n in range(NB)]
        return found

    for load in loads[2:]:
        load.wait()
    x_row, p_row = blocks(x, row_at), blocks(p, row_at)
    both = [nn(jnp.concatenate([x_row[n], p_row[n]], 0), h[n]) for n in range(NB)]
    m_x, m_p = (jnp.concatenate([both[n][k : k + K] for n in range(NB)], 1) for k in (0, K))

    @pl.when(reads)
    def _():
        m[...] = m_x
        send(m, m_near, ms_sem, m_sem, source)

    @pl.when(jnp.logical_not(reads))
    def _():
        m_near[...] = m_x

    pl.semaphore_wait(step2, Y - 1)
    greet(Z, step3, lambda k: at(yy, rem(z + k, Z), l))

    @pl.when(reads)
    def _():
        done(wanted, want_sem)

    want = wanted[...]
    want_at = [jnp.broadcast_to(want[n : n + 1], (K, B)) for n in range(NB)]
    picked = jnp.concatenate([jnp.concatenate(blocks(x, want_at), 1), jnp.concatenate(blocks(p, want_at), 1)], 0)

    @pl.when(reads)
    def _():
        pick[...] = picked
        send(pick, far, fs_sem, f_sem, user(l))

    @pl.when(jnp.logical_not(reads))
    def _():
        far[...] = picked

    near_last = (4, 5, 3, 6, 2, 7, 1, 0)

    y_par, y_pair = rem(yy, 2), div(yy, 2)
    slot_a = y_par * L + l
    slot_b = y_pair * Z + z

    def first(tile):
        mine[0] = tile
        for k in range(2 * L - 1):
            y_to = 2 * y_pair + rem(y_par + 1 + k // L, 2)
            send(mine.at[0], buf_a.at[slot_a], as_sem, a_sem, at(y_to, z, rem(l + near_last[k % L], L)))
        pltpu.make_async_copy(mine.at[0], buf_a.at[slot_a], a_sem).start()

    def second():
        done(buf_a, a_sem)
        mine[1] = summed([buf_a[s] for s in range(2 * L)])
        for y_k in (2, 1, 3, 0):
            for z_k in near_last:
                if y_k or z_k:
                    y_to = 2 * rem(y_pair + y_k, Y // 2) + y_par
                    send(mine.at[1], buf_b.at[slot_b], bs_sem, b_sem, at(y_to, rem(z + z_k, Z), l))
        pltpu.make_async_copy(mine.at[1], buf_b.at[slot_b], b_sem).start()

    def third():
        done(buf_b, b_sem)
        return summed([buf_b[s] for s in range(Z * Y // 2)])

    def start(i, step, tile):
        line[i, step] = tile
        slot = (l, yy, z)[step]
        for k in near_last[:-1]:
            to = (at(yy, z, rem(l + k, L)), at(rem(yy + k, Y), z, l), at(yy, rem(z + k, Z), l))[step]
            send(line.at[i, step], buf_c.at[i, step, slot], cs_sem.at[i, step], c_sem.at[i, step], to)
        pltpu.make_async_copy(line.at[i, step], buf_c.at[i, step, slot], c_sem.at[i, step]).start()

    def finish(i, step):
        done(buf_c.at[i, step], c_sem.at[i, step])
        return summed([buf_c[i, step, s] for s in range(8)])

    @pl.when(reads)
    def _():
        done(far, f_sem)

    xc, p_col = far[:K], far[K:]
    direct = [nt(xc[:, n * B : (n + 1) * B], h[n]) for n in range(NB)]

    @pl.when(reads)
    def _():
        done(m_near, m_sem)

    terms = [direct[n] for n in range(NB)] + [m_near[:, n * B : (n + 1) * B] for n in range(NB)]
    for b in range(SEGB):
        total = jnp.zeros((K, B), F32)
        for place, term in zip(row_at + want_at, terms):
            total = total + jnp.where(place == b, term, 0.0)
        d[:, b * B : (b + 1) * B] = total
    pl.semaphore_wait(step3, Z - 1)

    def share(l_at):
        return pl.ds(pl.multiple_of(l_at * OWNED, OWNED), OWNED)

    for k in near_last[:-1]:
        j = rem(l + k, L)
        send(d.at[:, share(j)], got.at[l], ds_sem, d_sem, at(yy, z, j))
    pltpu.make_async_copy(d.at[:, share(l)], got.at[l], d_sem).start()

    start(0, 0, nt(m_x, padded(xc)) + nt(xc, padded(m_x)))
    start(0, 1, finish(0, 0))
    done(got, d_sem)
    part[...] = summed([got[s] for s in range(L)])
    send(part, other, os_sem, o_sem, (r, rem(y_hi + 1, YH) * L + l))
    start(0, 2, finish(0, 1))
    done(other, o_sem)
    piece[...] = part[...] + other[...]

    mine_of = share(l)
    for l_to in near_last:
        if l_to:
            send(piece, y_far.at[:, mine_of], yfs_sem, yfar_sem, user(l_to))
        else:
            @pl.when(c == 0)
            def _():
                pltpu.make_async_copy(piece, y_far.at[:, mine_of], yfar_sem).start()

            @pl.when(reads)
            def _():
                send(piece, y_far.at[:, mine_of], yfs_sem, yfar_sem, user(0))

    for k in near_last[:-1]:
        send(piece, y.at[:, mine_of], ys_sem, y_sem, at(yy, z, rem(l + k, L)))
    pltpu.make_async_copy(piece, y.at[:, mine_of], y_sem).start()

    theta = finish(0, 2)[:, :K] / ROWS
    half = pl.ds(pl.multiple_of(l * OWNED + y_hi * SHARE, SHARE), SHARE)
    half_of = pl.ds(pl.multiple_of(y_hi * SHARE, SHARE), SHARE)
    own = pl.ds(pl.multiple_of(c * SHARE, SHARE), SHARE)
    residual = piece[:, half_of] - nn(theta, x[:, half])
    basis = jnp.concatenate([residual, x[:, half], p[:, half]], 0)
    start(1, 0, packed(nt(basis, padded(basis))))
    taken = nn(theta, jnp.concatenate([m_x, xc, x[:, own]], 1))

    done(y, y_sem)
    y_row = blocks(y, row_at)
    m_r = jnp.concatenate([nn(y_row[n], h[n]) for n in range(NB)], 1) - taken[:, : NB * B]

    done(y_far, yfar_sem)
    r_col = jnp.concatenate(blocks(y_far, col_at), 1) - taken[:, NB * B : 2 * NB * B]
    left, right = jnp.concatenate([m_r, m_x, m_p], 0), jnp.concatenate([r_col, xc, p_col], 0)
    first(packed(nt(left, padded(right)) + nt(right, padded(left))))
    start(1, 1, finish(1, 0))
    second()
    start(1, 2, finish(1, 1))
    inverse = inverse_factor(unpacked(finish(1, 2)) / ROWS)[:, :24]
    q_ref[...] = nn(inverse, jnp.concatenate([y[:, own] - taken[:, 2 * NB * B :], x[:, own], p[:, own]], 0))

    @pl.when(reads)
    def _():
        done(m, ms_sem)
        done(asked, wants_sem)

    @pl.when(reads)
    def _():
        done(pick, fs_sem)

    done(got.at[pl.ds(0, L - 1)], ds_sem)
    done(part, os_sem)
    done(got.at[pl.ds(0, L - 1)], yfs_sem)
    done(got.at[pl.ds(0, L - 1)], ys_sem)

    @pl.when(reads)
    def _():
        done(piece, yfs_sem)

    for step in range(3):
        done(buf_c.at[0, step, pl.ds(0, 7)], cs_sem.at[0, step])
    for step in range(3):
        done(buf_c.at[1, step, pl.ds(0, 7)], cs_sem.at[1, step])
    done(buf_a.at[pl.ds(0, 2 * L - 1)], as_sem)

    ray_ref[...] = nt(nn(inverse, unpacked(third())[:, :24] / ROWS), inverse)
    done(buf_b.at[pl.ds(0, Z * Y // 2 - 1)], bs_sem)


def body(hamiltonian_blocks, block_rows, block_cols, current_states, previous_steps):
    vmem, anywhere = (pl.BlockSpec(memory_space=s) for s in (pltpu.VMEM, pl.ANY))
    dma, regular = pltpu.SemaphoreType.DMA, pltpu.SemaphoreType.REGULAR
    return pl.pallas_call(
        kernel,
        out_shape=(jax.ShapeDtypeStruct((3 * K, SHARE), F32), jax.ShapeDtypeStruct((3 * K, 3 * K), F32)),
        in_specs=[anywhere, anywhere, anywhere, anywhere, anywhere],
        out_specs=(vmem, vmem),
        scratch_shapes=[
            pltpu.SMEM((NB,), jnp.int32),
            pltpu.SMEM((NB,), jnp.int32),
            pltpu.VMEM((NB, B, B), F32),
            pltpu.VMEM((K, SEG), F32),
            pltpu.VMEM((K, SEG), F32),
            pltpu.VMEM((2 * K, NB * B), F32),
            pltpu.VMEM((2 * K, NB * B), F32),
            pltpu.VMEM((8, B), jnp.int32),
            pltpu.VMEM((8, B), jnp.int32),
            pltpu.VMEM((K, NB * B), F32),
            pltpu.VMEM((K, NB * B), F32),
            pltpu.VMEM((K, SEG), F32),
            pltpu.VMEM((L, K, OWNED), F32),
            pltpu.VMEM((K, OWNED), F32),
            pltpu.VMEM((K, OWNED), F32),
            pltpu.VMEM((K, OWNED), F32),
            pltpu.VMEM((K, SEG), F32),
            pltpu.VMEM((K, SEG), F32),
            pltpu.VMEM((2, 8, B), F32),
            pltpu.VMEM((2, 3, 8, B), F32),
            pltpu.VMEM((2 * L, 8, B), F32),
            pltpu.VMEM((Z * Y // 2, 8, B), F32),
            pltpu.VMEM((2, 3, 8, 8, B), F32),
            dma((5,)), dma, dma, dma, dma, dma, dma, dma, dma, dma, dma,
            dma, dma, dma, dma, dma, dma, dma((2, 3)), dma, dma, dma((2, 3)), regular, regular,
        ],
        compiler_params=pltpu.CompilerParams(collective_id=0, has_side_effects=True, vmem_limit_bytes=62 * 1024 * 1024),
        name="lobpcg_step",
    )(block_rows.reshape(NB), block_cols.reshape(NB), hamiltonian_blocks.reshape(NB, B, B), current_states, previous_steps)


def solution(mesh):
    return jax.shard_map(
        body,
        mesh=mesh,
        in_specs=(
            P("row", "col", None, None, None),
            P("row", "col", None),
            P("row", "col", None),
            P(None, "row"),
            P(None, "row"),
        ),
        out_specs=(P(None, ("row", "col")), P()),
        check_vma=False,
    )
```

```python
import functools

import jax
import jax.numpy as jnp
from jax import lax
from jax.experimental import pallas as pl
from jax.experimental.pallas import tpu as pltpu
from jax.sharding import PartitionSpec as P

MESH = pl.DeviceIdType.MESH
F32 = jnp.float32
exactness = lax.Precision.HIGHEST

Z, YL, YH, L = 8, 4, 2, 8
Y = YL * YH
N_ROW, N_COL = Z * YL, L * YH
K, B, SEGB, NB = 8, 128, 32, 4
SEG = SEGB * B
SHARE, OWNED = SEG // N_COL, SEG // L
ROWS = N_ROW * SEG
rem, div = lax.rem, lax.div


def nn(a, b):
    return jnp.dot(a, b, precision=exactness, preferred_element_type=F32)


def nt(a, b):
    return lax.dot_general(a, b, (((1,), (1,)), ((), ())), precision=exactness, preferred_element_type=F32)


def lane_ids(shape):
    return lax.broadcasted_iota(jnp.int32, shape, 1)


def row_ids(shape):
    return lax.broadcasted_iota(jnp.int32, shape, 0)


def padded(a):
    return jnp.concatenate([a, jnp.zeros((B - a.shape[0], a.shape[1]), F32)], 0)


def summed(terms):
    while len(terms) > 1:
        terms = [sum(terms[i + 1 : i + 2], terms[i]) for i in range(0, len(terms), 2)]
    return terms[0]


def folded(t):
    return t[0:4] + pltpu.roll(t[4:8], 64, 1)


def unfolded(t):
    t = jnp.concatenate([t, pltpu.roll(t, 64, 1)], 0)
    return jnp.where(lane_ids(t.shape) < 64, t, 0.0)


def between(a, low, high):
    lanes = lane_ids(a.shape)
    return jnp.where(jnp.logical_and(lanes >= low, lanes < high), a, 0.0)


def packed(a):
    return folded(between(a[0:8], 0, 24) + pltpu.roll(between(a[8:16], 8, 24), 16, 1) + pltpu.roll(between(a[16:24], 16, 24), 24, 1))


def unpacked(t):
    t = unfolded(t)
    a = jnp.concatenate([between(t, 0, 24), between(pltpu.roll(t, 112, 1), 8, 24), between(pltpu.roll(t, 104, 1), 16, 24)], 0)
    same = lax.shift_right_logical(lane_ids(a.shape), 3) == lax.shift_right_logical(row_ids(a.shape), 3)
    return jnp.where(same, 0.5 * a, a)


def symmetric(a):
    unit = (lane_ids((24, B)) == row_ids((24, B))).astype(F32)
    return a + nt(unit, padded(a))


def inverse_factor(gram):
    rows, lanes = row_ids(gram.shape), lane_ids(gram.shape)
    left = gram
    right = (rows == lanes).astype(F32)
    for j in range(24):
        pivot = left[j : j + 1, j : j + 1]
        factor = jnp.where(rows[:, :1] > j, left[:, j : j + 1] / pivot, 0.0)
        top, unit = left[j : j + 1], right[j : j + 1]
        left = left - factor * top
        right = right - factor * unit
    diagonal = jnp.sum(jnp.where(rows == lanes, left, 0.0), 1, keepdims=True)
    return right / jnp.sqrt(diagonal)


def kernel(rows_ref, cols_ref, h_ref, x_ref, p_ref, q_ref, ray_ref,
           rows, cols, h, x, p, pick, far, asked, wanted, m, m_near, d, got, part, other, piece, y, y_far, mine,
           line, buf_a, buf_b, buf_c, load_sem, m_sem, ms_sem, want_sem, wants_sem, f_sem, fs_sem, d_sem, ds_sem, o_sem, os_sem,
           y_sem, ys_sem, yfar_sem, yfs_sem, a_sem, b_sem, c_sem, as_sem, bs_sem, cs_sem, step2, step3):
    r, c = lax.axis_index("row"), lax.axis_index("col")
    z, y_lo, l, y_hi = rem(r, Z), div(r, Z), rem(c, L), div(c, L)
    yy = y_hi * YL + y_lo

    def at(y_at, z_at, l_at):
        return (rem(y_at, YL) * Z + z_at, div(y_at, YL) * L + l_at)

    def send(src, dst, ss, rs, dev):
        pltpu.make_async_remote_copy(src_ref=src, dst_ref=dst, send_sem=ss, recv_sem=rs,
                                     device_id=dev, device_id_type=MESH).start()

    def done(ref, sem):
        pltpu.make_async_copy(ref, ref, sem).wait()

    reads = c != 0
    q = rem(r + c, N_ROW)
    turned = jnp.logical_and(div(q, Z) == 0, z + l >= Z).astype(jnp.int32)
    source = (q, rem(y_hi + turned, YH) * L + l)

    def user(l_at):
        over = jnp.logical_and(y_lo == 0, z < l_at).astype(jnp.int32)
        to = rem(y_hi + over, YH) * L + l_at
        return rem(r + N_ROW - to, N_ROW), to

    barrier = pltpu.get_barrier_semaphore()

    @pl.when(reads)
    def _():
        pl.semaphore_signal(barrier, inc=1, device_id=source, device_id_type=MESH)
        pl.semaphore_signal(barrier, inc=1, device_id=user(l), device_id_type=MESH)

    def greet(n, sem, place):
        for k in range(1, n):
            pl.semaphore_signal(sem, inc=1, device_id=place(k), device_id_type=MESH)

    greet(Z, barrier, lambda k: at(yy, rem(z + k, Z), l))
    greet(Y, barrier, lambda k: at(rem(yy + k, Y), z, l))
    greet(L, barrier, lambda k: at(yy, z, rem(l + k, L)))

    loads = [pltpu.make_async_copy(src, dst, load_sem.at[i]) for i, (src, dst) in enumerate(
        ((rows_ref, rows), (cols_ref, cols), (x_ref, x), (h_ref, h), (p_ref, p)))]
    for load in loads:
        load.start()

    for load in loads[:2]:
        load.wait()
    row_at = [jnp.full((K, B), rows[n], jnp.int32) for n in range(NB)]
    col_at = [jnp.full((K, B), cols[n], jnp.int32) for n in range(NB)]
    asks = jnp.zeros((8, B), jnp.int32)
    for n in range(NB):
        asks = jnp.where(row_ids((8, B)) == n, col_at[n], asks)
    asked[...] = asks

    @pl.when(jnp.logical_not(reads))
    def _():
        wanted[...] = asks

    pl.semaphore_wait(barrier, Z - 1 + Y - 1 + L - 1 + 2 * reads.astype(jnp.int32))

    @pl.when(reads)
    def _():
        send(asked, wanted, wants_sem, want_sem, source)

    greet(Y, step2, lambda k: at(rem(yy + k, Y), z, l))

    def blocks(ref, places):
        found = [ref[:, :B]] * NB
        for b in range(1, SEGB):
            here = ref[:, b * B : (b + 1) * B]
            found = [jnp.where(places[n] == b, here, found[n]) for n in range(NB)]
        return found

    for load in loads[2:]:
        load.wait()
    x_row, p_row = blocks(x, row_at), blocks(p, row_at)
    both = [nn(jnp.concatenate([x_row[n], p_row[n]], 0), h[n]) for n in range(NB)]
    m_x, m_p = (jnp.concatenate([both[n][k : k + K] for n in range(NB)], 1) for k in (0, K))

    @pl.when(reads)
    def _():
        m[...] = m_x
        send(m, m_near, ms_sem, m_sem, source)

    @pl.when(jnp.logical_not(reads))
    def _():
        m_near[...] = m_x

    pl.semaphore_wait(step2, Y - 1)
    greet(Z, step3, lambda k: at(yy, rem(z + k, Z), l))

    @pl.when(reads)
    def _():
        done(wanted, want_sem)

    want = wanted[...]
    want_at = [jnp.broadcast_to(want[n : n + 1], (K, B)) for n in range(NB)]
    picked = jnp.concatenate([jnp.concatenate(blocks(x, want_at), 1), jnp.concatenate(blocks(p, want_at), 1)], 0)

    @pl.when(reads)
    def _():
        pick[...] = picked
        send(pick, far, fs_sem, f_sem, user(l))

    @pl.when(jnp.logical_not(reads))
    def _():
        far[...] = picked

    near_last = (4, 5, 3, 6, 2, 7, 1, 0)

    y_par, y_pair = rem(yy, 2), div(yy, 2)
    slot_a = y_par * L + l
    slot_b = y_pair * Z + z

    def first(tile):
        mine[0] = tile
        for k in range(2 * L - 1):
            y_to = 2 * y_pair + rem(y_par + 1 + k // L, 2)
            send(mine.at[0], buf_a.at[slot_a], as_sem, a_sem, at(y_to, z, rem(l + near_last[k % L], L)))
        pltpu.make_async_copy(mine.at[0], buf_a.at[slot_a], a_sem).start()

    def second():
        done(buf_a, a_sem)
        mine[1] = summed([buf_a[s] for s in range(2 * L)])
        for y_k in (2, 1, 3, 0):
            for z_k in near_last:
                if y_k or z_k:
                    y_to = 2 * rem(y_pair + y_k, Y // 2) + y_par
                    send(mine.at[1], buf_b.at[slot_b], bs_sem, b_sem, at(y_to, rem(z + z_k, Z), l))
        pltpu.make_async_copy(mine.at[1], buf_b.at[slot_b], b_sem).start()

    def third():
        done(buf_b, b_sem)
        return summed([buf_b[s] for s in range(Z * Y // 2)])

    def start(i, step, tile):
        line[i, step] = tile
        slot = (l, yy, z)[step]
        for k in near_last[:-1]:
            to = (at(yy, z, rem(l + k, L)), at(rem(yy + k, Y), z, l), at(yy, rem(z + k, Z), l))[step]
            send(line.at[i, step], buf_c.at[i, step, slot], cs_sem.at[i, step], c_sem.at[i, step], to)
        pltpu.make_async_copy(line.at[i, step], buf_c.at[i, step, slot], c_sem.at[i, step]).start()

    def finish(i, step):
        done(buf_c.at[i, step], c_sem.at[i, step])
        return summed([buf_c[i, step, s] for s in range(8)])

    @pl.when(reads)
    def _():
        done(far, f_sem)

    xc, p_col = far[:K], far[K:]
    direct = [nt(xc[:, n * B : (n + 1) * B], h[n]) for n in range(NB)]

    @pl.when(reads)
    def _():
        done(m_near, m_sem)

    terms = [direct[n] for n in range(NB)] + [m_near[:, n * B : (n + 1) * B] for n in range(NB)]
    for b in range(SEGB):
        total = jnp.zeros((K, B), F32)
        for place, term in zip(row_at + want_at, terms):
            total = total + jnp.where(place == b, term, 0.0)
        d[:, b * B : (b + 1) * B] = total
    pl.semaphore_wait(step3, Z - 1)

    def share(l_at):
        return pl.ds(pl.multiple_of(l_at * OWNED, OWNED), OWNED)

    for k in near_last[:-1]:
        j = rem(l + k, L)
        send(d.at[:, share(j)], got.at[l], ds_sem, d_sem, at(yy, z, j))
    pltpu.make_async_copy(d.at[:, share(l)], got.at[l], d_sem).start()

    start(0, 0, folded(nt(m_x, padded(xc)) + nt(xc, padded(m_x))))
    start(0, 1, finish(0, 0))
    done(got, d_sem)
    part[...] = summed([got[s] for s in range(L)])
    send(part, other, os_sem, o_sem, (r, rem(y_hi + 1, YH) * L + l))
    start(0, 2, finish(0, 1))
    done(other, o_sem)
    piece[...] = part[...] + other[...]

    mine_of = share(l)
    for l_to in near_last:
        if l_to:
            send(piece, y_far.at[:, mine_of], yfs_sem, yfar_sem, user(l_to))
        else:
            @pl.when(c == 0)
            def _():
                pltpu.make_async_copy(piece, y_far.at[:, mine_of], yfar_sem).start()

            @pl.when(reads)
            def _():
                send(piece, y_far.at[:, mine_of], yfs_sem, yfar_sem, user(0))

    for k in near_last[:-1]:
        send(piece, y.at[:, mine_of], ys_sem, y_sem, at(yy, z, rem(l + k, L)))
    pltpu.make_async_copy(piece, y.at[:, mine_of], y_sem).start()

    theta = unfolded(finish(0, 2))[:, :K] / ROWS
    half = pl.ds(pl.multiple_of(l * OWNED + y_hi * SHARE, SHARE), SHARE)
    half_of = pl.ds(pl.multiple_of(y_hi * SHARE, SHARE), SHARE)
    own = pl.ds(pl.multiple_of(c * SHARE, SHARE), SHARE)
    residual = piece[:, half_of] - nn(theta, x[:, half])
    basis = jnp.concatenate([residual, x[:, half], p[:, half]], 0)
    start(1, 0, packed(nt(basis, padded(basis))))
    taken = nn(theta, jnp.concatenate([m_x, xc, x[:, own]], 1))

    done(y, y_sem)
    y_row = blocks(y, row_at)
    m_r = jnp.concatenate([nn(y_row[n], h[n]) for n in range(NB)], 1) - taken[:, : NB * B]

    done(y_far, yfar_sem)
    r_col = jnp.concatenate(blocks(y_far, col_at), 1) - taken[:, NB * B : 2 * NB * B]
    left, right = jnp.concatenate([m_r, m_x, m_p], 0), jnp.concatenate([r_col, xc, p_col], 0)
    first(packed(nt(left, padded(right)) + nt(right, padded(left))))
    start(1, 1, finish(1, 0))
    second()
    start(1, 2, finish(1, 1))
    inverse = inverse_factor(symmetric(unpacked(finish(1, 2))) / ROWS)[:, :24]
    q_ref[...] = nn(inverse, jnp.concatenate([y[:, own] - taken[:, 2 * NB * B :], x[:, own], p[:, own]], 0))

    @pl.when(reads)
    def _():
        done(m, ms_sem)
        done(asked, wants_sem)

    @pl.when(reads)
    def _():
        done(pick, fs_sem)

    done(got.at[pl.ds(0, L - 1)], ds_sem)
    done(part, os_sem)
    done(got.at[pl.ds(0, L - 1)], yfs_sem)
    done(got.at[pl.ds(0, L - 1)], ys_sem)

    @pl.when(reads)
    def _():
        done(piece, yfs_sem)

    for step in range(3):
        done(buf_c.at[0, step, pl.ds(0, 7)], cs_sem.at[0, step])
    for step in range(3):
        done(buf_c.at[1, step, pl.ds(0, 7)], cs_sem.at[1, step])
    done(buf_a.at[pl.ds(0, 2 * L - 1)], as_sem)

    half_way = nn(inverse, unpacked(third())[:, :24] / ROWS)
    ray_ref[...] = nt(half_way, inverse) + nt(inverse, half_way)
    done(buf_b.at[pl.ds(0, Z * Y // 2 - 1)], bs_sem)


def body(hamiltonian_blocks, block_rows, block_cols, current_states, previous_steps):
    vmem, anywhere = (pl.BlockSpec(memory_space=s) for s in (pltpu.VMEM, pl.ANY))
    dma, regular = pltpu.SemaphoreType.DMA, pltpu.SemaphoreType.REGULAR
    return pl.pallas_call(
        kernel,
        out_shape=(jax.ShapeDtypeStruct((3 * K, SHARE), F32), jax.ShapeDtypeStruct((3 * K, 3 * K), F32)),
        in_specs=[anywhere, anywhere, anywhere, anywhere, anywhere],
        out_specs=(vmem, vmem),
        scratch_shapes=[
            pltpu.SMEM((NB,), jnp.int32),
            pltpu.SMEM((NB,), jnp.int32),
            pltpu.VMEM((NB, B, B), F32),
            pltpu.VMEM((K, SEG), F32),
            pltpu.VMEM((K, SEG), F32),
            pltpu.VMEM((2 * K, NB * B), F32),
            pltpu.VMEM((2 * K, NB * B), F32),
            pltpu.VMEM((8, B), jnp.int32),
            pltpu.VMEM((8, B), jnp.int32),
            pltpu.VMEM((K, NB * B), F32),
            pltpu.VMEM((K, NB * B), F32),
            pltpu.VMEM((K, SEG), F32),
            pltpu.VMEM((L, K, OWNED), F32),
            pltpu.VMEM((K, OWNED), F32),
            pltpu.VMEM((K, OWNED), F32),
            pltpu.VMEM((K, OWNED), F32),
            pltpu.VMEM((K, SEG), F32),
            pltpu.VMEM((K, SEG), F32),
            pltpu.VMEM((2, 4, B), F32),
            pltpu.VMEM((2, 3, 4, B), F32),
            pltpu.VMEM((2 * L, 4, B), F32),
            pltpu.VMEM((Z * Y // 2, 4, B), F32),
            pltpu.VMEM((2, 3, 8, 4, B), F32),
            dma((5,)), dma, dma, dma, dma, dma, dma, dma, dma, dma, dma,
            dma, dma, dma, dma, dma, dma, dma((2, 3)), dma, dma, dma((2, 3)), regular, regular,
        ],
        compiler_params=pltpu.CompilerParams(collective_id=0, has_side_effects=True, vmem_limit_bytes=62 * 1024 * 1024),
        name="lobpcg_step",
    )(block_rows.reshape(NB), block_cols.reshape(NB), hamiltonian_blocks.reshape(NB, B, B), current_states, previous_steps)


def solution(mesh):
    return jax.shard_map(
        body,
        mesh=mesh,
        in_specs=(
            P("row", "col", None, None, None),
            P("row", "col", None),
            P("row", "col", None),
            P(None, "row"),
            P(None, "row"),
        ),
        out_specs=(P(None, ("row", "col")), P()),
        check_vma=False,
    )
```

```python
import functools

import jax
import jax.numpy as jnp
from jax import lax
from jax.experimental import pallas as pl
from jax.experimental.pallas import tpu as pltpu
from jax.sharding import PartitionSpec as P

MESH = pl.DeviceIdType.MESH
F32 = jnp.float32
exactness = lax.Precision.HIGHEST

Z, YL, YH, L = 8, 4, 2, 8
Y = YL * YH
N_ROW, N_COL = Z * YL, L * YH
K, B, SEGB, NB = 8, 128, 32, 4
SEG = SEGB * B
SHARE, OWNED = SEG // N_COL, SEG // L
ROWS = N_ROW * SEG
rem, div = lax.rem, lax.div


def nn(a, b):
    return jnp.dot(a, b, precision=exactness, preferred_element_type=F32)


def nt(a, b):
    return lax.dot_general(a, b, (((1,), (1,)), ((), ())), precision=exactness, preferred_element_type=F32)


def lane_ids(shape):
    return lax.broadcasted_iota(jnp.int32, shape, 1)


def row_ids(shape):
    return lax.broadcasted_iota(jnp.int32, shape, 0)


def padded(a):
    return jnp.concatenate([a, jnp.zeros((B - a.shape[0], a.shape[1]), F32)], 0)


def summed(terms):
    while len(terms) > 1:
        terms = [sum(terms[i + 1 : i + 2], terms[i]) for i in range(0, len(terms), 2)]
    return terms[0]


def folded(t):
    return t[0:4] + pltpu.roll(t[4:8], 64, 1)


def unfolded(t):
    t = jnp.concatenate([t, pltpu.roll(t, 64, 1)], 0)
    return jnp.where(lane_ids(t.shape) < 64, t, 0.0)


def between(a, low, high):
    lanes = lane_ids(a.shape)
    return jnp.where(jnp.logical_and(lanes >= low, lanes < high), a, 0.0)


def packed(a):
    return folded(between(a[0:8], 0, 24) + pltpu.roll(between(a[8:16], 8, 24), 16, 1) + pltpu.roll(between(a[16:24], 16, 24), 24, 1))


def unpacked(t):
    t = unfolded(t)
    a = jnp.concatenate([between(t, 0, 24), between(pltpu.roll(t, 112, 1), 8, 24), between(pltpu.roll(t, 104, 1), 16, 24)], 0)
    same = lax.shift_right_logical(lane_ids(a.shape), 3) == lax.shift_right_logical(row_ids(a.shape), 3)
    return jnp.where(same, 0.5 * a, a)


def symmetric(a):
    unit = (lane_ids((24, B)) == row_ids((24, B))).astype(F32)
    return a + nt(unit, padded(a))


def inverse_factor(gram):
    rows, lanes = row_ids(gram.shape), lane_ids(gram.shape)
    left = gram
    right = (rows == lanes).astype(F32)
    for j in range(24):
        pivot = left[j : j + 1, j : j + 1]
        factor = jnp.where(rows[:, :1] > j, left[:, j : j + 1] / pivot, 0.0)
        top, unit = left[j : j + 1], right[j : j + 1]
        left = left - factor * top
        right = right - factor * unit
    diagonal = jnp.sum(jnp.where(rows == lanes, left, 0.0), 1, keepdims=True)
    return right / jnp.sqrt(diagonal)


def kernel(rows_ref, cols_ref, h_ref, x_ref, p_ref, q_ref, ray_ref,
           rows, cols, h, x, p, pick, far, asked, wanted, m, m_near, d, got, part, other, piece, y, y_far, mine,
           line, buf_a, buf_b, buf_c, load_sem, m_sem, ms_sem, want_sem, wants_sem, f_sem, fs_sem, d_sem, ds_sem, o_sem, os_sem,
           y_sem, ys_sem, yfar_sem, yfs_sem, a_sem, b_sem, c_sem, as_sem, bs_sem, cs_sem, step2, step3):
    r, c = lax.axis_index("row"), lax.axis_index("col")
    z, y_lo, l, y_hi = rem(r, Z), div(r, Z), rem(c, L), div(c, L)
    yy = y_hi * YL + y_lo

    def at(y_at, z_at, l_at):
        return (rem(y_at, YL) * Z + z_at, div(y_at, YL) * L + l_at)

    def send(src, dst, ss, rs, dev):
        pltpu.make_async_remote_copy(src_ref=src, dst_ref=dst, send_sem=ss, recv_sem=rs,
                                     device_id=dev, device_id_type=MESH).start()

    def done(ref, sem):
        pltpu.make_async_copy(ref, ref, sem).wait()

    loads = [pltpu.make_async_copy(src, dst, load_sem.at[i]) for i, (src, dst) in enumerate(
        ((rows_ref, rows), (cols_ref, cols), (x_ref, x), (h_ref, h), (p_ref, p)))]
    for load in loads[:2]:
        load.start()

    reads = c != 0
    q = rem(r + c, N_ROW)
    turned = jnp.logical_and(div(q, Z) == 0, z + l >= Z).astype(jnp.int32)
    source = (q, rem(y_hi + turned, YH) * L + l)

    def user(l_at):
        over = jnp.logical_and(y_lo == 0, z < l_at).astype(jnp.int32)
        to = rem(y_hi + over, YH) * L + l_at
        return rem(r + N_ROW - to, N_ROW), to

    barrier = pltpu.get_barrier_semaphore()

    @pl.when(reads)
    def _():
        pl.semaphore_signal(barrier, inc=1, device_id=source, device_id_type=MESH)
        pl.semaphore_signal(barrier, inc=1, device_id=user(l), device_id_type=MESH)

    for load in loads[2:]:
        load.start()

    def greet(n, sem, place):
        for k in range(1, n):
            pl.semaphore_signal(sem, inc=1, device_id=place(k), device_id_type=MESH)

    greet(Z, barrier, lambda k: at(yy, rem(z + k, Z), l))
    greet(Y, barrier, lambda k: at(rem(yy + k, Y), z, l))
    greet(L, barrier, lambda k: at(yy, z, rem(l + k, L)))

    for load in loads[:2]:
        load.wait()
    row_at = [jnp.full((K, B), rows[n], jnp.int32) for n in range(NB)]
    col_at = [jnp.full((K, B), cols[n], jnp.int32) for n in range(NB)]
    asks = jnp.zeros((8, B), jnp.int32)
    for n in range(NB):
        asks = jnp.where(row_ids((8, B)) == n, col_at[n], asks)
    asked[...] = asks

    @pl.when(jnp.logical_not(reads))
    def _():
        wanted[...] = asks

    pl.semaphore_wait(barrier, Z - 1 + Y - 1 + L - 1 + 2 * reads.astype(jnp.int32))

    @pl.when(reads)
    def _():
        send(asked, wanted, wants_sem, want_sem, source)

    greet(Y, step2, lambda k: at(rem(yy + k, Y), z, l))

    def blocks(ref, places):
        found = [ref[:, :B]] * NB
        for b in range(1, SEGB):
            here = ref[:, b * B : (b + 1) * B]
            found = [jnp.where(places[n] == b, here, found[n]) for n in range(NB)]
        return found

    for load in loads[2:]:
        load.wait()
    x_row, p_row = blocks(x, row_at), blocks(p, row_at)
    both = [nn(jnp.concatenate([x_row[n], p_row[n]], 0), h[n]) for n in range(NB)]
    m_x, m_p = (jnp.concatenate([both[n][k : k + K] for n in range(NB)], 1) for k in (0, K))

    @pl.when(reads)
    def _():
        m[...] = m_x
        send(m, m_near, ms_sem, m_sem, source)

    @pl.when(jnp.logical_not(reads))
    def _():
        m_near[...] = m_x

    @pl.when(reads)
    def _():
        done(wanted, want_sem)

    want = wanted[...]
    want_at = [jnp.broadcast_to(want[n : n + 1], (K, B)) for n in range(NB)]
    for i, held in enumerate((x, p)):
        picked = jnp.concatenate(blocks(held, want_at), 1)

        @pl.when(reads)
        def _(i=i, picked=picked):
            pick[i] = picked
            send(pick.at[i], far.at[i], fs_sem.at[i], f_sem.at[i], user(l))

        @pl.when(jnp.logical_not(reads))
        def _(i=i, picked=picked):
            far[i] = picked

    pl.semaphore_wait(step2, Y - 1)
    greet(Z, step3, lambda k: at(yy, rem(z + k, Z), l))

    near_last = (4, 5, 3, 6, 2, 7, 1, 0)

    y_par, y_pair = rem(yy, 2), div(yy, 2)
    slot_a = y_par * L + l
    slot_b = y_pair * Z + z

    def first(tile):
        mine[0] = tile
        for k in range(2 * L - 1):
            y_to = 2 * y_pair + rem(y_par + 1 + k // L, 2)
            send(mine.at[0], buf_a.at[slot_a], as_sem, a_sem, at(y_to, z, rem(l + near_last[k % L], L)))
        pltpu.make_async_copy(mine.at[0], buf_a.at[slot_a], a_sem).start()

    def second():
        done(buf_a, a_sem)
        mine[1] = summed([buf_a[s] for s in range(2 * L)])
        for y_k in (2, 1, 3, 0):
            for z_k in near_last:
                if y_k or z_k:
                    y_to = 2 * rem(y_pair + y_k, Y // 2) + y_par
                    send(mine.at[1], buf_b.at[slot_b], bs_sem, b_sem, at(y_to, rem(z + z_k, Z), l))
        pltpu.make_async_copy(mine.at[1], buf_b.at[slot_b], b_sem).start()

    def third():
        done(buf_b, b_sem)
        return summed([buf_b[s] for s in range(Z * Y // 2)])

    def start(i, step, tile):
        line[i, step] = tile
        slot = (l, yy, z)[step]
        for k in near_last[:-1]:
            to = (at(yy, z, rem(l + k, L)), at(rem(yy + k, Y), z, l), at(yy, rem(z + k, Z), l))[step]
            send(line.at[i, step], buf_c.at[i, step, slot], cs_sem.at[i, step], c_sem.at[i, step], to)
        pltpu.make_async_copy(line.at[i, step], buf_c.at[i, step, slot], c_sem.at[i, step]).start()

    def finish(i, step):
        done(buf_c.at[i, step], c_sem.at[i, step])
        return summed([buf_c[i, step, s] for s in range(8)])

    @pl.when(reads)
    def _():
        done(far.at[0], f_sem.at[0])

    xc = far[0]
    direct = [nt(xc[:, n * B : (n + 1) * B], h[n]) for n in range(NB)]

    @pl.when(reads)
    def _():
        done(m_near, m_sem)

    terms = [direct[n] for n in range(NB)] + [m_near[:, n * B : (n + 1) * B] for n in range(NB)]
    for b in range(SEGB):
        total = jnp.zeros((K, B), F32)
        for place, term in zip(row_at + want_at, terms):
            total = total + jnp.where(place == b, term, 0.0)
        d[:, b * B : (b + 1) * B] = total
    pl.semaphore_wait(step3, Z - 1)

    def share(l_at):
        return pl.ds(pl.multiple_of(l_at * OWNED, OWNED), OWNED)

    for k in near_last[:-1]:
        j = rem(l + k, L)
        send(d.at[:, share(j)], got.at[l], ds_sem, d_sem, at(yy, z, j))
    pltpu.make_async_copy(d.at[:, share(l)], got.at[l], d_sem).start()

    start(0, 0, folded(nt(m_x, padded(xc)) + nt(xc, padded(m_x))))
    start(0, 1, finish(0, 0))
    done(got, d_sem)
    part[...] = summed([got[s] for s in range(L)])
    send(part, other, os_sem, o_sem, (r, rem(y_hi + 1, YH) * L + l))
    start(0, 2, finish(0, 1))
    done(other, o_sem)
    piece[...] = part[...] + other[...]

    mine_of = share(l)
    for l_to in near_last:
        if l_to:
            send(piece, y_far.at[:, mine_of], yfs_sem, yfar_sem, user(l_to))
        else:
            @pl.when(c == 0)
            def _():
                pltpu.make_async_copy(piece, y_far.at[:, mine_of], yfar_sem).start()

            @pl.when(reads)
            def _():
                send(piece, y_far.at[:, mine_of], yfs_sem, yfar_sem, user(0))

    for k in near_last[:-1]:
        send(piece, y.at[:, mine_of], ys_sem, y_sem, at(yy, z, rem(l + k, L)))
    pltpu.make_async_copy(piece, y.at[:, mine_of], y_sem).start()

    theta = unfolded(finish(0, 2))[:, :K] / ROWS
    half = pl.ds(pl.multiple_of(l * OWNED + y_hi * SHARE, SHARE), SHARE)
    half_of = pl.ds(pl.multiple_of(y_hi * SHARE, SHARE), SHARE)
    own = pl.ds(pl.multiple_of(c * SHARE, SHARE), SHARE)
    residual = piece[:, half_of] - nn(theta, x[:, half])
    basis = jnp.concatenate([residual, x[:, half], p[:, half]], 0)
    start(1, 0, packed(nt(basis, padded(basis))))
    taken = nn(theta, jnp.concatenate([m_x, xc, x[:, own]], 1))

    @pl.when(reads)
    def _():
        done(far.at[1], f_sem.at[1])

    p_col = far[1]
    done(y, y_sem)
    y_row = blocks(y, row_at)
    m_r = jnp.concatenate([nn(y_row[n], h[n]) for n in range(NB)], 1) - taken[:, : NB * B]

    done(y_far, yfar_sem)
    r_col = jnp.concatenate(blocks(y_far, col_at), 1) - taken[:, NB * B : 2 * NB * B]
    left, right = jnp.concatenate([m_r, m_x, m_p], 0), jnp.concatenate([r_col, xc, p_col], 0)
    first(packed(nt(left, padded(right)) + nt(right, padded(left))))
    start(1, 1, finish(1, 0))
    second()
    start(1, 2, finish(1, 1))
    inverse = inverse_factor(symmetric(unpacked(finish(1, 2))) / ROWS)[:, :24]
    q_ref[...] = nn(inverse, jnp.concatenate([y[:, own] - taken[:, 2 * NB * B :], x[:, own], p[:, own]], 0))

    @pl.when(reads)
    def _():
        done(m, ms_sem)
        done(asked, wants_sem)

    @pl.when(reads)
    def _():
        for i in range(2):
            done(pick.at[i], fs_sem.at[i])

    done(got.at[pl.ds(0, L - 1)], ds_sem)
    done(part, os_sem)
    done(got.at[pl.ds(0, L - 1)], yfs_sem)
    done(got.at[pl.ds(0, L - 1)], ys_sem)

    @pl.when(reads)
    def _():
        done(piece, yfs_sem)

    for step in range(3):
        done(buf_c.at[0, step, pl.ds(0, 7)], cs_sem.at[0, step])
    for step in range(3):
        done(buf_c.at[1, step, pl.ds(0, 7)], cs_sem.at[1, step])
    done(buf_a.at[pl.ds(0, 2 * L - 1)], as_sem)

    half_way = nn(inverse, unpacked(third())[:, :24] / ROWS)
    ray_ref[...] = nt(half_way, inverse) + nt(inverse, half_way)
    done(buf_b.at[pl.ds(0, Z * Y // 2 - 1)], bs_sem)


def body(hamiltonian_blocks, block_rows, block_cols, current_states, previous_steps):
    vmem, anywhere = (pl.BlockSpec(memory_space=s) for s in (pltpu.VMEM, pl.ANY))
    dma, regular = pltpu.SemaphoreType.DMA, pltpu.SemaphoreType.REGULAR
    return pl.pallas_call(
        kernel,
        out_shape=(jax.ShapeDtypeStruct((3 * K, SHARE), F32), jax.ShapeDtypeStruct((3 * K, 3 * K), F32)),
        in_specs=[anywhere, anywhere, anywhere, anywhere, anywhere],
        out_specs=(vmem, vmem),
        scratch_shapes=[
            pltpu.SMEM((NB,), jnp.int32),
            pltpu.SMEM((NB,), jnp.int32),
            pltpu.VMEM((NB, B, B), F32),
            pltpu.VMEM((K, SEG), F32),
            pltpu.VMEM((K, SEG), F32),
            pltpu.VMEM((2, K, NB * B), F32),
            pltpu.VMEM((2, K, NB * B), F32),
            pltpu.VMEM((8, B), jnp.int32),
            pltpu.VMEM((8, B), jnp.int32),
            pltpu.VMEM((K, NB * B), F32),
            pltpu.VMEM((K, NB * B), F32),
            pltpu.VMEM((K, SEG), F32),
            pltpu.VMEM((L, K, OWNED), F32),
            pltpu.VMEM((K, OWNED), F32),
            pltpu.VMEM((K, OWNED), F32),
            pltpu.VMEM((K, OWNED), F32),
            pltpu.VMEM((K, SEG), F32),
            pltpu.VMEM((K, SEG), F32),
            pltpu.VMEM((2, 4, B), F32),
            pltpu.VMEM((2, 3, 4, B), F32),
            pltpu.VMEM((2 * L, 4, B), F32),
            pltpu.VMEM((Z * Y // 2, 4, B), F32),
            pltpu.VMEM((2, 3, 8, 4, B), F32),
            dma((5,)), dma, dma, dma, dma, dma((2,)), dma((2,)), dma, dma, dma, dma,
            dma, dma, dma, dma, dma, dma, dma((2, 3)), dma, dma, dma((2, 3)), regular, regular,
        ],
        compiler_params=pltpu.CompilerParams(collective_id=0, has_side_effects=True, vmem_limit_bytes=62 * 1024 * 1024),
        name="lobpcg_step",
    )(block_rows.reshape(NB), block_cols.reshape(NB), hamiltonian_blocks.reshape(NB, B, B), current_states, previous_steps)


def solution(mesh):
    return jax.shard_map(
        body,
        mesh=mesh,
        in_specs=(
            P("row", "col", None, None, None),
            P("row", "col", None),
            P("row", "col", None),
            P(None, "row"),
            P(None, "row"),
        ),
        out_specs=(P(None, ("row", "col")), P()),
        check_vma=False,
    )
```

```python
import functools

import jax
import jax.numpy as jnp
from jax import lax
from jax.experimental import pallas as pl
from jax.experimental.pallas import tpu as pltpu
from jax.sharding import PartitionSpec as P

MESH = pl.DeviceIdType.MESH
F32 = jnp.float32
exactness = lax.Precision.HIGHEST

Z, YL, YH, L = 8, 4, 2, 8
Y = YL * YH
N_ROW, N_COL = Z * YL, L * YH
K, B, SEGB, NB = 8, 128, 32, 4
SEG = SEGB * B
X = L // 2
SHARE, OWNED = SEG // N_COL, SEG // X
ROWS = N_ROW * SEG
rem, div = lax.rem, lax.div


def nn(a, b):
    return jnp.dot(a, b, precision=exactness, preferred_element_type=F32)


def nt(a, b):
    return lax.dot_general(a, b, (((1,), (1,)), ((), ())), precision=exactness, preferred_element_type=F32)


def lane_ids(shape):
    return lax.broadcasted_iota(jnp.int32, shape, 1)


def row_ids(shape):
    return lax.broadcasted_iota(jnp.int32, shape, 0)


def padded(a):
    return jnp.concatenate([a, jnp.zeros((B - a.shape[0], a.shape[1]), F32)], 0)


def summed(terms):
    while len(terms) > 1:
        terms = [sum(terms[i + 1 : i + 2], terms[i]) for i in range(0, len(terms), 2)]
    return terms[0]


def folded(t):
    return t[0:4] + pltpu.roll(t[4:8], 64, 1)


def unfolded(t):
    t = jnp.concatenate([t, pltpu.roll(t, 64, 1)], 0)
    return jnp.where(lane_ids(t.shape) < 64, t, 0.0)


def between(a, low, high):
    lanes = lane_ids(a.shape)
    return jnp.where(jnp.logical_and(lanes >= low, lanes < high), a, 0.0)


def packed(a):
    return folded(between(a[0:8], 0, 24) + pltpu.roll(between(a[8:16], 8, 24), 16, 1) + pltpu.roll(between(a[16:24], 16, 24), 24, 1))


def unpacked(t):
    t = unfolded(t)
    a = jnp.concatenate([between(t, 0, 24), between(pltpu.roll(t, 112, 1), 8, 24), between(pltpu.roll(t, 104, 1), 16, 24)], 0)
    same = lax.shift_right_logical(lane_ids(a.shape), 3) == lax.shift_right_logical(row_ids(a.shape), 3)
    return jnp.where(same, 0.5 * a, a)


def symmetric(a):
    unit = (lane_ids((24, B)) == row_ids((24, B))).astype(F32)
    return a + nt(unit, padded(a))


def inverse_factor(gram):
    rows, lanes = row_ids(gram.shape), lane_ids(gram.shape)
    left = gram
    right = (rows == lanes).astype(F32)
    for j in range(24):
        pivot = left[j : j + 1, j : j + 1]
        factor = jnp.where(rows[:, :1] > j, left[:, j : j + 1] / pivot, 0.0)
        top, unit = left[j : j + 1], right[j : j + 1]
        left = left - factor * top
        right = right - factor * unit
    diagonal = jnp.sum(jnp.where(rows == lanes, left, 0.0), 1, keepdims=True)
    return right / jnp.sqrt(diagonal)


def kernel(rows_ref, cols_ref, h_ref, x_ref, p_ref, q_ref, ray_ref,
           rows, cols, h, x, p, pick, far, asked, wanted, m, m_near, d, got, part, other, piece, products, y, y_far, mine,
           line, buf_a, buf_b, buf_c, load_sem, m_sem, ms_sem, want_sem, wants_sem, f_sem, fs_sem, d_sem, ds_sem, o_sem, os_sem,
           y_sem, ys_sem, yfar_sem, yfs_sem, a_sem, b_sem, c_sem, as_sem, bs_sem, cs_sem, step2, step3):
    r, c = lax.axis_index("row"), lax.axis_index("col")
    z, y_lo, l, y_hi = rem(r, Z), div(r, Z), rem(c, L), div(c, L)
    yy = y_hi * YL + y_lo
    xx = div(l, 2)
    main = rem(l, 2) == 1
    aside = jnp.logical_not(main)

    def at(y_at, z_at, l_at):
        return (rem(y_at, YL) * Z + z_at, div(y_at, YL) * L + l_at)

    def send(src, dst, ss, rs, dev):
        pltpu.make_async_remote_copy(src_ref=src, dst_ref=dst, send_sem=ss, recv_sem=rs,
                                     device_id=dev, device_id_type=MESH).start()

    def done(ref, sem):
        pltpu.make_async_copy(ref, ref, sem).wait()

    loads = [pltpu.make_async_copy(src, dst, load_sem.at[i]) for i, (src, dst) in enumerate(
        ((rows_ref, rows), (cols_ref, cols), (x_ref, x), (h_ref, h), (p_ref, p)))]
    for load in loads[:2]:
        load.start()

    reads = c != 0
    q = rem(r + c, N_ROW)
    turned = jnp.logical_and(div(q, Z) == 0, z + l >= Z).astype(jnp.int32)
    source = (q, rem(y_hi + turned, YH) * L + l)

    def user(l_at):
        over = jnp.logical_and(y_lo == 0, z < l_at).astype(jnp.int32)
        to = rem(y_hi + over, YH) * L + l_at
        return rem(r + N_ROW - to, N_ROW), to

    barrier = pltpu.get_barrier_semaphore()

    @pl.when(reads)
    def _():
        pl.semaphore_signal(barrier, inc=1, device_id=source, device_id_type=MESH)
        pl.semaphore_signal(barrier, inc=1, device_id=user(l), device_id_type=MESH)

    for load in loads[2:]:
        load.start()

    def greet(n, sem, place):
        for k in range(1, n):
            pl.semaphore_signal(sem, inc=1, device_id=place(k), device_id_type=MESH)

    greet(Z, barrier, lambda k: at(yy, rem(z + k, Z), l))
    greet(Y, barrier, lambda k: at(rem(yy + k, Y), z, l))
    greet(L, barrier, lambda k: at(yy, z, rem(l + k, L)))

    for load in loads[:2]:
        load.wait()
    row_at = [jnp.full((K, B), rows[n], jnp.int32) for n in range(NB)]
    col_at = [jnp.full((K, B), cols[n], jnp.int32) for n in range(NB)]
    asks = jnp.zeros((8, B), jnp.int32)
    for n in range(NB):
        asks = jnp.where(row_ids((8, B)) == n, col_at[n], asks)
    asked[...] = asks

    @pl.when(jnp.logical_not(reads))
    def _():
        wanted[...] = asks

    pl.semaphore_wait(barrier, Z - 1 + Y - 1 + L - 1 + 2 * reads.astype(jnp.int32))

    @pl.when(reads)
    def _():
        send(asked, wanted, wants_sem, want_sem, source)

    greet(Y, step2, lambda k: at(rem(yy + k, Y), z, l))

    def blocks(ref, places):
        found = [ref[:, :B]] * NB
        for b in range(1, SEGB):
            here = ref[:, b * B : (b + 1) * B]
            found = [jnp.where(places[n] == b, here, found[n]) for n in range(NB)]
        return found

    for load in loads[2:]:
        load.wait()
    x_row, p_row = blocks(x, row_at), blocks(p, row_at)
    both = [nn(jnp.concatenate([x_row[n], p_row[n]], 0), h[n]) for n in range(NB)]
    m_x, m_p = (jnp.concatenate([both[n][k : k + K] for n in range(NB)], 1) for k in (0, K))

    @pl.when(reads)
    def _():
        m[...] = m_x
        send(m, m_near, ms_sem, m_sem, source)

    @pl.when(jnp.logical_not(reads))
    def _():
        m_near[...] = m_x

    @pl.when(reads)
    def _():
        done(wanted, want_sem)

    want = wanted[...]
    want_at = [jnp.broadcast_to(want[n : n + 1], (K, B)) for n in range(NB)]
    for i, held in enumerate((x, p)):
        picked = jnp.concatenate(blocks(held, want_at), 1)

        @pl.when(reads)
        def _(i=i, picked=picked):
            pick[i] = picked
            send(pick.at[i], far.at[i], fs_sem.at[i], f_sem.at[i], user(l))

        @pl.when(jnp.logical_not(reads))
        def _(i=i, picked=picked):
            far[i] = picked

    pl.semaphore_wait(step2, Y - 1)
    greet(Z, step3, lambda k: at(yy, rem(z + k, Z), l))

    near_last = (4, 5, 3, 6, 2, 7, 1, 0)

    y_par, y_pair = rem(yy, 2), div(yy, 2)
    slot_a = y_par * L + l
    slot_b = y_pair * Z + z

    def first(tile):
        mine[0] = tile
        for y_k in (1, 0):
            for x_k in (2, 1, 3, 0):
                to = at(2 * y_pair + rem(y_par + y_k, 2), z, 2 * rem(xx + x_k, X) + 1)
                if y_k or x_k:
                    send(mine.at[0], buf_a.at[slot_a], as_sem, a_sem, to)
                else:
                    @pl.when(main)
                    def _():
                        pltpu.make_async_copy(mine.at[0], buf_a.at[slot_a], a_sem).start()

                    @pl.when(aside)
                    def _(to=to):
                        send(mine.at[0], buf_a.at[slot_a], as_sem, a_sem, to)

    def second():
        @pl.when(main)
        def _():
            done(buf_a, a_sem)
            mine[1] = summed([buf_a[s] for s in range(2 * L)])
            for y_k in (2, 1, 3, 0):
                for z_k in near_last:
                    for core in (0, 1):
                        if y_k or z_k or core == 0:
                            to = at(2 * rem(y_pair + y_k, Y // 2) + y_par, rem(z + z_k, Z), 2 * xx + core)
                            send(mine.at[1], buf_b.at[slot_b], bs_sem, b_sem, to)
            pltpu.make_async_copy(mine.at[1], buf_b.at[slot_b], b_sem).start()

    def third():
        done(buf_b, b_sem)
        return summed([buf_b[s] for s in range(Z * Y // 2)])

    def start(i, step, tile):
        line[i, step] = tile
        slot = (l, yy, z)[step]
        for k in near_last[:-1]:
            to = (at(yy, z, rem(l + k, L)), at(rem(yy + k, Y), z, l), at(yy, rem(z + k, Z), l))[step]
            send(line.at[i, step], buf_c.at[i, step, slot], cs_sem.at[i, step], c_sem.at[i, step], to)
        pltpu.make_async_copy(line.at[i, step], buf_c.at[i, step, slot], c_sem.at[i, step]).start()

    def finish(i, step):
        done(buf_c.at[i, step], c_sem.at[i, step])
        return summed([buf_c[i, step, s] for s in range(8)])

    @pl.when(reads)
    def _():
        done(far.at[0], f_sem.at[0])

    xc = far[0]
    direct = [nt(xc[:, n * B : (n + 1) * B], h[n]) for n in range(NB)]

    @pl.when(reads)
    def _():
        done(m_near, m_sem)

    terms = [direct[n] for n in range(NB)] + [m_near[:, n * B : (n + 1) * B] for n in range(NB)]
    for b in range(SEGB):
        total = jnp.zeros((K, B), F32)
        for place, term in zip(row_at + want_at, terms):
            total = total + jnp.where(place == b, term, 0.0)
        d[:, b * B : (b + 1) * B] = total
    pl.semaphore_wait(step3, Z - 1)

    def share(x_at):
        return pl.ds(pl.multiple_of(x_at * OWNED, OWNED), OWNED)

    for k in (2, 1, 3, 0):
        j = rem(xx + k, X)
        src, to = d.at[:, share(j)], at(yy, z, 2 * j + 1)
        if k:
            send(src, got.at[l], ds_sem, d_sem, to)
        else:
            @pl.when(main)
            def _(src=src):
                pltpu.make_async_copy(src, got.at[l], d_sem).start()

            @pl.when(aside)
            def _(src=src, to=to):
                send(src, got.at[l], ds_sem, d_sem, to)

    start(0, 0, folded(nt(m_x, padded(xc)) + nt(xc, padded(m_x))))
    start(0, 1, finish(0, 0))
    @pl.when(main)
    def _():
        done(got, d_sem)
        part[...] = summed([got[s] for s in range(L)])
        send(part, other, os_sem, o_sem, (r, rem(y_hi + 1, YH) * L + l))

    start(0, 2, finish(0, 1))

    @pl.when(main)
    def _():
        done(other, o_sem)
        piece[...] = part[...] + other[...]
        mine_of = share(xx)
        for l_to in near_last:
            send(piece, y_far.at[:, mine_of], yfs_sem, yfar_sem, user(l_to))
        for k in near_last[:-1]:
            send(piece, y.at[:, mine_of], ys_sem, y_sem, at(yy, z, rem(l + k, L)))
        pltpu.make_async_copy(piece, y.at[:, mine_of], y_sem).start()

    theta = unfolded(finish(0, 2))[:, :K] / ROWS
    own = pl.ds(pl.multiple_of(c * SHARE, SHARE), SHARE)

    @pl.when(main)
    def _():
        width = OWNED // YH
        half = pl.ds(pl.multiple_of(xx * OWNED + y_hi * width, width), width)
        half_of = pl.ds(pl.multiple_of(y_hi * width, width), width)
        residual = piece[:, half_of] - nn(theta, x[:, half])
        basis = jnp.concatenate([residual, x[:, half], p[:, half]], 0)
        products[...] = packed(nt(basis, padded(basis)))

    @pl.when(aside)
    def _():
        products[...] = jnp.zeros_like(products)

    start(1, 0, products[...])
    taken = nn(theta, jnp.concatenate([m_x, xc, x[:, own]], 1))

    @pl.when(reads)
    def _():
        done(far.at[1], f_sem.at[1])

    p_col = far[1]
    done(y, y_sem)
    y_row = blocks(y, row_at)
    m_r = jnp.concatenate([nn(y_row[n], h[n]) for n in range(NB)], 1) - taken[:, : NB * B]

    done(y_far, yfar_sem)
    r_col = jnp.concatenate(blocks(y_far, col_at), 1) - taken[:, NB * B : 2 * NB * B]
    left, right = jnp.concatenate([m_r, m_x, m_p], 0), jnp.concatenate([r_col, xc, p_col], 0)
    first(packed(nt(left, padded(right)) + nt(right, padded(left))))
    start(1, 1, finish(1, 0))
    second()
    start(1, 2, finish(1, 1))
    inverse = inverse_factor(symmetric(unpacked(finish(1, 2))) / ROWS)[:, :24]
    q_ref[...] = nn(inverse, jnp.concatenate([y[:, own] - taken[:, 2 * NB * B :], x[:, own], p[:, own]], 0))

    @pl.when(reads)
    def _():
        done(m, ms_sem)
        done(asked, wants_sem)

    @pl.when(reads)
    def _():
        for i in range(2):
            done(pick.at[i], fs_sem.at[i])

    done(got.at[pl.ds(0, X - 1)], ds_sem)
    done(buf_a.at[pl.ds(0, L - 1)], as_sem)

    @pl.when(aside)
    def _():
        done(got.at[0], ds_sem)
        done(buf_a.at[0], as_sem)

    @pl.when(main)
    def _():
        done(part, os_sem)
        done(got, yfs_sem)
        done(got.at[pl.ds(0, L - 1)], ys_sem)

    for step in range(3):
        done(buf_c.at[0, step, pl.ds(0, 7)], cs_sem.at[0, step])
    for step in range(3):
        done(buf_c.at[1, step, pl.ds(0, 7)], cs_sem.at[1, step])

    half_way = nn(inverse, unpacked(third())[:, :24] / ROWS)
    ray_ref[...] = nt(half_way, inverse) + nt(inverse, half_way)

    @pl.when(main)
    def _():
        done(buf_b, bs_sem)
        done(buf_b.at[pl.ds(0, Z * Y // 2 - 1)], bs_sem)


def body(hamiltonian_blocks, block_rows, block_cols, current_states, previous_steps):
    vmem, anywhere = (pl.BlockSpec(memory_space=s) for s in (pltpu.VMEM, pl.ANY))
    dma, regular = pltpu.SemaphoreType.DMA, pltpu.SemaphoreType.REGULAR
    return pl.pallas_call(
        kernel,
        out_shape=(jax.ShapeDtypeStruct((3 * K, SHARE), F32), jax.ShapeDtypeStruct((3 * K, 3 * K), F32)),
        in_specs=[anywhere, anywhere, anywhere, anywhere, anywhere],
        out_specs=(vmem, vmem),
        scratch_shapes=[
            pltpu.SMEM((NB,), jnp.int32),
            pltpu.SMEM((NB,), jnp.int32),
            pltpu.VMEM((NB, B, B), F32),
            pltpu.VMEM((K, SEG), F32),
            pltpu.VMEM((K, SEG), F32),
            pltpu.VMEM((2, K, NB * B), F32),
            pltpu.VMEM((2, K, NB * B), F32),
            pltpu.VMEM((8, B), jnp.int32),
            pltpu.VMEM((8, B), jnp.int32),
            pltpu.VMEM((K, NB * B), F32),
            pltpu.VMEM((K, NB * B), F32),
            pltpu.VMEM((K, SEG), F32),
            pltpu.VMEM((L, K, OWNED), F32),
            pltpu.VMEM((K, OWNED), F32),
            pltpu.VMEM((K, OWNED), F32),
            pltpu.VMEM((K, OWNED), F32),
            pltpu.VMEM((4, B), F32),
            pltpu.VMEM((K, SEG), F32),
            pltpu.VMEM((K, SEG), F32),
            pltpu.VMEM((2, 4, B), F32),
            pltpu.VMEM((2, 3, 4, B), F32),
            pltpu.VMEM((2 * L, 4, B), F32),
            pltpu.VMEM((Z * Y // 2, 4, B), F32),
            pltpu.VMEM((2, 3, 8, 4, B), F32),
            dma((5,)), dma, dma, dma, dma, dma((2,)), dma((2,)), dma, dma, dma, dma,
            dma, dma, dma, dma, dma, dma, dma((2, 3)), dma, dma, dma((2, 3)), regular, regular,
        ],
        compiler_params=pltpu.CompilerParams(collective_id=0, has_side_effects=True, vmem_limit_bytes=62 * 1024 * 1024),
        name="lobpcg_step",
    )(block_rows.reshape(NB), block_cols.reshape(NB), hamiltonian_blocks.reshape(NB, B, B), current_states, previous_steps)


def solution(mesh):
    return jax.shard_map(
        body,
        mesh=mesh,
        in_specs=(
            P("row", "col", None, None, None),
            P("row", "col", None),
            P("row", "col", None),
            P(None, "row"),
            P(None, "row"),
        ),
        out_specs=(P(None, ("row", "col")), P()),
        check_vma=False,
    )
```

```python
import functools

import jax
import jax.numpy as jnp
from jax import lax
from jax.experimental import pallas as pl
from jax.experimental.pallas import tpu as pltpu
from jax.sharding import PartitionSpec as P

MESH = pl.DeviceIdType.MESH
F32 = jnp.float32
exactness = lax.Precision.HIGHEST

Z, YL, YH, L = 8, 4, 2, 8
Y = YL * YH
N_ROW, N_COL = Z * YL, L * YH
K, B, SEGB, NB = 8, 128, 32, 4
SEG = SEGB * B
X = L // 2
SHARE, OWNED = SEG // N_COL, SEG // X
ROWS = N_ROW * SEG
rem, div = lax.rem, lax.div


def nn(a, b):
    return jnp.dot(a, b, precision=exactness, preferred_element_type=F32)


def nt(a, b):
    return lax.dot_general(a, b, (((1,), (1,)), ((), ())), precision=exactness, preferred_element_type=F32)


def lane_ids(shape):
    return lax.broadcasted_iota(jnp.int32, shape, 1)


def row_ids(shape):
    return lax.broadcasted_iota(jnp.int32, shape, 0)


def padded(a):
    return jnp.concatenate([a, jnp.zeros((B - a.shape[0], a.shape[1]), F32)], 0)


def summed(terms):
    while len(terms) > 1:
        terms = [sum(terms[i + 1 : i + 2], terms[i]) for i in range(0, len(terms), 2)]
    return terms[0]


def folded(t):
    return t[0:4] + pltpu.roll(t[4:8], 64, 1)


def unfolded(t):
    t = jnp.concatenate([t, pltpu.roll(t, 64, 1)], 0)
    return jnp.where(lane_ids(t.shape) < 64, t, 0.0)


def between(a, low, high):
    lanes = lane_ids(a.shape)
    return jnp.where(jnp.logical_and(lanes >= low, lanes < high), a, 0.0)


def packed(a):
    return folded(between(a[0:8], 0, 24) + pltpu.roll(between(a[8:16], 8, 24), 16, 1) + pltpu.roll(between(a[16:24], 16, 24), 24, 1))


def unpacked(t):
    t = unfolded(t)
    a = jnp.concatenate([between(t, 0, 24), between(pltpu.roll(t, 112, 1), 8, 24), between(pltpu.roll(t, 104, 1), 16, 24)], 0)
    same = lax.shift_right_logical(lane_ids(a.shape), 3) == lax.shift_right_logical(row_ids(a.shape), 3)
    return jnp.where(same, 0.5 * a, a)


def symmetric(a):
    unit = (lane_ids((24, B)) == row_ids((24, B))).astype(F32)
    return a + nt(unit, padded(a))


def inverse_factor(gram):
    rows, lanes = row_ids(gram.shape), lane_ids(gram.shape)
    left = gram
    right = (rows == lanes).astype(F32)
    for j in range(24):
        pivot = left[j : j + 1, j : j + 1]
        factor = jnp.where(rows[:, :1] > j, left[:, j : j + 1] / pivot, 0.0)
        top, unit = left[j : j + 1], right[j : j + 1]
        left = left - factor * top
        right = right - factor * unit
    diagonal = jnp.sum(jnp.where(rows == lanes, left, 0.0), 1, keepdims=True)
    return right / jnp.sqrt(diagonal)


def kernel(rows_ref, cols_ref, h_ref, x_ref, p_ref, q_ref, ray_ref,
           rows, cols, h, x, p, pick, far, asked, wanted, m, m_near, d, got, part, other, piece, products, y, y_far, mine,
           buf_a, buf_b, whole, load_sem, m_sem, ms_sem, want_sem, wants_sem, f_sem, fs_sem, d_sem, ds_sem, o_sem, os_sem,
           y_sem, ys_sem, yfar_sem, yfs_sem, a_sem, b_sem, w_sem, as_sem, bs_sem, ws_sem, step2, step3):
    r, c = lax.axis_index("row"), lax.axis_index("col")
    z, y_lo, l, y_hi = rem(r, Z), div(r, Z), rem(c, L), div(c, L)
    yy = y_hi * YL + y_lo
    xx = div(l, 2)
    main = rem(l, 2) == 1
    aside = jnp.logical_not(main)

    def at(y_at, z_at, l_at):
        return (rem(y_at, YL) * Z + z_at, div(y_at, YL) * L + l_at)

    def send(src, dst, ss, rs, dev):
        pltpu.make_async_remote_copy(src_ref=src, dst_ref=dst, send_sem=ss, recv_sem=rs,
                                     device_id=dev, device_id_type=MESH).start()

    def done(ref, sem):
        pltpu.make_async_copy(ref, ref, sem).wait()

    loads = [pltpu.make_async_copy(src, dst, load_sem.at[i]) for i, (src, dst) in enumerate(
        ((rows_ref, rows), (cols_ref, cols), (x_ref, x), (h_ref, h), (p_ref, p)))]
    for load in loads[:2]:
        load.start()

    reads = c != 0
    q = rem(r + c, N_ROW)
    turned = jnp.logical_and(div(q, Z) == 0, z + l >= Z).astype(jnp.int32)
    source = (q, rem(y_hi + turned, YH) * L + l)

    def user(l_at):
        over = jnp.logical_and(y_lo == 0, z < l_at).astype(jnp.int32)
        to = rem(y_hi + over, YH) * L + l_at
        return rem(r + N_ROW - to, N_ROW), to

    barrier = pltpu.get_barrier_semaphore()

    @pl.when(reads)
    def _():
        pl.semaphore_signal(barrier, inc=1, device_id=source, device_id_type=MESH)
        pl.semaphore_signal(barrier, inc=1, device_id=user(l), device_id_type=MESH)

    for load in loads[2:]:
        load.start()

    def greet(n, sem, place):
        for k in range(1, n):
            pl.semaphore_signal(sem, inc=1, device_id=place(k), device_id_type=MESH)

    greet(Z, barrier, lambda k: at(yy, rem(z + k, Z), l))
    greet(Y, barrier, lambda k: at(rem(yy + k, Y), z, l))
    greet(L, barrier, lambda k: at(yy, z, rem(l + k, L)))

    for load in loads[:2]:
        load.wait()
    row_at = [jnp.full((K, B), rows[n], jnp.int32) for n in range(NB)]
    col_at = [jnp.full((K, B), cols[n], jnp.int32) for n in range(NB)]
    asks = jnp.zeros((8, B), jnp.int32)
    for n in range(NB):
        asks = jnp.where(row_ids((8, B)) == n, col_at[n], asks)
    asked[...] = asks

    @pl.when(jnp.logical_not(reads))
    def _():
        wanted[...] = asks

    pl.semaphore_wait(barrier, Z - 1 + Y - 1 + L - 1 + 2 * reads.astype(jnp.int32))

    @pl.when(reads)
    def _():
        send(asked, wanted, wants_sem, want_sem, source)

    greet(Y, step2, lambda k: at(rem(yy + k, Y), z, l))

    def blocks(ref, places):
        found = [ref[:, :B]] * NB
        for b in range(1, SEGB):
            here = ref[:, b * B : (b + 1) * B]
            found = [jnp.where(places[n] == b, here, found[n]) for n in range(NB)]
        return found

    for load in loads[2:]:
        load.wait()
    x_row, p_row = blocks(x, row_at), blocks(p, row_at)
    both = [nn(jnp.concatenate([x_row[n], p_row[n]], 0), h[n]) for n in range(NB)]
    m_x, m_p = (jnp.concatenate([both[n][k : k + K] for n in range(NB)], 1) for k in (0, K))

    @pl.when(reads)
    def _():
        m[...] = m_x
        send(m, m_near, ms_sem, m_sem, source)

    @pl.when(jnp.logical_not(reads))
    def _():
        m_near[...] = m_x

    @pl.when(reads)
    def _():
        done(wanted, want_sem)

    want = wanted[...]
    want_at = [jnp.broadcast_to(want[n : n + 1], (K, B)) for n in range(NB)]
    for i, held in enumerate((x, p)):
        picked = jnp.concatenate(blocks(held, want_at), 1)

        @pl.when(reads)
        def _(i=i, picked=picked):
            pick[i] = picked
            send(pick.at[i], far.at[i], fs_sem.at[i], f_sem.at[i], user(l))

        @pl.when(jnp.logical_not(reads))
        def _(i=i, picked=picked):
            far[i] = picked

    pl.semaphore_wait(step2, Y - 1)
    greet(Z, step3, lambda k: at(yy, rem(z + k, Z), l))

    near_last = (4, 5, 3, 6, 2, 7, 1, 0)

    y_par, y_pair = rem(yy, 2), div(yy, 2)
    slot_a = y_par * L + l
    slot_b = y_pair * Z + z

    def first(i, tile):
        mine[i, 0] = tile
        src, dst = mine.at[i, 0], buf_a.at[i, slot_a]
        for y_k in (1, 0):
            for x_k in (2, 1, 3, 0):
                to = at(2 * y_pair + rem(y_par + y_k, 2), z, 2 * rem(xx + x_k, X) + 1)
                if y_k or x_k:
                    send(src, dst, as_sem.at[i], a_sem.at[i], to)
                else:
                    @pl.when(main)
                    def _():
                        pltpu.make_async_copy(src, dst, a_sem.at[i]).start()

                    @pl.when(aside)
                    def _(to=to):
                        send(src, dst, as_sem.at[i], a_sem.at[i], to)

    def second(i):
        @pl.when(main)
        def _():
            done(buf_a.at[i], a_sem.at[i])
            mine[i, 1] = summed([buf_a[i, s] for s in range(2 * L)])
            src, dst = mine.at[i, 1], buf_b.at[i, slot_b]
            for y_k in (2, 1, 3, 0):
                for z_k in near_last:
                    for core in (0, 1) if i == 2 else (1,):
                        if y_k or z_k or core == 0:
                            to = at(2 * rem(y_pair + y_k, Y // 2) + y_par, rem(z + z_k, Z), 2 * xx + core)
                            send(src, dst, bs_sem.at[i], b_sem.at[i], to)
            pltpu.make_async_copy(src, dst, b_sem.at[i]).start()

    def third(i):
        if i == 2:
            done(buf_b.at[i], b_sem.at[i])
            return summed([buf_b[i, s] for s in range(Z * Y // 2)])

        @pl.when(main)
        def _():
            done(buf_b.at[i], b_sem.at[i])
            whole[i] = summed([buf_b[i, s] for s in range(Z * Y // 2)])
            send(whole.at[i], whole.at[i], ws_sem.at[i], w_sem.at[i], at(yy, z, 2 * xx))

        @pl.when(aside)
        def _():
            done(whole.at[i], w_sem.at[i])

        return whole[i]

    @pl.when(reads)
    def _():
        done(far.at[0], f_sem.at[0])

    xc = far[0]
    direct = [nt(xc[:, n * B : (n + 1) * B], h[n]) for n in range(NB)]

    @pl.when(reads)
    def _():
        done(m_near, m_sem)

    terms = [direct[n] for n in range(NB)] + [m_near[:, n * B : (n + 1) * B] for n in range(NB)]
    for b in range(SEGB):
        total = jnp.zeros((K, B), F32)
        for place, term in zip(row_at + want_at, terms):
            total = total + jnp.where(place == b, term, 0.0)
        d[:, b * B : (b + 1) * B] = total
    pl.semaphore_wait(step3, Z - 1)

    def share(x_at):
        return pl.ds(pl.multiple_of(x_at * OWNED, OWNED), OWNED)

    for k in (2, 1, 3, 0):
        j = rem(xx + k, X)
        src, to = d.at[:, share(j)], at(yy, z, 2 * j + 1)
        if k:
            send(src, got.at[l], ds_sem, d_sem, to)
        else:
            @pl.when(main)
            def _(src=src):
                pltpu.make_async_copy(src, got.at[l], d_sem).start()

            @pl.when(aside)
            def _(src=src, to=to):
                send(src, got.at[l], ds_sem, d_sem, to)

    first(0, folded(nt(m_x, padded(xc)) + nt(xc, padded(m_x))))
    @pl.when(main)
    def _():
        done(got, d_sem)
        part[...] = summed([got[s] for s in range(L)])
        send(part, other, os_sem, o_sem, (r, rem(y_hi + 1, YH) * L + l))

    second(0)

    @pl.when(main)
    def _():
        done(other, o_sem)
        piece[...] = part[...] + other[...]
        mine_of = share(xx)
        for l_to in near_last:
            send(piece, y_far.at[:, mine_of], yfs_sem, yfar_sem, user(l_to))
        for k in near_last[:-1]:
            send(piece, y.at[:, mine_of], ys_sem, y_sem, at(yy, z, rem(l + k, L)))
        pltpu.make_async_copy(piece, y.at[:, mine_of], y_sem).start()

    theta = unfolded(third(0))[:, :K] / ROWS
    own = pl.ds(pl.multiple_of(c * SHARE, SHARE), SHARE)

    @pl.when(main)
    def _():
        width = OWNED // YH
        half = pl.ds(pl.multiple_of(xx * OWNED + y_hi * width, width), width)
        half_of = pl.ds(pl.multiple_of(y_hi * width, width), width)
        residual = piece[:, half_of] - nn(theta, x[:, half])
        basis = jnp.concatenate([residual, x[:, half], p[:, half]], 0)
        products[...] = packed(nt(basis, padded(basis)))

    @pl.when(aside)
    def _():
        products[...] = jnp.zeros_like(products)

    first(1, products[...])
    taken = nn(theta, jnp.concatenate([m_x, xc, x[:, own]], 1))

    @pl.when(reads)
    def _():
        done(far.at[1], f_sem.at[1])

    p_col = far[1]
    done(y, y_sem)
    y_row = blocks(y, row_at)
    m_r = jnp.concatenate([nn(y_row[n], h[n]) for n in range(NB)], 1) - taken[:, : NB * B]

    second(1)
    done(y_far, yfar_sem)
    r_col = jnp.concatenate(blocks(y_far, col_at), 1) - taken[:, NB * B : 2 * NB * B]
    left, right = jnp.concatenate([m_r, m_x, m_p], 0), jnp.concatenate([r_col, xc, p_col], 0)
    first(2, packed(nt(left, padded(right)) + nt(right, padded(left))))
    second(2)
    inverse = inverse_factor(symmetric(unpacked(third(1))) / ROWS)[:, :24]
    q_ref[...] = nn(inverse, jnp.concatenate([y[:, own] - taken[:, 2 * NB * B :], x[:, own], p[:, own]], 0))

    @pl.when(reads)
    def _():
        done(m, ms_sem)
        done(asked, wants_sem)

    @pl.when(reads)
    def _():
        for i in range(2):
            done(pick.at[i], fs_sem.at[i])

    done(got.at[pl.ds(0, X - 1)], ds_sem)
    for i in range(3):
        done(buf_a.at[i, pl.ds(0, L - 1)], as_sem.at[i])

    @pl.when(aside)
    def _():
        done(got.at[0], ds_sem)
        for i in range(3):
            done(buf_a.at[i, 0], as_sem.at[i])

    @pl.when(main)
    def _():
        done(part, os_sem)
        done(got, yfs_sem)
        done(got.at[pl.ds(0, L - 1)], ys_sem)
        for i in range(2):
            done(buf_b.at[i, pl.ds(0, Z * Y // 2 - 1)], bs_sem.at[i])
            done(whole.at[i], ws_sem.at[i])

    half_way = nn(inverse, unpacked(third(2))[:, :24] / ROWS)
    ray_ref[...] = nt(half_way, inverse) + nt(inverse, half_way)

    @pl.when(main)
    def _():
        done(buf_b.at[2], bs_sem.at[2])
        done(buf_b.at[2, pl.ds(0, Z * Y // 2 - 1)], bs_sem.at[2])


def body(hamiltonian_blocks, block_rows, block_cols, current_states, previous_steps):
    vmem, anywhere = (pl.BlockSpec(memory_space=s) for s in (pltpu.VMEM, pl.ANY))
    dma, regular = pltpu.SemaphoreType.DMA, pltpu.SemaphoreType.REGULAR
    return pl.pallas_call(
        kernel,
        out_shape=(jax.ShapeDtypeStruct((3 * K, SHARE), F32), jax.ShapeDtypeStruct((3 * K, 3 * K), F32)),
        in_specs=[anywhere, anywhere, anywhere, anywhere, anywhere],
        out_specs=(vmem, vmem),
        scratch_shapes=[
            pltpu.SMEM((NB,), jnp.int32),
            pltpu.SMEM((NB,), jnp.int32),
            pltpu.VMEM((NB, B, B), F32),
            pltpu.VMEM((K, SEG), F32),
            pltpu.VMEM((K, SEG), F32),
            pltpu.VMEM((2, K, NB * B), F32),
            pltpu.VMEM((2, K, NB * B), F32),
            pltpu.VMEM((8, B), jnp.int32),
            pltpu.VMEM((8, B), jnp.int32),
            pltpu.VMEM((K, NB * B), F32),
            pltpu.VMEM((K, NB * B), F32),
            pltpu.VMEM((K, SEG), F32),
            pltpu.VMEM((L, K, OWNED), F32),
            pltpu.VMEM((K, OWNED), F32),
            pltpu.VMEM((K, OWNED), F32),
            pltpu.VMEM((K, OWNED), F32),
            pltpu.VMEM((4, B), F32),
            pltpu.VMEM((K, SEG), F32),
            pltpu.VMEM((K, SEG), F32),
            pltpu.VMEM((3, 2, 4, B), F32),
            pltpu.VMEM((3, 2 * L, 4, B), F32),
            pltpu.VMEM((3, Z * Y // 2, 4, B), F32),
            pltpu.VMEM((2, 4, B), F32),
            dma((5,)), dma, dma, dma, dma, dma((2,)), dma((2,)), dma, dma, dma, dma,
            dma, dma, dma, dma, dma((3,)), dma((3,)), dma((2,)), dma((3,)), dma((3,)), dma((2,)), regular, regular,
        ],
        compiler_params=pltpu.CompilerParams(collective_id=0, has_side_effects=True, vmem_limit_bytes=62 * 1024 * 1024),
        name="lobpcg_step",
    )(block_rows.reshape(NB), block_cols.reshape(NB), hamiltonian_blocks.reshape(NB, B, B), current_states, previous_steps)


def solution(mesh):
    return jax.shard_map(
        body,
        mesh=mesh,
        in_specs=(
            P("row", "col", None, None, None),
            P("row", "col", None),
            P("row", "col", None),
            P(None, "row"),
            P(None, "row"),
        ),
        out_specs=(P(None, ("row", "col")), P()),
        check_vma=False,
    )
```

```python
import functools

import jax
import jax.numpy as jnp
from jax import lax
from jax.experimental import pallas as pl
from jax.experimental.pallas import tpu as pltpu
from jax.sharding import PartitionSpec as P

MESH = pl.DeviceIdType.MESH
F32 = jnp.float32
exactness = lax.Precision.HIGHEST

Z, YL, YH, L = 8, 4, 2, 8
Y = YL * YH
N_ROW, N_COL = Z * YL, L * YH
K, B, SEGB, NB = 8, 128, 32, 4
SEG = SEGB * B
X = L // 2
SHARE, OWNED = SEG // N_COL, SEG // X
ROWS = N_ROW * SEG
rem, div = lax.rem, lax.div


def nn(a, b):
    return jnp.dot(a, b, precision=exactness, preferred_element_type=F32)


def nt(a, b):
    return lax.dot_general(a, b, (((1,), (1,)), ((), ())), precision=exactness, preferred_element_type=F32)


def lane_ids(shape):
    return lax.broadcasted_iota(jnp.int32, shape, 1)


def row_ids(shape):
    return lax.broadcasted_iota(jnp.int32, shape, 0)


def padded(a):
    return jnp.concatenate([a, jnp.zeros((B - a.shape[0], a.shape[1]), F32)], 0)


def summed(terms):
    while len(terms) > 1:
        terms = [sum(terms[i + 1 : i + 2], terms[i]) for i in range(0, len(terms), 2)]
    return terms[0]


def folded(t):
    return t[0:4] + pltpu.roll(t[4:8], 64, 1)


def unfolded(t):
    t = jnp.concatenate([t, pltpu.roll(t, 64, 1)], 0)
    return jnp.where(lane_ids(t.shape) < 64, t, 0.0)


def between(a, low, high):
    lanes = lane_ids(a.shape)
    return jnp.where(jnp.logical_and(lanes >= low, lanes < high), a, 0.0)


def packed(a):
    return folded(between(a[0:8], 0, 24) + pltpu.roll(between(a[8:16], 8, 24), 16, 1) + pltpu.roll(between(a[16:24], 16, 24), 24, 1))


def unpacked(t):
    t = unfolded(t)
    a = jnp.concatenate([between(t, 0, 24), between(pltpu.roll(t, 112, 1), 8, 24), between(pltpu.roll(t, 104, 1), 16, 24)], 0)
    same = lax.shift_right_logical(lane_ids(a.shape), 3) == lax.shift_right_logical(row_ids(a.shape), 3)
    return jnp.where(same, 0.5 * a, a)


def symmetric(a):
    unit = (lane_ids((24, B)) == row_ids((24, B))).astype(F32)
    return a + nt(unit, padded(a))


def inverse_factor(gram):
    rows, lanes = row_ids(gram.shape), lane_ids(gram.shape)
    left = gram
    right = (rows == lanes).astype(F32)
    for j in range(24):
        pivot = left[j : j + 1, j : j + 1]
        factor = jnp.where(rows[:, :1] > j, left[:, j : j + 1] / pivot, 0.0)
        top, unit = left[j : j + 1], right[j : j + 1]
        left = left - factor * top
        right = right - factor * unit
    diagonal = jnp.sum(jnp.where(rows == lanes, left, 0.0), 1, keepdims=True)
    return right / jnp.sqrt(diagonal)


def kernel(rows_ref, cols_ref, h_ref, x_ref, p_ref, q_ref, ray_ref,
           rows, cols, h, x, p, pick, far, asked, wanted, m, m_near, d, got, part, other, piece, products, y, y_far, mine,
           buf_a, buf_b, whole, load_sem, m_sem, ms_sem, want_sem, wants_sem, f_sem, fs_sem, d_sem, ds_sem, o_sem, os_sem,
           y_sem, ys_sem, yfar_sem, yfs_sem, a_sem, b_sem, w_sem, as_sem, bs_sem, ws_sem, step2, step3):
    r, c = lax.axis_index("row"), lax.axis_index("col")
    z, y_lo, l, y_hi = rem(r, Z), div(r, Z), rem(c, L), div(c, L)
    yy = y_hi * YL + y_lo
    xx = div(l, 2)
    main = rem(l, 2) == 1
    aside = jnp.logical_not(main)

    def at(y_at, z_at, l_at):
        return (rem(y_at, YL) * Z + z_at, div(y_at, YL) * L + l_at)

    def send(src, dst, ss, rs, dev):
        pltpu.make_async_remote_copy(src_ref=src, dst_ref=dst, send_sem=ss, recv_sem=rs,
                                     device_id=dev, device_id_type=MESH).start()

    def done(ref, sem):
        pltpu.make_async_copy(ref, ref, sem).wait()

    loads = [pltpu.make_async_copy(src, dst, load_sem.at[i]) for i, (src, dst) in enumerate(
        ((rows_ref, rows), (cols_ref, cols), (x_ref, x), (h_ref, h), (p_ref, p)))]
    for load in loads[:2]:
        load.start()

    reads = c != 0
    q = rem(r + c, N_ROW)
    turned = jnp.logical_and(div(q, Z) == 0, z + l >= Z).astype(jnp.int32)
    source = (q, rem(y_hi + turned, YH) * L + l)

    def user(l_at):
        over = jnp.logical_and(y_lo == 0, z < l_at).astype(jnp.int32)
        to = rem(y_hi + over, YH) * L + l_at
        return rem(r + N_ROW - to, N_ROW), to

    barrier = pltpu.get_barrier_semaphore()

    @pl.when(reads)
    def _():
        pl.semaphore_signal(barrier, inc=1, device_id=source, device_id_type=MESH)
        pl.semaphore_signal(barrier, inc=1, device_id=user(l), device_id_type=MESH)

    for load in loads[2:]:
        load.start()

    def greet(n, sem, place):
        for k in range(1, n):
            pl.semaphore_signal(sem, inc=1, device_id=place(k), device_id_type=MESH)

    greet(Z, barrier, lambda k: at(yy, rem(z + k, Z), l))
    greet(Y, barrier, lambda k: at(rem(yy + k, Y), z, l))
    greet(L, barrier, lambda k: at(yy, z, rem(l + k, L)))

    for load in loads[:2]:
        load.wait()
    row_at = [jnp.full((K, B), rows[n], jnp.int32) for n in range(NB)]
    col_at = [jnp.full((K, B), cols[n], jnp.int32) for n in range(NB)]
    asks = jnp.zeros((8, B), jnp.int32)
    for n in range(NB):
        asks = jnp.where(row_ids((8, B)) == n, col_at[n], asks)
    asked[...] = asks

    @pl.when(jnp.logical_not(reads))
    def _():
        wanted[...] = asks

    pl.semaphore_wait(barrier, Z - 1 + Y - 1 + L - 1 + 2 * reads.astype(jnp.int32))

    @pl.when(reads)
    def _():
        send(asked, wanted, wants_sem, want_sem, source)

    greet(Y, step2, lambda k: at(rem(yy + k, Y), z, l))

    def blocks(ref, places):
        found = [ref[:, :B]] * NB
        for b in range(1, SEGB):
            here = ref[:, b * B : (b + 1) * B]
            found = [jnp.where(places[n] == b, here, found[n]) for n in range(NB)]
        return found

    for load in loads[2:]:
        load.wait()
    x_row, p_row = blocks(x, row_at), blocks(p, row_at)
    both = [nn(jnp.concatenate([x_row[n], p_row[n]], 0), h[n]) for n in range(NB)]
    m_x, m_p = (jnp.concatenate([both[n][k : k + K] for n in range(NB)], 1) for k in (0, K))

    @pl.when(reads)
    def _():
        m[...] = m_x
        send(m, m_near, ms_sem, m_sem, source)

    @pl.when(jnp.logical_not(reads))
    def _():
        m_near[...] = m_x

    @pl.when(reads)
    def _():
        done(wanted, want_sem)

    want = wanted[...]
    want_at = [jnp.broadcast_to(want[n : n + 1], (K, B)) for n in range(NB)]
    for i, held in enumerate((x, p)):
        picked = jnp.concatenate(blocks(held, want_at), 1)

        @pl.when(reads)
        def _(i=i, picked=picked):
            pick[i] = picked
            send(pick.at[i], far.at[i], fs_sem.at[i], f_sem.at[i], user(l))

        @pl.when(jnp.logical_not(reads))
        def _(i=i, picked=picked):
            far[i] = picked

    pl.semaphore_wait(step2, Y - 1)
    greet(Z, step3, lambda k: at(yy, rem(z + k, Z), l))

    near_last = (4, 5, 3, 6, 2, 7, 1, 0)

    y_par, y_pair = rem(yy, 2), div(yy, 2)
    slot_a = y_par * L + l
    slot_b = y_pair * Z + z

    def first(i, tile):
        mine[i, 0] = tile
        src, dst = mine.at[i, 0], buf_a.at[i, slot_a]
        for y_k in (1, 0):
            for x_k in (2, 1, 3, 0):
                to = at(2 * y_pair + rem(y_par + y_k, 2), z, 2 * rem(xx + x_k, X) + 1)
                if y_k or x_k:
                    send(src, dst, as_sem.at[i], a_sem.at[i], to)
                else:
                    @pl.when(main)
                    def _():
                        pltpu.make_async_copy(src, dst, a_sem.at[i]).start()

                    @pl.when(aside)
                    def _(to=to):
                        send(src, dst, as_sem.at[i], a_sem.at[i], to)

    def second(i):
        @pl.when(main)
        def _():
            done(buf_a.at[i], a_sem.at[i])
            mine[i, 1] = summed([buf_a[i, s] for s in range(2 * L)])
            src, dst = mine.at[i, 1], buf_b.at[i, slot_b]
            for y_k in (2, 1, 3, 0):
                for z_k in near_last:
                    for core in (0, 1) if i == 2 else (1,):
                        if y_k or z_k or core == 0:
                            to = at(2 * rem(y_pair + y_k, Y // 2) + y_par, rem(z + z_k, Z), 2 * xx + core)
                            send(src, dst, bs_sem.at[i], b_sem.at[i], to)
            pltpu.make_async_copy(src, dst, b_sem.at[i]).start()

    def third(i):
        if i == 2:
            done(buf_b.at[i], b_sem.at[i])
            return summed([buf_b[i, s] for s in range(Z * Y // 2)])

        @pl.when(main)
        def _():
            done(buf_b.at[i], b_sem.at[i])
            whole[i] = summed([buf_b[i, s] for s in range(Z * Y // 2)])
            send(whole.at[i], whole.at[i], ws_sem.at[i], w_sem.at[i], at(yy, z, 2 * xx))

        @pl.when(aside)
        def _():
            done(whole.at[i], w_sem.at[i])

        return whole[i]

    @pl.when(reads)
    def _():
        done(far.at[0], f_sem.at[0])

    xc = far[0]
    direct = [nt(xc[:, n * B : (n + 1) * B], h[n]) for n in range(NB)]

    @pl.when(reads)
    def _():
        done(m_near, m_sem)

    terms = [direct[n] for n in range(NB)] + [m_near[:, n * B : (n + 1) * B] for n in range(NB)]
    for b in range(SEGB):
        total = jnp.zeros((K, B), F32)
        for place, term in zip(row_at + want_at, terms):
            total = total + jnp.where(place == b, term, 0.0)
        d[:, b * B : (b + 1) * B] = total
    pl.semaphore_wait(step3, Z - 1)

    def share(x_at):
        return pl.ds(pl.multiple_of(x_at * OWNED, OWNED), OWNED)

    for k in (2, 1, 3, 0):
        j = rem(xx + k, X)
        src, to = d.at[:, share(j)], at(yy, z, 2 * j + 1)
        if k:
            send(src, got.at[l], ds_sem, d_sem, to)
        else:
            @pl.when(main)
            def _(src=src):
                pltpu.make_async_copy(src, got.at[l], d_sem).start()

            @pl.when(aside)
            def _(src=src, to=to):
                send(src, got.at[l], ds_sem, d_sem, to)

    first(0, folded(nt(m_x, padded(xc)) + nt(xc, padded(m_x))))
    @pl.when(main)
    def _():
        done(got, d_sem)
        part[...] = summed([got[s] for s in range(L)])
        send(part, other, os_sem, o_sem, (r, rem(y_hi + 1, YH) * L + l))

    second(0)

    @pl.when(main)
    def _():
        done(other, o_sem)
        piece[...] = part[...] + other[...]
        mine_of = share(xx)
        for l_to in near_last:
            send(piece, y_far.at[:, mine_of], yfs_sem, yfar_sem, user(l_to))
        for k in near_last[:-1]:
            send(piece, y.at[:, mine_of], ys_sem, y_sem, at(yy, z, rem(l + k, L)))
        pltpu.make_async_copy(piece, y.at[:, mine_of], y_sem).start()

    theta = unfolded(third(0))[:, :K] / ROWS
    own = pl.ds(pl.multiple_of(c * SHARE, SHARE), SHARE)

    @pl.when(main)
    def _():
        width = OWNED // YH
        half = pl.ds(pl.multiple_of(xx * OWNED + y_hi * width, width), width)
        half_of = pl.ds(pl.multiple_of(y_hi * width, width), width)
        residual = piece[:, half_of] - nn(theta, x[:, half])
        basis = jnp.concatenate([residual, x[:, half], p[:, half]], 0)
        products[...] = packed(nt(basis, padded(basis)))

    @pl.when(aside)
    def _():
        products[...] = jnp.zeros_like(products)

    first(1, products[...])
    taken = nn(theta, jnp.concatenate([m_x, xc, x[:, own]], 1))

    @pl.when(reads)
    def _():
        done(far.at[1], f_sem.at[1])

    p_col = far[1]
    done(y, y_sem)
    y_row = blocks(y, row_at)
    m_r = jnp.concatenate([nn(y_row[n], h[n]) for n in range(NB)], 1) - taken[:, : NB * B]

    second(1)
    done(y_far, yfar_sem)
    r_col = jnp.concatenate(blocks(y_far, col_at), 1) - taken[:, NB * B : 2 * NB * B]
    left, right = jnp.concatenate([m_r, m_x, m_p], 0), jnp.concatenate([r_col, xc, p_col], 0)
    first(2, packed(nt(left, padded(right)) + nt(right, padded(left))))
    second(2)
    inverse = inverse_factor(symmetric(unpacked(third(1))) / ROWS)[:, :24]
    q_ref[...] = nn(inverse, jnp.concatenate([y[:, own] - taken[:, 2 * NB * B :], x[:, own], p[:, own]], 0))

    @pl.when(reads)
    def _():
        done(m, ms_sem)
        done(asked, wants_sem)

    @pl.when(reads)
    def _():
        for i in range(2):
            done(pick.at[i], fs_sem.at[i])

    done(got.at[pl.ds(0, X - 1)], ds_sem)
    for i in range(3):
        done(buf_a.at[i, pl.ds(0, L - 1)], as_sem.at[i])

    @pl.when(aside)
    def _():
        done(got.at[0], ds_sem)
        for i in range(3):
            done(buf_a.at[i, 0], as_sem.at[i])

    @pl.when(main)
    def _():
        done(part, os_sem)
        done(got, yfs_sem)
        done(got.at[pl.ds(0, L - 1)], ys_sem)
        for i in range(2):
            done(buf_b.at[i, pl.ds(0, Z * Y // 2 - 1)], bs_sem.at[i])
            done(whole.at[i], ws_sem.at[i])

    half_way = nn(inverse, unpacked(third(2))[:, :24] / ROWS)
    ray_ref[...] = nt(half_way, inverse) + nt(inverse, half_way)

    @pl.when(main)
    def _():
        done(buf_b.at[2], bs_sem.at[2])
        done(buf_b.at[2, pl.ds(0, Z * Y // 2 - 1)], bs_sem.at[2])


def body(hamiltonian_blocks, block_rows, block_cols, current_states, previous_steps):
    vmem, anywhere = (pl.BlockSpec(memory_space=s) for s in (pltpu.VMEM, pl.ANY))
    dma, regular = pltpu.SemaphoreType.DMA, pltpu.SemaphoreType.REGULAR
    return pl.pallas_call(
        kernel,
        out_shape=(jax.ShapeDtypeStruct((3 * K, SHARE), F32), jax.ShapeDtypeStruct((3 * K, 3 * K), F32)),
        in_specs=[anywhere, anywhere, anywhere, anywhere, anywhere],
        out_specs=(vmem, vmem),
        scratch_shapes=[
            pltpu.SMEM((NB,), jnp.int32),
            pltpu.SMEM((NB,), jnp.int32),
            pltpu.VMEM((NB, B, B), F32),
            pltpu.VMEM((K, SEG), F32),
            pltpu.VMEM((K, SEG), F32),
            pltpu.VMEM((2, K, NB * B), F32),
            pltpu.VMEM((2, K, NB * B), F32),
            pltpu.VMEM((8, B), jnp.int32),
            pltpu.VMEM((8, B), jnp.int32),
            pltpu.VMEM((K, NB * B), F32),
            pltpu.VMEM((K, NB * B), F32),
            pltpu.VMEM((K, SEG), F32),
            pltpu.VMEM((L, K, OWNED), F32),
            pltpu.VMEM((K, OWNED), F32),
            pltpu.VMEM((K, OWNED), F32),
            pltpu.VMEM((K, OWNED), F32),
            pltpu.VMEM((4, B), F32),
            pltpu.VMEM((K, SEG), F32),
            pltpu.VMEM((K, SEG), F32),
            pltpu.VMEM((3, 2, 4, B), F32),
            pltpu.VMEM((3, 2 * L, 4, B), F32),
            pltpu.VMEM((3, Z * Y // 2, 4, B), F32),
            pltpu.VMEM((2, 4, B), F32),
            dma((5,)), dma, dma, dma, dma, dma((2,)), dma((2,)), dma, dma, dma, dma,
            dma, dma, dma, dma, dma((3,)), dma((3,)), dma((2,)), dma((3,)), dma((3,)), dma((2,)), regular, regular,
        ],
        compiler_params=pltpu.CompilerParams(collective_id=0, has_side_effects=True, vmem_limit_bytes=56426496),
        name="lobpcg_step",
    )(block_rows.reshape(NB), block_cols.reshape(NB), hamiltonian_blocks.reshape(NB, B, B), current_states, previous_steps)


def solution(mesh):
    return jax.shard_map(
        body,
        mesh=mesh,
        in_specs=(
            P("row", "col", None, None, None),
            P("row", "col", None),
            P("row", "col", None),
            P(None, "row"),
            P(None, "row"),
        ),
        out_specs=(P(None, ("row", "col")), P()),
        check_vma=False,
    )
```

```python
import functools

import jax
import jax.numpy as jnp
from jax import lax
from jax.experimental import pallas as pl
from jax.experimental.pallas import tpu as pltpu
from jax.sharding import PartitionSpec as P

MESH = pl.DeviceIdType.MESH
F32 = jnp.float32
exactness = lax.Precision.HIGHEST

Z, YL, YH, L = 8, 4, 2, 8
Y = YL * YH
N_ROW, N_COL = Z * YL, L * YH
K, B, SEGB, NB = 8, 128, 32, 4
SEG = SEGB * B
X = L // 2
SHARE, OWNED = SEG // N_COL, SEG // X
ROWS = N_ROW * SEG
rem, div = lax.rem, lax.div


def nn(a, b):
    return jnp.dot(a, b, precision=exactness, preferred_element_type=F32)


def nt(a, b):
    return lax.dot_general(a, b, (((1,), (1,)), ((), ())), precision=exactness, preferred_element_type=F32)


def lane_ids(shape):
    return lax.broadcasted_iota(jnp.int32, shape, 1)


def row_ids(shape):
    return lax.broadcasted_iota(jnp.int32, shape, 0)


def padded(a):
    return jnp.concatenate([a, jnp.zeros((B - a.shape[0], a.shape[1]), F32)], 0)


def summed(terms):
    while len(terms) > 1:
        terms = [sum(terms[i + 1 : i + 2], terms[i]) for i in range(0, len(terms), 2)]
    return terms[0]


def folded(t):
    return t[0:4] + pltpu.roll(t[4:8], 64, 1)


def unfolded(t):
    t = jnp.concatenate([t, pltpu.roll(t, 64, 1)], 0)
    return jnp.where(lane_ids(t.shape) < 64, t, 0.0)


def between(a, low, high):
    lanes = lane_ids(a.shape)
    return jnp.where(jnp.logical_and(lanes >= low, lanes < high), a, 0.0)


def packed(a):
    return folded(between(a[0:8], 0, 24) + pltpu.roll(between(a[8:16], 8, 24), 16, 1) + pltpu.roll(between(a[16:24], 16, 24), 24, 1))


def unpacked(t):
    t = unfolded(t)
    a = jnp.concatenate([between(t, 0, 24), between(pltpu.roll(t, 112, 1), 8, 24), between(pltpu.roll(t, 104, 1), 16, 24)], 0)
    same = lax.shift_right_logical(lane_ids(a.shape), 3) == lax.shift_right_logical(row_ids(a.shape), 3)
    return jnp.where(same, 0.5 * a, a)


def symmetric(a):
    unit = (lane_ids((24, B)) == row_ids((24, B))).astype(F32)
    return a + nt(unit, padded(a))


def inverse_factor(gram):
    rows, lanes = row_ids(gram.shape), lane_ids(gram.shape)
    left = gram
    right = (rows == lanes).astype(F32)
    for j in range(24):
        pivot = left[j : j + 1, j : j + 1]
        factor = jnp.where(rows[:, :1] > j, left[:, j : j + 1] / pivot, 0.0)
        top, unit = left[j : j + 1], right[j : j + 1]
        left = left - factor * top
        right = right - factor * unit
    diagonal = jnp.sum(jnp.where(rows == lanes, left, 0.0), 1, keepdims=True)
    return right / jnp.sqrt(diagonal)


def kernel(rows_ref, cols_ref, h_ref, x_ref, p_ref, q_ref, ray_ref,
           rows, cols, h, x, p, pick, far, asked, wanted, m, m_near, d, got, part, other, piece, products, y, y_far, mine,
           buf_a, buf_b, whole, load_sem, m_sem, ms_sem, want_sem, wants_sem, f_sem, fs_sem, d_sem, ds_sem, o_sem, os_sem,
           y_sem, ys_sem, yfar_sem, yfs_sem, a_sem, b_sem, w_sem, as_sem, bs_sem, ws_sem, step2, step3):
    r, c = lax.axis_index("row"), lax.axis_index("col")
    z, y_lo, l, y_hi = rem(r, Z), div(r, Z), rem(c, L), div(c, L)
    yy = y_hi * YL + y_lo
    xx = div(l, 2)
    main = rem(l, 2) == 1
    aside = jnp.logical_not(main)

    def at(y_at, z_at, l_at):
        return (rem(y_at, YL) * Z + z_at, div(y_at, YL) * L + l_at)

    def send(src, dst, ss, rs, dev):
        pltpu.make_async_remote_copy(src_ref=src, dst_ref=dst, send_sem=ss, recv_sem=rs,
                                     device_id=dev, device_id_type=MESH).start()

    def done(ref, sem):
        pltpu.make_async_copy(ref, ref, sem).wait()

    loads = [pltpu.make_async_copy(src, dst, load_sem.at[i]) for i, (src, dst) in enumerate(
        ((rows_ref, rows), (cols_ref, cols), (x_ref, x), (h_ref, h), (p_ref, p)))]
    for load in loads[:2]:
        load.start()

    reads = c != 0
    q = rem(r + c, N_ROW)
    turned = jnp.logical_and(div(q, Z) == 0, z + l >= Z).astype(jnp.int32)
    source = (q, rem(y_hi + turned, YH) * L + l)

    def user(l_at):
        over = jnp.logical_and(y_lo == 0, z < l_at).astype(jnp.int32)
        to = rem(y_hi + over, YH) * L + l_at
        return rem(r + N_ROW - to, N_ROW), to

    barrier = pltpu.get_barrier_semaphore()

    @pl.when(reads)
    def _():
        pl.semaphore_signal(barrier, inc=1, device_id=source, device_id_type=MESH)
        pl.semaphore_signal(barrier, inc=1, device_id=user(l), device_id_type=MESH)

    for load in loads[2:]:
        load.start()

    def greet(n, sem, place):
        for k in range(1, n):
            pl.semaphore_signal(sem, inc=1, device_id=place(k), device_id_type=MESH)

    greet(Z, barrier, lambda k: at(yy, rem(z + k, Z), l))
    greet(Y, barrier, lambda k: at(rem(yy + k, Y), z, l))
    greet(L, barrier, lambda k: at(yy, z, rem(l + k, L)))

    for load in loads[:2]:
        load.wait()
    row_at = [jnp.full((K, B), rows[n], jnp.int32) for n in range(NB)]
    col_at = [jnp.full((K, B), cols[n], jnp.int32) for n in range(NB)]
    asks = jnp.zeros((8, B), jnp.int32)
    for n in range(NB):
        asks = jnp.where(row_ids((8, B)) == n, col_at[n], asks)
    asked[...] = asks

    @pl.when(jnp.logical_not(reads))
    def _():
        wanted[...] = asks

    pl.semaphore_wait(barrier, Z - 1 + Y - 1 + L - 1 + 2 * reads.astype(jnp.int32))

    @pl.when(reads)
    def _():
        send(asked, wanted, wants_sem, want_sem, source)

    greet(Y, step2, lambda k: at(rem(yy + k, Y), z, l))

    def blocks(ref, places):
        found = [ref[:, :B]] * NB
        for b in range(1, SEGB):
            here = ref[:, b * B : (b + 1) * B]
            found = [jnp.where(places[n] == b, here, found[n]) for n in range(NB)]
        return found

    for load in loads[2:]:
        load.wait()
    x_row, p_row = blocks(x, row_at), blocks(p, row_at)
    both = [nn(jnp.concatenate([x_row[n], p_row[n]], 0), h[n]) for n in range(NB)]
    m_x, m_p = (jnp.concatenate([both[n][k : k + K] for n in range(NB)], 1) for k in (0, K))

    @pl.when(reads)
    def _():
        m[...] = m_x
        send(m, m_near, ms_sem, m_sem, source)

    @pl.when(jnp.logical_not(reads))
    def _():
        m_near[...] = m_x

    @pl.when(reads)
    def _():
        done(wanted, want_sem)

    want = wanted[...]
    want_at = [jnp.broadcast_to(want[n : n + 1], (K, B)) for n in range(NB)]
    for i, held in enumerate((x, p)):
        picked = jnp.concatenate(blocks(held, want_at), 1)

        @pl.when(reads)
        def _(i=i, picked=picked):
            pick[i] = picked
            send(pick.at[i], far.at[i], fs_sem.at[i], f_sem.at[i], user(l))

        @pl.when(jnp.logical_not(reads))
        def _(i=i, picked=picked):
            far[i] = picked

    pl.semaphore_wait(step2, Y - 1)
    greet(Z, step3, lambda k: at(yy, rem(z + k, Z), l))

    near_last = (4, 5, 3, 6, 2, 7, 1, 0)

    y_par, y_pair = rem(yy, 2), div(yy, 2)
    slot_a = y_par * L + l
    slot_b = y_pair * Z + z

    def first(i, tile):
        mine[i, 0] = tile
        src, dst = mine.at[i, 0], buf_a.at[i, slot_a]
        for y_k in (1, 0):
            for x_k in (2, 1, 3, 0):
                to = at(2 * y_pair + rem(y_par + y_k, 2), z, 2 * rem(xx + x_k, X) + 1)
                if y_k or x_k:
                    send(src, dst, as_sem.at[i], a_sem.at[i], to)
                else:
                    @pl.when(main)
                    def _():
                        pltpu.make_async_copy(src, dst, a_sem.at[i]).start()

                    @pl.when(aside)
                    def _(to=to):
                        send(src, dst, as_sem.at[i], a_sem.at[i], to)

    def second(i):
        @pl.when(main)
        def _():
            done(buf_a.at[i], a_sem.at[i])
            mine[i, 1] = summed([buf_a[i, s] for s in range(2 * L)])
            src, dst = mine.at[i, 1], buf_b.at[i, slot_b]
            for y_k in (2, 1, 3, 0):
                for z_k in near_last:
                    for core in (0, 1) if i == 2 else (1,):
                        if y_k or z_k or core == 0:
                            to = at(2 * rem(y_pair + y_k, Y // 2) + y_par, rem(z + z_k, Z), 2 * xx + core)
                            send(src, dst, bs_sem.at[i], b_sem.at[i], to)
            pltpu.make_async_copy(src, dst, b_sem.at[i]).start()

    def third(i):
        if i == 2:
            done(buf_b.at[i], b_sem.at[i])
            return summed([buf_b[i, s] for s in range(Z * Y // 2)])

        @pl.when(main)
        def _():
            done(buf_b.at[i], b_sem.at[i])
            whole[i] = summed([buf_b[i, s] for s in range(Z * Y // 2)])
            send(whole.at[i], whole.at[i], ws_sem.at[i], w_sem.at[i], at(yy, z, 2 * xx))

        @pl.when(aside)
        def _():
            done(whole.at[i], w_sem.at[i])

        return whole[i]

    @pl.when(reads)
    def _():
        done(far.at[0], f_sem.at[0])

    xc = far[0]
    direct = [nt(xc[:, n * B : (n + 1) * B], h[n]) for n in range(NB)]
    cross = folded(nt(m_x, padded(xc)) + nt(xc, padded(m_x)))

    @pl.when(reads)
    def _():
        done(m_near, m_sem)

    terms = [direct[n] for n in range(NB)] + [m_near[:, n * B : (n + 1) * B] for n in range(NB)]
    for b in range(SEGB):
        total = jnp.zeros((K, B), F32)
        for place, term in zip(row_at + want_at, terms):
            total = total + jnp.where(place == b, term, 0.0)
        d[:, b * B : (b + 1) * B] = total
    pl.semaphore_wait(step3, Z - 1)

    def share(x_at):
        return pl.ds(pl.multiple_of(x_at * OWNED, OWNED), OWNED)

    for k in (2, 1, 3, 0):
        j = rem(xx + k, X)
        src, to = d.at[:, share(j)], at(yy, z, 2 * j + 1)
        if k:
            send(src, got.at[l], ds_sem, d_sem, to)
        else:
            @pl.when(main)
            def _(src=src):
                pltpu.make_async_copy(src, got.at[l], d_sem).start()

            @pl.when(aside)
            def _(src=src, to=to):
                send(src, got.at[l], ds_sem, d_sem, to)

    first(0, cross)
    @pl.when(main)
    def _():
        done(got, d_sem)
        part[...] = summed([got[s] for s in range(L)])
        send(part, other, os_sem, o_sem, (r, rem(y_hi + 1, YH) * L + l))

    second(0)

    @pl.when(main)
    def _():
        done(other, o_sem)
        piece[...] = part[...] + other[...]
        mine_of = share(xx)
        for l_to in near_last:
            send(piece, y_far.at[:, mine_of], yfs_sem, yfar_sem, user(l_to))
        for k in near_last[:-1]:
            send(piece, y.at[:, mine_of], ys_sem, y_sem, at(yy, z, rem(l + k, L)))
        pltpu.make_async_copy(piece, y.at[:, mine_of], y_sem).start()

    theta = unfolded(third(0))[:, :K] / ROWS
    own = pl.ds(pl.multiple_of(c * SHARE, SHARE), SHARE)

    @pl.when(main)
    def _():
        width = OWNED // YH
        half = pl.ds(pl.multiple_of(xx * OWNED + y_hi * width, width), width)
        half_of = pl.ds(pl.multiple_of(y_hi * width, width), width)
        residual = piece[:, half_of] - nn(theta, x[:, half])
        basis = jnp.concatenate([residual, x[:, half], p[:, half]], 0)
        products[...] = packed(nt(basis, padded(basis)))

    @pl.when(aside)
    def _():
        products[...] = jnp.zeros_like(products)

    first(1, products[...])
    taken = nn(theta, jnp.concatenate([m_x, xc, x[:, own]], 1))

    @pl.when(reads)
    def _():
        done(far.at[1], f_sem.at[1])

    p_col = far[1]
    done(y, y_sem)
    y_row = blocks(y, row_at)
    m_r = jnp.concatenate([nn(y_row[n], h[n]) for n in range(NB)], 1) - taken[:, : NB * B]

    done(y_far, yfar_sem)
    r_col = jnp.concatenate(blocks(y_far, col_at), 1) - taken[:, NB * B : 2 * NB * B]
    left, right = jnp.concatenate([m_r, m_x, m_p], 0), jnp.concatenate([r_col, xc, p_col], 0)
    first(2, packed(nt(left, padded(right)) + nt(right, padded(left))))
    second(1)
    second(2)
    inverse = inverse_factor(symmetric(unpacked(third(1))) / ROWS)[:, :24]
    q_ref[...] = nn(inverse, jnp.concatenate([y[:, own] - taken[:, 2 * NB * B :], x[:, own], p[:, own]], 0))

    @pl.when(reads)
    def _():
        done(m, ms_sem)
        done(asked, wants_sem)

    @pl.when(reads)
    def _():
        for i in range(2):
            done(pick.at[i], fs_sem.at[i])

    done(got.at[pl.ds(0, X - 1)], ds_sem)
    for i in range(3):
        done(buf_a.at[i, pl.ds(0, L - 1)], as_sem.at[i])

    @pl.when(aside)
    def _():
        done(got.at[0], ds_sem)
        for i in range(3):
            done(buf_a.at[i, 0], as_sem.at[i])

    @pl.when(main)
    def _():
        done(part, os_sem)
        done(got, yfs_sem)
        done(got.at[pl.ds(0, L - 1)], ys_sem)
        for i in range(2):
            done(buf_b.at[i, pl.ds(0, Z * Y // 2 - 1)], bs_sem.at[i])
            done(whole.at[i], ws_sem.at[i])

    half_way = nn(inverse, unpacked(third(2))[:, :24] / ROWS)
    ray_ref[...] = nt(half_way, inverse) + nt(inverse, half_way)

    @pl.when(main)
    def _():
        done(buf_b.at[2], bs_sem.at[2])
        done(buf_b.at[2, pl.ds(0, Z * Y // 2 - 1)], bs_sem.at[2])


def body(hamiltonian_blocks, block_rows, block_cols, current_states, previous_steps):
    vmem, anywhere = (pl.BlockSpec(memory_space=s) for s in (pltpu.VMEM, pl.ANY))
    dma, regular = pltpu.SemaphoreType.DMA, pltpu.SemaphoreType.REGULAR
    return pl.pallas_call(
        kernel,
        out_shape=(jax.ShapeDtypeStruct((3 * K, SHARE), F32), jax.ShapeDtypeStruct((3 * K, 3 * K), F32)),
        in_specs=[anywhere, anywhere, anywhere, anywhere, anywhere],
        out_specs=(vmem, vmem),
        scratch_shapes=[
            pltpu.SMEM((NB,), jnp.int32),
            pltpu.SMEM((NB,), jnp.int32),
            pltpu.VMEM((NB, B, B), F32),
            pltpu.VMEM((K, SEG), F32),
            pltpu.VMEM((K, SEG), F32),
            pltpu.VMEM((2, K, NB * B), F32),
            pltpu.VMEM((2, K, NB * B), F32),
            pltpu.VMEM((8, B), jnp.int32),
            pltpu.VMEM((8, B), jnp.int32),
            pltpu.VMEM((K, NB * B), F32),
            pltpu.VMEM((K, NB * B), F32),
            pltpu.VMEM((K, SEG), F32),
            pltpu.VMEM((L, K, OWNED), F32),
            pltpu.VMEM((K, OWNED), F32),
            pltpu.VMEM((K, OWNED), F32),
            pltpu.VMEM((K, OWNED), F32),
            pltpu.VMEM((4, B), F32),
            pltpu.VMEM((K, SEG), F32),
            pltpu.VMEM((K, SEG), F32),
            pltpu.VMEM((3, 2, 4, B), F32),
            pltpu.VMEM((3, 2 * L, 4, B), F32),
            pltpu.VMEM((3, Z * Y // 2, 4, B), F32),
            pltpu.VMEM((2, 4, B), F32),
            dma((5,)), dma, dma, dma, dma, dma((2,)), dma((2,)), dma, dma, dma, dma,
            dma, dma, dma, dma, dma((3,)), dma((3,)), dma((2,)), dma((3,)), dma((3,)), dma((2,)), regular, regular,
        ],
        compiler_params=pltpu.CompilerParams(collective_id=0, has_side_effects=True, vmem_limit_bytes=56426496),
        name="lobpcg_step",
    )(block_rows.reshape(NB), block_cols.reshape(NB), hamiltonian_blocks.reshape(NB, B, B), current_states, previous_steps)


def solution(mesh):
    return jax.shard_map(
        body,
        mesh=mesh,
        in_specs=(
            P("row", "col", None, None, None),
            P("row", "col", None),
            P("row", "col", None),
            P(None, "row"),
            P(None, "row"),
        ),
        out_specs=(P(None, ("row", "col")), P()),
        check_vma=False,
    )
```

```python
import functools

import jax
import jax.numpy as jnp
from jax import lax
from jax.experimental import pallas as pl
from jax.experimental.pallas import tpu as pltpu
from jax.sharding import PartitionSpec as P

MESH = pl.DeviceIdType.MESH
F32 = jnp.float32
exactness = lax.Precision.HIGHEST

Z, YL, YH, L = 8, 4, 2, 8
Y = YL * YH
N_ROW, N_COL = Z * YL, L * YH
K, B, SEGB, NB = 8, 128, 32, 4
SEG = SEGB * B
X = L // 2
SHARE, OWNED = SEG // N_COL, SEG // X
ROWS = N_ROW * SEG
rem, div = lax.rem, lax.div


def nn(a, b):
    return jnp.dot(a, b, precision=exactness, preferred_element_type=F32)


def nt(a, b):
    return lax.dot_general(a, b, (((1,), (1,)), ((), ())), precision=exactness, preferred_element_type=F32)


def lane_ids(shape):
    return lax.broadcasted_iota(jnp.int32, shape, 1)


def row_ids(shape):
    return lax.broadcasted_iota(jnp.int32, shape, 0)


def padded(a):
    return jnp.concatenate([a, jnp.zeros((B - a.shape[0], a.shape[1]), F32)], 0)


def summed(terms):
    while len(terms) > 1:
        terms = [sum(terms[i + 1 : i + 2], terms[i]) for i in range(0, len(terms), 2)]
    return terms[0]


def folded(t):
    return t[0:4] + pltpu.roll(t[4:8], 64, 1)


def unfolded(t):
    t = jnp.concatenate([t, pltpu.roll(t, 64, 1)], 0)
    return jnp.where(lane_ids(t.shape) < 64, t, 0.0)


def between(a, low, high):
    lanes = lane_ids(a.shape)
    return jnp.where(jnp.logical_and(lanes >= low, lanes < high), a, 0.0)


def packed(a):
    return folded(between(a[0:8], 0, 24) + pltpu.roll(between(a[8:16], 8, 24), 16, 1) + pltpu.roll(between(a[16:24], 16, 24), 24, 1))


def unpacked(t):
    t = unfolded(t)
    a = jnp.concatenate([between(t, 0, 24), between(pltpu.roll(t, 112, 1), 8, 24), between(pltpu.roll(t, 104, 1), 16, 24)], 0)
    same = lax.shift_right_logical(lane_ids(a.shape), 3) == lax.shift_right_logical(row_ids(a.shape), 3)
    return jnp.where(same, 0.5 * a, a)


def symmetric(a):
    unit = (lane_ids((24, B)) == row_ids((24, B))).astype(F32)
    return a + nt(unit, padded(a))


def inverse_factor(gram):
    rows, lanes = row_ids(gram.shape), lane_ids(gram.shape)
    left = gram
    right = (rows == lanes).astype(F32)
    for j in range(24):
        pivot = left[j : j + 1, j : j + 1]
        factor = jnp.where(rows[:, :1] > j, left[:, j : j + 1] / pivot, 0.0)
        top, unit = left[j : j + 1], right[j : j + 1]
        left = left - factor * top
        right = right - factor * unit
    diagonal = jnp.sum(jnp.where(rows == lanes, left, 0.0), 1, keepdims=True)
    return right / jnp.sqrt(diagonal)


def kernel(rows_ref, cols_ref, h_ref, x_ref, p_ref, q_ref, ray_ref,
           rows, cols, h, x, p, pick, far, asked, wanted, m, m_near, d, got, part, other, piece, y, y_far, mine,
           buf_a, buf_b, whole, load_sem, m_sem, ms_sem, want_sem, wants_sem, f_sem, fs_sem, d_sem, ds_sem, o_sem, os_sem,
           y_sem, ys_sem, yfar_sem, yfs_sem, a_sem, b_sem, w_sem, as_sem, bs_sem, ws_sem, step2, step3):
    r, c = lax.axis_index("row"), lax.axis_index("col")
    z, y_lo, l, y_hi = rem(r, Z), div(r, Z), rem(c, L), div(c, L)
    yy = y_hi * YL + y_lo
    xx = div(l, 2)
    main = rem(l, 2) == 1
    aside = jnp.logical_not(main)

    def at(y_at, z_at, l_at):
        return (rem(y_at, YL) * Z + z_at, div(y_at, YL) * L + l_at)

    def send(src, dst, ss, rs, dev):
        pltpu.make_async_remote_copy(src_ref=src, dst_ref=dst, send_sem=ss, recv_sem=rs,
                                     device_id=dev, device_id_type=MESH).start()

    def done(ref, sem):
        pltpu.make_async_copy(ref, ref, sem).wait()

    loads = [pltpu.make_async_copy(src, dst, load_sem.at[i]) for i, (src, dst) in enumerate(
        ((rows_ref, rows), (cols_ref, cols), (x_ref, x), (h_ref, h), (p_ref, p)))]
    for load in loads[:2]:
        load.start()

    reads = c != 0
    q = rem(r + c, N_ROW)
    turned = jnp.logical_and(div(q, Z) == 0, z + l >= Z).astype(jnp.int32)
    source = (q, rem(y_hi + turned, YH) * L + l)

    def user(l_at):
        over = jnp.logical_and(y_lo == 0, z < l_at).astype(jnp.int32)
        to = rem(y_hi + over, YH) * L + l_at
        return rem(r + N_ROW - to, N_ROW), to

    barrier = pltpu.get_barrier_semaphore()

    @pl.when(reads)
    def _():
        pl.semaphore_signal(barrier, inc=1, device_id=source, device_id_type=MESH)
        pl.semaphore_signal(barrier, inc=1, device_id=user(l), device_id_type=MESH)

    for load in loads[2:]:
        load.start()

    def greet(n, sem, place):
        for k in range(1, n):
            pl.semaphore_signal(sem, inc=1, device_id=place(k), device_id_type=MESH)

    greet(Z, barrier, lambda k: at(yy, rem(z + k, Z), l))
    greet(Y, barrier, lambda k: at(rem(yy + k, Y), z, l))
    greet(L, barrier, lambda k: at(yy, z, rem(l + k, L)))

    for load in loads[:2]:
        load.wait()
    row_at = [jnp.full((K, B), rows[n], jnp.int32) for n in range(NB)]
    col_at = [jnp.full((K, B), cols[n], jnp.int32) for n in range(NB)]
    asks = jnp.zeros((8, B), jnp.int32)
    for n in range(NB):
        asks = jnp.where(row_ids((8, B)) == n, col_at[n], asks)
    asked[...] = asks

    @pl.when(jnp.logical_not(reads))
    def _():
        wanted[...] = asks

    pl.semaphore_wait(barrier, Z - 1 + Y - 1 + L - 1 + 2 * reads.astype(jnp.int32))

    @pl.when(reads)
    def _():
        send(asked, wanted, wants_sem, want_sem, source)

    greet(Y, step2, lambda k: at(rem(yy + k, Y), z, l))

    def blocks(ref, places):
        found = [ref[:, :B]] * NB
        for b in range(1, SEGB):
            here = ref[:, b * B : (b + 1) * B]
            found = [jnp.where(places[n] == b, here, found[n]) for n in range(NB)]
        return found

    for load in loads[2:]:
        load.wait()
    x_row, p_row = blocks(x, row_at), blocks(p, row_at)
    both = [nn(jnp.concatenate([x_row[n], p_row[n]], 0), h[n]) for n in range(NB)]
    m_x, m_p = (jnp.concatenate([both[n][k : k + K] for n in range(NB)], 1) for k in (0, K))

    @pl.when(reads)
    def _():
        m[...] = m_x
        send(m, m_near, ms_sem, m_sem, source)

    @pl.when(jnp.logical_not(reads))
    def _():
        m_near[...] = m_x

    @pl.when(reads)
    def _():
        done(wanted, want_sem)

    want = wanted[...]
    want_at = [jnp.broadcast_to(want[n : n + 1], (K, B)) for n in range(NB)]
    for i, held in enumerate((x, p)):
        picked = jnp.concatenate(blocks(held, want_at), 1)

        @pl.when(reads)
        def _(i=i, picked=picked):
            pick[i] = picked
            send(pick.at[i], far.at[i], fs_sem.at[i], f_sem.at[i], user(l))

        @pl.when(jnp.logical_not(reads))
        def _(i=i, picked=picked):
            far[i] = picked

    pl.semaphore_wait(step2, Y - 1)
    greet(Z, step3, lambda k: at(yy, rem(z + k, Z), l))

    near_last = (4, 5, 3, 6, 2, 7, 1, 0)

    y_par, y_pair = rem(yy, 2), div(yy, 2)
    slot_a = y_par * L + l
    slot_b = y_pair * Z + z

    def first(i, tile):
        mine[i, 0] = tile
        src, dst = mine.at[i, 0], buf_a.at[i, y_par * X + xx if i == 1 else slot_a]
        for y_k in (1, 0):
            for x_k in (2, 1, 3, 0):
                to = at(2 * y_pair + rem(y_par + y_k, 2), z, 2 * rem(xx + x_k, X) + 1)
                if y_k or x_k:
                    send(src, dst, as_sem.at[i], a_sem.at[i], to)
                else:
                    @pl.when(main)
                    def _():
                        pltpu.make_async_copy(src, dst, a_sem.at[i]).start()

                    @pl.when(aside)
                    def _(to=to):
                        send(src, dst, as_sem.at[i], a_sem.at[i], to)

    def second(i):
        @pl.when(main)
        def _():
            members = L if i == 1 else 2 * L
            done(buf_a.at[i, pl.ds(0, members)], a_sem.at[i])
            mine[i, 1] = summed([buf_a[i, s] for s in range(members)])
            src, dst = mine.at[i, 1], buf_b.at[i, slot_b]
            for y_k in (2, 1, 3, 0):
                for z_k in near_last:
                    for core in (0, 1) if i == 2 else (1,):
                        if y_k or z_k or core == 0:
                            to = at(2 * rem(y_pair + y_k, Y // 2) + y_par, rem(z + z_k, Z), 2 * xx + core)
                            send(src, dst, bs_sem.at[i], b_sem.at[i], to)
            pltpu.make_async_copy(src, dst, b_sem.at[i]).start()

    def third(i):
        if i == 2:
            done(buf_b.at[i], b_sem.at[i])
            return summed([buf_b[i, s] for s in range(Z * Y // 2)])

        @pl.when(main)
        def _():
            done(buf_b.at[i], b_sem.at[i])
            whole[i] = summed([buf_b[i, s] for s in range(Z * Y // 2)])
            send(whole.at[i], whole.at[i], ws_sem.at[i], w_sem.at[i], at(yy, z, 2 * xx))

        @pl.when(aside)
        def _():
            done(whole.at[i], w_sem.at[i])

        return whole[i]

    @pl.when(reads)
    def _():
        done(far.at[0], f_sem.at[0])

    xc = far[0]
    direct = [nt(xc[:, n * B : (n + 1) * B], h[n]) for n in range(NB)]
    cross = folded(nt(m_x, padded(xc)) + nt(xc, padded(m_x)))

    @pl.when(reads)
    def _():
        done(m_near, m_sem)

    terms = [direct[n] for n in range(NB)] + [m_near[:, n * B : (n + 1) * B] for n in range(NB)]
    for b in range(SEGB):
        total = jnp.zeros((K, B), F32)
        for place, term in zip(row_at + want_at, terms):
            total = total + jnp.where(place == b, term, 0.0)
        d[:, b * B : (b + 1) * B] = total
    pl.semaphore_wait(step3, Z - 1)

    def share(x_at):
        return pl.ds(pl.multiple_of(x_at * OWNED, OWNED), OWNED)

    for k in (2, 1, 3, 0):
        j = rem(xx + k, X)
        src, to = d.at[:, share(j)], at(yy, z, 2 * j + 1)
        if k:
            send(src, got.at[l], ds_sem, d_sem, to)
        else:
            @pl.when(main)
            def _(src=src):
                pltpu.make_async_copy(src, got.at[l], d_sem).start()

            @pl.when(aside)
            def _(src=src, to=to):
                send(src, got.at[l], ds_sem, d_sem, to)

    first(0, cross)
    @pl.when(main)
    def _():
        done(got, d_sem)
        part[...] = summed([got[s] for s in range(L)])
        send(part, other, os_sem, o_sem, (r, rem(y_hi + 1, YH) * L + l))

    second(0)

    @pl.when(main)
    def _():
        done(other, o_sem)
        piece[...] = part[...] + other[...]
        mine_of = share(xx)
        for l_to in near_last:
            send(piece, y_far.at[:, mine_of], yfs_sem, yfar_sem, user(l_to))
        for k in near_last[:-1]:
            send(piece, y.at[:, mine_of], ys_sem, y_sem, at(yy, z, rem(l + k, L)))
        pltpu.make_async_copy(piece, y.at[:, mine_of], y_sem).start()

    theta = unfolded(third(0))[:, :K] / ROWS
    own = pl.ds(pl.multiple_of(c * SHARE, SHARE), SHARE)

    @pl.when(main)
    def _():
        width = OWNED // YH
        half = pl.ds(pl.multiple_of(xx * OWNED + y_hi * width, width), width)
        half_of = pl.ds(pl.multiple_of(y_hi * width, width), width)
        residual = piece[:, half_of] - nn(theta, x[:, half])
        basis = jnp.concatenate([residual, x[:, half], p[:, half]], 0)
        first(1, packed(nt(basis, padded(basis))))

    taken = nn(theta, jnp.concatenate([m_x, xc, x[:, own]], 1))

    @pl.when(reads)
    def _():
        done(far.at[1], f_sem.at[1])

    p_col = far[1]
    done(y, y_sem)
    y_row = blocks(y, row_at)
    m_r = jnp.concatenate([nn(y_row[n], h[n]) for n in range(NB)], 1) - taken[:, : NB * B]

    done(y_far, yfar_sem)
    r_col = jnp.concatenate(blocks(y_far, col_at), 1) - taken[:, NB * B : 2 * NB * B]
    left, right = jnp.concatenate([m_r, m_x, m_p], 0), jnp.concatenate([r_col, xc, p_col], 0)
    first(2, packed(nt(left, padded(right)) + nt(right, padded(left))))
    second(1)
    second(2)
    inverse = inverse_factor(symmetric(unpacked(third(1))) / ROWS)[:, :24]
    q_ref[...] = nn(inverse, jnp.concatenate([y[:, own] - taken[:, 2 * NB * B :], x[:, own], p[:, own]], 0))

    @pl.when(reads)
    def _():
        done(m, ms_sem)
        done(asked, wants_sem)

    @pl.when(reads)
    def _():
        for i in range(2):
            done(pick.at[i], fs_sem.at[i])

    done(got.at[pl.ds(0, X - 1)], ds_sem)
    for i in (0, 2):
        done(buf_a.at[i, pl.ds(0, L - 1)], as_sem.at[i])

    @pl.when(aside)
    def _():
        done(got.at[0], ds_sem)
        for i in (0, 2):
            done(buf_a.at[i, 0], as_sem.at[i])

    @pl.when(main)
    def _():
        done(part, os_sem)
        done(buf_a.at[1, pl.ds(0, L - 1)], as_sem.at[1])
        done(got, yfs_sem)
        done(got.at[pl.ds(0, L - 1)], ys_sem)
        for i in range(2):
            done(buf_b.at[i, pl.ds(0, Z * Y // 2 - 1)], bs_sem.at[i])
            done(whole.at[i], ws_sem.at[i])

    half_way = nn(inverse, unpacked(third(2))[:, :24] / ROWS)
    ray_ref[...] = nt(half_way, inverse) + nt(inverse, half_way)

    @pl.when(main)
    def _():
        done(buf_b.at[2], bs_sem.at[2])
        done(buf_b.at[2, pl.ds(0, Z * Y // 2 - 1)], bs_sem.at[2])


def body(hamiltonian_blocks, block_rows, block_cols, current_states, previous_steps):
    vmem, anywhere = (pl.BlockSpec(memory_space=s) for s in (pltpu.VMEM, pl.ANY))
    dma, regular = pltpu.SemaphoreType.DMA, pltpu.SemaphoreType.REGULAR
    return pl.pallas_call(
        kernel,
        out_shape=(jax.ShapeDtypeStruct((3 * K, SHARE), F32), jax.ShapeDtypeStruct((3 * K, 3 * K), F32)),
        in_specs=[anywhere, anywhere, anywhere, anywhere, anywhere],
        out_specs=(vmem, vmem),
        scratch_shapes=[
            pltpu.SMEM((NB,), jnp.int32),
            pltpu.SMEM((NB,), jnp.int32),
            pltpu.VMEM((NB, B, B), F32),
            pltpu.VMEM((K, SEG), F32),
            pltpu.VMEM((K, SEG), F32),
            pltpu.VMEM((2, K, NB * B), F32),
            pltpu.VMEM((2, K, NB * B), F32),
            pltpu.VMEM((8, B), jnp.int32),
            pltpu.VMEM((8, B), jnp.int32),
            pltpu.VMEM((K, NB * B), F32),
            pltpu.VMEM((K, NB * B), F32),
            pltpu.VMEM((K, SEG), F32),
            pltpu.VMEM((L, K, OWNED), F32),
            pltpu.VMEM((K, OWNED), F32),
            pltpu.VMEM((K, OWNED), F32),
            pltpu.VMEM((K, OWNED), F32),
            pltpu.VMEM((K, SEG), F32),
            pltpu.VMEM((K, SEG), F32),
            pltpu.VMEM((3, 2, 4, B), F32),
            pltpu.VMEM((3, 2 * L, 4, B), F32),
            pltpu.VMEM((3, Z * Y // 2, 4, B), F32),
            pltpu.VMEM((2, 4, B), F32),
            dma((5,)), dma, dma, dma, dma, dma((2,)), dma((2,)), dma, dma, dma, dma,
            dma, dma, dma, dma, dma((3,)), dma((3,)), dma((2,)), dma((3,)), dma((3,)), dma((2,)), regular, regular,
        ],
        compiler_params=pltpu.CompilerParams(collective_id=0, has_side_effects=True, vmem_limit_bytes=56426496),
        name="lobpcg_step",
    )(block_rows.reshape(NB), block_cols.reshape(NB), hamiltonian_blocks.reshape(NB, B, B), current_states, previous_steps)


def solution(mesh):
    return jax.shard_map(
        body,
        mesh=mesh,
        in_specs=(
            P("row", "col", None, None, None),
            P("row", "col", None),
            P("row", "col", None),
            P(None, "row"),
            P(None, "row"),
        ),
        out_specs=(P(None, ("row", "col")), P()),
        check_vma=False,
    )
```
